512 devices in a mesh: row: 64 (over y_hi, z, core), col: 8 (over x, y_lo).
Axes of the slice: x: 4, y: 8 (y_hi: 4, y_lo: 2; y = y_hi * 2 + y_lo), z: 8, core: 2. Of those that a mesh axis runs over, the one named last changes fastest.
Arguments:
- samples: bfloat16 [49152, 32], P(('row', 'col')), may hold values from -4 to 4
- targets: float32 [49152, 8], P(('row', 'col')), may hold values from -8 to 8
- amplitude: float32 [8], replicated, may hold values from 0.3 to 3
- noise: float32 [8], replicated, may hold values from 0.3 to 3
Outputs:
- solution: float32 [49152, 8], P(('row', 'col'))
- residual: float32 [49152, 8], P(('row', 'col'))
The draws below stay inside these ranges and needn't reach their ends.
All inputs are finite; a program needn't handle non-finite values.
Results may differ from the reference program's by a relative error of at most 0.0003.
Values may be sent and summed in bfloat16 or wider, within the bound.
No kernel may reach another device: no remote copies, remote signals or barrier semaphores. Data moves between devices by JAX's collectives and lax.ppermute only.
A program may use at most 64 MiB of HBM per device.

```python
import math
import jax
import jax.numpy as jnp
from jax import lax

FEATURES = 32
PROBES = 8
ITERS = 2
SAMPLES = 49152


def draw_samples(key, part):
    key = jax.random.fold_in(key, 11)
    values = jnp.clip(jax.random.normal(key, (SAMPLES, FEATURES), jnp.float32), -4.0, 4.0)
    return values.astype(jnp.bfloat16)


def level_of(key, shape, pieces, smallest, top_value):
    def one(position, blocks):
        draws = jax.random.uniform(jax.random.fold_in(jax.random.fold_in(key, 6), position), (blocks,), jnp.float32, smallest / len(pieces), top_value / len(pieces))
        return jnp.repeat(jnp.exp(draws), shape[position] // blocks).reshape((-1,) + (1,) * (len(shape) - position - 1))

    gain = one(*pieces[0])
    for cut in pieces[1:]:
        gain = gain * one(*cut)
    return gain


def normal_values(stream_key, shape, width, limit, shards=(), dtype=jnp.bfloat16):
    drawn = width * jax.random.normal(stream_key, shape, jnp.float32)
    if shards:
        drawn = drawn * level_of(stream_key, shape, shards, -0.22, 0.18)
    return jnp.clip(drawn, -limit, limit).astype(dtype)


def setup_inputs(seed: int = 0) -> dict:
    key_of = jax.random.split(jax.random.key(seed), 5)
    return {
        "samples": draw_samples(jax.random.fold_in(key_of[4], 71), 0),
        "targets": normal_values(key_of[1], (SAMPLES, PROBES), 1.0, 8.0, ((0, 512),), jnp.float32),
        "amplitude": jnp.clip(jnp.exp(jax.random.uniform(key_of[2], (PROBES,), jnp.float32, math.log(0.3), math.log(3.0))), 0.3, 3.0),
        "noise": jnp.clip(jnp.exp(jax.random.uniform(key_of[3], (PROBES,), jnp.float32, math.log(0.3), math.log(3.0))), 0.3, 3.0),
    }


def kernel_apply(samples, vec, amplitude, noise):
    exact = samples.astype(jnp.float32)
    sq = jnp.sum(exact * exact, axis=1)
    height = math.gcd(SAMPLES, 512)
    blocks = exact.reshape(SAMPLES // height, height, FEATURES)
    block_sq = sq.reshape(SAMPLES // height, height)

    def one_block(pair):
        rows, rows_sq = pair
        inner = jnp.dot(rows, exact.T, precision=lax.Precision.HIGHEST)
        expo = jnp.exp(-4.0 * (rows_sq[:, None] + sq[None, :] - 2.0 * inner) / FEATURES)
        return jnp.dot(expo, vec, precision=lax.Precision.HIGHEST)

    applied = lax.map(one_block, (blocks, block_sq)).reshape(SAMPLES, PROBES)
    return amplitude[None, :] * applied + noise[None, :] * vec


def reference(samples, targets, amplitude, noise):
    solution = jnp.zeros_like(targets)
    residual = targets
    direction = targets
    norm_now = jnp.sum(residual * residual, axis=0)
    for step in range(ITERS):
        image = kernel_apply(samples, direction, amplitude, noise)
        alpha = norm_now / jnp.sum(direction * image, axis=0)
        solution = solution + alpha[None, :] * direction
        residual = residual - alpha[None, :] * image
        norm_next = jnp.sum(residual * residual, axis=0)
        direction = residual + (norm_next / norm_now)[None, :] * direction
        norm_now = norm_next
    return solution, residual
```

```python
import functools

import jax
import jax.numpy as jnp
import numpy as np
from jax import lax
from jax.experimental import pallas as pl
from jax.experimental.pallas import tpu as pltpu
from jax.sharding import Mesh
from jax.sharding import PartitionSpec as P

AXES = ("yh", "z", "core", "x", "yl")
SIZES = (4, 8, 2, 4, 2)
COLS = ("yh", "z", "yl")
ROWS = ("core", "x")
LANES = 128
LOG2E = 1.4426950408889634
F32 = jnp.float32
BF16 = jnp.bfloat16


def group(axes):
    return int(np.prod([SIZES[AXES.index(a)] for a in axes]))


def iota(shape, dim):
    return lax.broadcasted_iota(jnp.int32, shape, dim)


def rounded(v):
    return v.astype(BF16).astype(F32)


def lane(block, k):
    return jnp.sum(jnp.where(iota(block.shape, 1) == k, block, 0.0), axis=1, keepdims=True)


def total(v):
    return jnp.sum(v, axis=1, keepdims=True)


def exchange(blocks, axes):
    return lax.all_to_all(blocks, axes, 0, 0)


def pack_kernel(x_ref, b_ref, cols_ref, rows_ref, b_out_ref):
    own = x_ref.shape[1]
    x = x_ref[...].astype(F32)
    b = b_ref[...]
    hi = rounded(b)
    lo = b - hi
    block = jnp.concatenate([x, hi, lo], axis=0).astype(BF16)
    pad = jnp.zeros((block.shape[0], LANES - own), BF16)
    block = jnp.concatenate([block, pad], axis=1)
    for i in range(cols_ref.shape[0]):
        cols_ref[i] = block
    for i in range(rows_ref.shape[0]):
        rows_ref[i] = block
    b_out_ref[...] = jnp.concatenate([b, jnp.zeros((b.shape[0], LANES - own), F32)], axis=1)


def operand(block, features, is_row):
    full = block.astype(F32)
    x = full[:features]
    half = 0.5 * jnp.sum(x * x, axis=0, keepdims=True)
    h1 = rounded(half)
    h2 = rounded(half - h1)
    h3 = half - h1 - h2
    k = iota((16, LANES), 0)
    at = 0 if is_row else 3
    pieces = jnp.where(k == at, -h1, jnp.where(k == at + 1, -h2, jnp.where(k == at + 2, -h3, 0.0)))
    ones = jnp.where((k >= 3 - at) & (k < 6 - at), 1.0, 0.0)
    middle = jnp.zeros_like(full[features:]) if is_row else full[features:]
    return jnp.concatenate([x, middle, pieces + ones], axis=0).T


def tile_product(rows_ref, cols_ref, vec_ref, out_ref, scale, height, width):
    n_rows, n_cols = rows_ref.shape[0], cols_ref.shape[0]

    def chunk(r, carry):
        at = pl.multiple_of(r * height, height)
        rows = rows_ref[pl.ds(at, height), :]
        acc = jnp.zeros((height, vec_ref.shape[1]), F32)
        for c in range(0, n_cols, width):
            inner = lax.dot_general(
                rows, cols_ref[c : c + width, :], (((1,), (1,)), ((), ())), preferred_element_type=F32
            )
            e = jnp.exp2(inner * scale)
            hi = e.astype(BF16)
            lo = (e - hi.astype(F32)).astype(BF16)
            vec = vec_ref[c : c + width, :]
            acc += jnp.dot(hi, vec, preferred_element_type=F32)
            acc += jnp.dot(lo, vec, preferred_element_type=F32)
        out_ref[pl.ds(at, height), :] = acc
        return carry

    lax.fori_loop(0, n_rows // height, chunk, 0)


def row_blocks(prod_ref, own, at, n):
    keep = iota((8, LANES), 1) < own
    for i in range(n):
        t = prod_ref[own * i : own * i + LANES, :].T
        yield i, jnp.where(keep, t[at : at + 8] + t[at + 8 : at + 16], 0.0)


def first_kernel(scale, own, features, height, width, gcols_ref, grows_ref, rows_ref, cols_ref, out_ref, prod_ref):
    n_c, n_r = gcols_ref.shape[0], grows_ref.shape[0]

    def col(i, carry):
        at = pl.multiple_of(i * own, own)
        cols_ref[pl.ds(at, own), :] = operand(gcols_ref[i], features, False)[:own].astype(BF16)
        return carry

    lax.fori_loop(0, n_c, col, 0)
    for i in range(n_r):
        rows_ref[own * i : own * (i + 1), :] = operand(grows_ref[i], features, True)[:own].astype(BF16)
    tile_product(rows_ref, cols_ref, cols_ref, prod_ref.at[0 : n_r * own], scale, height, width)
    for i, t in row_blocks(prod_ref, own, features, n_r):
        for j in range(n_r):
            out_ref[j, i] = t


def first_product(gcols, grows, own, scale):
    n_c, n_r = gcols.shape[0], grows.shape[0]
    features = gcols.shape[1] - 16
    depth = features + 32
    return pl.pallas_call(
        functools.partial(first_kernel, scale, own, features, 256, 512),
        out_shape=(
            jax.ShapeDtypeStruct((n_r * own, depth), BF16),
            jax.ShapeDtypeStruct((n_c * own, depth), BF16),
            jax.ShapeDtypeStruct((n_r, n_r, 8, LANES), F32),
        ),
        scratch_shapes=[pltpu.VMEM((n_r * own + LANES - own, depth), F32)],
        compiler_params=pltpu.CompilerParams(vmem_limit_bytes=48 * 1024 * 1024),
    )(gcols, grows)


def image_kernel(own, features, parts_ref, grows_ref, b_ref, amp_ref, noise_ref, me_ref, w_ref, out_ref):
    n = parts_ref.shape[0]
    amp, noise = amp_ref[...], noise_ref[...]
    curve = jnp.zeros((8, 1), F32)
    norm = jnp.zeros((8, 1), F32)
    for i in range(n):
        e = parts_ref[0, i]
        for j in range(1, n):
            e = e + parts_ref[j, i]
        pieces = grows_ref[i].astype(F32)[features:]
        b = pieces[:8] + pieces[8:]
        w = amp * e + noise * b
        w_ref[i] = w
        curve += total(b * w)
        norm += total(b * b)
    k = iota((8, LANES), 1)
    own_w = w_ref[me_ref[0]]
    message = jnp.where(k < own, own_w, jnp.where(k == own, curve, jnp.where(k == own + 1, norm, 0.0)))
    for i in range(out_ref.shape[0]):
        out_ref[i] = message


def second_kernel(scale, own, features, height, width, gw_ref, gcols_ref, grows_ref, w_ref, rows_ref, cols_ref, out_ref, stats_ref, vec_ref, prod_ref):
    n_c, n_r = gcols_ref.shape[0], grows_ref.shape[0]
    sums = gw_ref[0]
    for i in range(1, n_c):
        sums = sums + gw_ref[i]
    curve, norm = lane(sums, own), lane(sums, own + 1)
    alpha = norm / curve
    keep = iota((8, LANES), 1) < own

    def targets(ref, i):
        pieces = ref[i].astype(F32)[features:]
        return pieces[:8] + pieces[8:]

    def col(i, carry):
        r = jnp.where(keep, targets(gcols_ref, i) - alpha * gw_ref[i], 0.0)
        hi = rounded(r)
        at = pl.multiple_of(i * own, own)
        vec_ref[pl.ds(at, own), :] = jnp.concatenate([hi, r - hi], axis=0).T[:own].astype(BF16)
        return carry

    lax.fori_loop(0, n_c, col, 0)
    tile_product(rows_ref, cols_ref, vec_ref, prod_ref.at[0 : n_r * own], scale, height, width)
    rr = jnp.zeros((8, 1), F32)
    rw = jnp.zeros((8, 1), F32)
    br = jnp.zeros((8, 1), F32)
    rer = jnp.zeros((8, 1), F32)
    ber = jnp.zeros((8, 1), F32)
    blocks = []
    for i, t in row_blocks(prod_ref, own, 0, n_r):
        b, w = targets(grows_ref, i), w_ref[i]
        r = b - alpha * w
        rr += total(r * r)
        rw += total(r * w)
        br += total(b * r)
        rer += total(r * t)
        ber += total(b * t)
        blocks.append(t)
    k = iota((8, LANES), 1)
    for i, t in enumerate(blocks):
        out_ref[i] = jnp.where(k == own, rer, jnp.where(k == own + 1, ber, t))
    stats = jnp.zeros((8, LANES), F32)
    for j, v in enumerate((alpha, norm, curve, rr, rw, br)):
        stats = jnp.where(k == j, v, stats)
    stats_ref[...] = stats


def scalars_kernel(own, parts_ref, stats_ref, out_ref, sum_ref):
    n = parts_ref.shape[0]
    e = parts_ref[0]
    for j in range(1, n):
        e = e + parts_ref[j]
    sum_ref[...] = e
    stats = stats_ref[...]
    sub, k = iota((8, LANES), 0), iota((8, LANES), 1)
    row = jnp.zeros((8, LANES), F32)
    for j, v in enumerate((lane(e, own), lane(e, own + 1), lane(stats, 3), lane(stats, 4), lane(stats, 5))):
        row = jnp.where(k == 8 * j + sub, v, row)
    row = jnp.sum(row, axis=0, keepdims=True)
    out_ref[...] = jnp.broadcast_to(row, out_ref.shape)


def last_kernel(own, gs_ref, stats_ref, sum_ref, w_ref, b_ref, amp_ref, noise_ref, me_ref, x_ref, r_ref):
    row = jnp.sum(gs_ref[...], axis=0, keepdims=True)
    sub, k = iota((8, LANES), 0), iota((8, LANES), 1)
    rows = jnp.broadcast_to(row, (8, LANES))
    rer, ber, rr, rw, br = (total(jnp.where(k == 8 * j + sub, rows, 0.0)) for j in range(5))
    stats = stats_ref[...]
    alpha, norm, curve = lane(stats, 0), lane(stats, 1), lane(stats, 2)
    amp, noise = amp_ref[...], noise_ref[...]
    b, w = b_ref[...], w_ref[me_ref[0]]
    r = b - alpha * w
    s = amp * sum_ref[...] + noise * r
    beta = rr / norm
    direction = r + beta * b
    image = s + beta * w
    rs = amp * rer + noise * rr
    bs = amp * ber + noise * br
    curve2 = rs + beta * (rw + bs) + beta * beta * curve
    alpha2 = rr / curve2
    x_ref[...] = (alpha * b + alpha2 * direction)[:, :own]
    r_ref[...] = (r - alpha2 * image)[:, :own]


def shards(samples, targets, amplitude, noise):
    own, features = samples.shape
    n_c, n_r = group(COLS), group(ROWS)
    scale = 4.0 * 2.0 / features * LOG2E
    depth = features + 32
    amp = amplitude.reshape(-1, 1)
    noi = noise.reshape(-1, 1)
    me = lax.axis_index(ROWS).astype(jnp.int32).reshape(1)
    vmem = pl.BlockSpec(memory_space=pltpu.VMEM)
    smem = pl.BlockSpec(memory_space=pltpu.SMEM)
    tile = jax.ShapeDtypeStruct((8, LANES), F32)
    mcols, mrows, b = pl.pallas_call(
        pack_kernel,
        out_shape=(
            jax.ShapeDtypeStruct((n_c, features + 16, LANES), BF16),
            jax.ShapeDtypeStruct((n_r, features + 16, LANES), BF16),
            tile,
        ),
    )(samples.T, targets.T)
    grows = exchange(mrows, ROWS)
    gcols = exchange(mcols, COLS)
    rows, cols, parts = first_product(gcols, grows, own, scale)
    parts = exchange(parts, ROWS)
    w, message = pl.pallas_call(
        functools.partial(image_kernel, own, features),
        out_shape=(
            jax.ShapeDtypeStruct((n_r, 8, LANES), F32),
            jax.ShapeDtypeStruct((n_c, 8, LANES), F32),
        ),
        in_specs=[vmem] * 5 + [smem],
    )(parts, grows, b, amp, noi, me)
    gw = exchange(message, COLS)
    parts, stats = pl.pallas_call(
        functools.partial(second_kernel, scale, own, features, 256, 512),
        out_shape=(jax.ShapeDtypeStruct((n_r, 8, LANES), F32), tile),
        scratch_shapes=[
            pltpu.VMEM((n_c * own, 16), BF16),
            pltpu.VMEM((n_r * own + LANES - own, 16), F32),
        ],
        compiler_params=pltpu.CompilerParams(vmem_limit_bytes=48 * 1024 * 1024),
    )(gw, gcols, grows, w, rows, cols)
    parts = exchange(parts, ROWS)
    message, total_e = pl.pallas_call(
        functools.partial(scalars_kernel, own),
        out_shape=(jax.ShapeDtypeStruct((n_c, LANES), F32), tile),
    )(parts, stats)
    gs = exchange(message, COLS)
    x, r = pl.pallas_call(
        functools.partial(last_kernel, own),
        out_shape=(jax.ShapeDtypeStruct((8, own), F32),) * 2,
        in_specs=[vmem] * 7 + [smem],
    )(gs, stats, total_e, w, b, amp, noi, me)
    return x.T, r.T


def solution(mesh):
    fine = Mesh(mesh.devices.reshape(SIZES), AXES)
    split = P(AXES, None)
    return jax.shard_map(
        shards,
        mesh=fine,
        in_specs=(split, split, P(), P()),
        out_specs=(split, split),
        check_vma=False,
    )
```

```python
import functools
import math

import jax
import jax.numpy as jnp
import numpy as np
from jax import lax
from jax.experimental import pallas as pl
from jax.experimental.pallas import tpu as pltpu
from jax.sharding import Mesh
from jax.sharding import PartitionSpec as P

AXES = ("yh", "z", "core", "x", "yl")
SIZES = (4, 8, 2, 4, 2)
COLS = ("yh", "z", "yl")
ROWS = ("core", "x")
LANES = 128
LOG2E = 1.4426950408889634
F32 = jnp.float32
BF16 = jnp.bfloat16
SMALL = pltpu.CompilerParams(vmem_limit_bytes=4 * 1024 * 1024)
LARGE = pltpu.CompilerParams(vmem_limit_bytes=24 * 1024 * 1024)


def group(axes):
    return int(np.prod([SIZES[AXES.index(a)] for a in axes]))


def iota(shape, dim):
    return lax.broadcasted_iota(jnp.int32, shape, dim)


def rounded(v):
    return v.astype(BF16).astype(F32)


def lane(block, k):
    return total(jnp.where(iota(block.shape, 1) == k, block, 0.0))


def total(v):
    return jnp.sum(v, axis=1, keepdims=True)


def exchange(blocks, axes):
    return lax.all_to_all(blocks, axes, 0, 0)


def packed(blocks, own):
    k = iota(blocks[0].shape, 1)
    rolled = [b if own * i % LANES == 0 else pltpu.roll(b, own * i % LANES, 1) for i, b in enumerate(blocks)]
    outs = []
    for q in range(own * len(blocks) // LANES):
        out = None
        for i, b in enumerate(rolled):
            at = own * i - LANES * q
            if at + own <= 0 or at >= LANES:
                continue
            out = b if out is None else jnp.where(k < at, out, b)
        outs.append(out)
    return jnp.concatenate(outs, axis=1)


def block_of(dense, i, own):
    q, s = divmod(own * i, LANES)
    out = dense[:, LANES * q : LANES * (q + 1)]
    if s == 0:
        return out
    out = pltpu.roll(out, LANES - s, 1)
    if s + own > LANES:
        after = pltpu.roll(dense[:, LANES * (q + 1) : LANES * (q + 2)], LANES - s, 1)
        out = jnp.where(iota(out.shape, 1) < LANES - s, out, after)
    return out


def step_of(own):
    return LANES // math.gcd(own, LANES)


def pack_kernel(x_ref, b_ref, amp_ref, noise_ref, cols_ref, rows_ref, b_out_ref, consts_ref):
    own = x_ref.shape[1]
    b = b_ref[...]
    hi = rounded(b)
    block = jnp.concatenate([x_ref[...].astype(F32), hi, b - hi], axis=0).astype(BF16)
    block = jnp.concatenate([block, jnp.zeros((block.shape[0], LANES - own), BF16)], axis=1)
    for i in range(cols_ref.shape[0]):
        cols_ref[i] = block
    for i in range(rows_ref.shape[0]):
        rows_ref[i] = block
    b_out_ref[...] = jnp.concatenate([b, jnp.zeros((b.shape[0], LANES - own), F32)], axis=1)
    diagonal = iota((8, 8), 0) == iota((8, 8), 1)
    amp = total(jnp.where(diagonal, jnp.broadcast_to(amp_ref[...], (8, 8)), 0.0))
    noise = total(jnp.where(diagonal, jnp.broadcast_to(noise_ref[...], (8, 8)), 0.0))
    consts_ref[...] = jnp.where(iota((8, LANES), 1) == 0, amp, noise)


def operand(block, features, own, is_row):
    x = block[:features].astype(F32)
    half = 0.5 * jnp.sum(x * x, axis=0, keepdims=True)
    h1 = rounded(half)
    h2 = rounded(half - h1)
    h3 = half - h1 - h2
    k = iota((16, LANES), 0)
    at = 0 if is_row else 3
    pieces = jnp.where(k == at, -h1, jnp.where(k == at + 1, -h2, jnp.where(k == at + 2, -h3, 0.0)))
    ones = jnp.where((k >= 3 - at) & (k < 6 - at), 1.0, 0.0)
    return jnp.concatenate([x, pieces + ones], axis=0).T[:own].astype(BF16)


def tile_product(rows_ref, cols_ref, vec_ref, scale, height, width):
    n_rows, n_cols = rows_ref.shape[0], cols_ref.shape[0]
    outs = []
    for at in range(0, n_rows, height):
        rows = rows_ref[at : at + height, :]
        acc = jnp.zeros((vec_ref.shape[0], height), F32)
        for c in range(0, n_cols, width):
            inner = lax.dot_general(
                cols_ref[c : c + width, :], rows, (((1,), (1,)), ((), ())), preferred_element_type=F32
            )
            e = jnp.exp2(inner * scale)
            hi = e.astype(BF16)
            lo = (e - hi.astype(F32)).astype(BF16)
            vec = vec_ref[:, c : c + width]
            acc += jnp.dot(vec, hi, preferred_element_type=F32)
            acc += jnp.dot(vec, lo, preferred_element_type=F32)
        outs.append(acc[:8] + acc[8:])
    return jnp.concatenate(outs, axis=1)


def targets_of(ref, i, features):
    pieces = ref[i, features : features + 16].astype(F32)
    return pieces[:8] + pieces[8:]


def first_kernel(scale, own, features, height, width, gcols_ref, grows_ref, rows_ref, cols_ref, out_ref, vec_ref):
    n_c, n_r = gcols_ref.shape[0], grows_ref.shape[0]
    step = step_of(own)
    for i in range(n_c):
        cols_ref[own * i : own * (i + 1), :] = operand(gcols_ref[i], features, own, False)
    for i in range(0, n_c, step):
        pieces = [gcols_ref[j, features : features + 16].astype(F32) for j in range(i, i + step)]
        vec_ref[:, own * i : own * (i + step)] = packed(pieces, own).astype(BF16)
    for i in range(n_r):
        rows_ref[own * i : own * (i + 1), :] = operand(grows_ref[i], features, own, True)
    t = tile_product(rows_ref, cols_ref, vec_ref, scale, height, width)
    for j in range(n_r):
        out_ref[j] = t


def image_kernel(own, features, parts_ref, grows_ref, own_b_ref, consts_ref, me_ref, w_ref, b_ref, own_ref, out_ref, blocks_ref):
    n = parts_ref.shape[0]
    step = step_of(own)
    consts = consts_ref[...]
    amp, noise = consts[:, :1], consts[:, 1:2]
    e = parts_ref[0]
    for j in range(1, n):
        e = e + parts_ref[j]
    b = jnp.concatenate(
        [packed([targets_of(grows_ref, j, features) for j in range(i, i + step)], own) for i in range(0, n, step)],
        axis=1,
    )
    w = amp * e + noise * b
    w_ref[...] = w
    b_ref[...] = b
    curve, norm = total(b * w), total(b * b)
    for i in range(n):
        blocks_ref[i] = block_of(e, i, own)
    own_w = amp * blocks_ref[me_ref[0]] + noise * own_b_ref[...]
    own_ref[...] = own_w
    k = iota((8, LANES), 1)
    message = jnp.where(k < own, own_w, jnp.where(k == own, curve, norm))
    for i in range(out_ref.shape[0]):
        out_ref[i] = message


def second_kernel(scale, own, features, height, width, gw_ref, gcols_ref, w_ref, b_ref, rows_ref, cols_ref, out_ref, stats_ref, vec_ref):
    n_c, n_r = gcols_ref.shape[0], out_ref.shape[0]
    step = step_of(own)
    sums = gw_ref[0]
    for i in range(1, n_c):
        sums = sums + gw_ref[i]
    curve, norm = lane(sums, own), lane(sums, own + 1)
    alpha = norm / curve
    for i in range(0, n_c, step):
        r = packed([targets_of(gcols_ref, j, features) - alpha * gw_ref[j] for j in range(i, i + step)], own)
        hi = rounded(r)
        vec_ref[:, own * i : own * (i + step)] = jnp.concatenate([hi, r - hi], axis=0).astype(BF16)
    t = tile_product(rows_ref, cols_ref, vec_ref, scale, height, width)
    b, w = b_ref[...], w_ref[...]
    r = b - alpha * w
    rr, rw, br, rer, ber = total(r * r), total(r * w), total(b * r), total(r * t), total(b * t)
    k = iota((8, LANES), 1)
    for i in range(n_r):
        out_ref[i] = jnp.where(k < own, block_of(t, i, own), jnp.where(k == own, rer, ber))
    stats = jnp.zeros((8, LANES), F32)
    for j, v in enumerate((alpha, norm, curve, rr, rw, br)):
        stats = jnp.where(k == j, v, stats)
    stats_ref[...] = stats


def scalars_kernel(own, parts_ref, stats_ref, out_ref, sum_ref):
    e = parts_ref[0]
    for j in range(1, parts_ref.shape[0]):
        e = e + parts_ref[j]
    sum_ref[...] = e
    stats = stats_ref[...]
    sub, k = iota((8, LANES), 0), iota((8, LANES), 1)
    row = jnp.zeros((8, LANES), F32)
    for j, v in enumerate((lane(e, own), lane(e, own + 1), lane(stats, 3), lane(stats, 4), lane(stats, 5))):
        row = jnp.where(k == 8 * j + sub, v, row)
    row = jnp.sum(row, axis=0, keepdims=True)
    out_ref[...] = jnp.broadcast_to(row, out_ref.shape)


def last_kernel(own, gs_ref, stats_ref, sum_ref, w_ref, b_ref, consts_ref, x_ref, r_ref):
    row = jnp.sum(gs_ref[...], axis=0, keepdims=True)
    sub, k = iota((8, LANES), 0), iota((8, LANES), 1)
    rows = jnp.broadcast_to(row, (8, LANES))
    rer, ber, rr, rw, br = (total(jnp.where(k == 8 * j + sub, rows, 0.0)) for j in range(5))
    stats = stats_ref[...]
    alpha, norm, curve = lane(stats, 0), lane(stats, 1), lane(stats, 2)
    consts = consts_ref[...]
    amp, noise = consts[:, :1], consts[:, 1:2]
    b, w = b_ref[...], w_ref[...]
    r = b - alpha * w
    s = amp * sum_ref[...] + noise * r
    beta = rr / norm
    direction = r + beta * b
    image = s + beta * w
    rs = amp * rer + noise * rr
    bs = amp * ber + noise * br
    curve2 = rs + beta * (rw + bs) + beta * beta * curve
    alpha2 = rr / curve2
    x_ref[...] = (alpha * b + alpha2 * direction)[:, :own]
    r_ref[...] = (r - alpha2 * image)[:, :own]


def shards(samples, targets, amplitude, noise):
    own, features = samples.shape
    n_c, n_r = group(COLS), group(ROWS)
    scale = 4.0 * 2.0 / features * LOG2E
    depth = features + 16
    height, width = HEIGHT, WIDTH
    me = lax.axis_index(ROWS).astype(jnp.int32).reshape(1)
    vmem = pl.BlockSpec(memory_space=pltpu.VMEM)
    smem = pl.BlockSpec(memory_space=pltpu.SMEM)

    def array(*shape, dtype=F32):
        return jax.ShapeDtypeStruct(shape, dtype)

    tile = array(8, LANES)
    mcols, mrows, b, consts = pl.pallas_call(
        pack_kernel,
        out_shape=(array(n_c, depth, LANES, dtype=BF16), array(n_r, depth, LANES, dtype=BF16), tile, tile),
        compiler_params=SMALL,
    )(samples.T, targets.T, amplitude.reshape(1, -1), noise.reshape(1, -1))
    grows = exchange(mrows, ROWS)
    gcols = exchange(mcols, COLS)
    rows, cols, parts = pl.pallas_call(
        functools.partial(first_kernel, scale, own, features, height, width),
        out_shape=(
            array(n_r * own, depth, dtype=BF16),
            array(n_c * own, depth, dtype=BF16),
            array(n_r, 8, n_r * own),
        ),
        scratch_shapes=[pltpu.VMEM((16, n_c * own), BF16)],
        compiler_params=LARGE,
    )(gcols, grows)
    parts = exchange(parts, ROWS)
    w, b_rows, own_w, message = pl.pallas_call(
        functools.partial(image_kernel, own, features),
        out_shape=(array(8, n_r * own), array(8, n_r * own), tile, array(n_c, 8, LANES)),
        in_specs=[vmem] * 4 + [smem],
        scratch_shapes=[pltpu.VMEM((n_r, 8, LANES), F32)],
        compiler_params=SMALL,
    )(parts, grows, b, consts, me)
    gw = exchange(message, COLS)
    parts, stats = pl.pallas_call(
        functools.partial(second_kernel, scale, own, features, height, width),
        out_shape=(array(n_r, 8, LANES), tile),
        scratch_shapes=[pltpu.VMEM((16, n_c * own), BF16)],
        compiler_params=LARGE,
    )(gw, gcols, w, b_rows, rows, cols)
    parts = exchange(parts, ROWS)
    message, total_e = pl.pallas_call(
        functools.partial(scalars_kernel, own),
        out_shape=(array(n_c, LANES), tile),
        compiler_params=SMALL,
    )(parts, stats)
    gs = exchange(message, COLS)
    x, r = pl.pallas_call(
        functools.partial(last_kernel, own),
        out_shape=(array(8, own), array(8, own)),
        compiler_params=SMALL,
    )(gs, stats, total_e, own_w, b, consts)
    return x.T, r.T


HEIGHT, WIDTH = 256, 512


def solution(mesh):
    fine = Mesh(mesh.devices.reshape(SIZES), AXES)
    split = P(AXES, None)
    return jax.shard_map(
        shards,
        mesh=fine,
        in_specs=(split, split, P(), P()),
        out_specs=(split, split),
        check_vma=False,
    )
```

```python
import functools
import math

import jax
import jax.numpy as jnp
import numpy as np
from jax import lax
from jax.experimental import pallas as pl
from jax.experimental.pallas import tpu as pltpu
from jax.sharding import Mesh
from jax.sharding import PartitionSpec as P

AXES = ("yh", "z", "core", "x", "yl")
SIZES = (4, 8, 2, 4, 2)
COLS = ("yh", "x", "yl")
ROWS = ("z", "core")
LANES = 128
LOG2E = 1.4426950408889634
F32 = jnp.float32
BF16 = jnp.bfloat16
SMALL = pltpu.CompilerParams(vmem_limit_bytes=4 * 1024 * 1024)
LARGE = pltpu.CompilerParams(vmem_limit_bytes=24 * 1024 * 1024)
WHOLE = pltpu.CompilerParams(vmem_limit_bytes=60 * 1024 * 1024)


def group(axes):
    return int(np.prod([SIZES[AXES.index(a)] for a in axes]))


def iota(shape, dim):
    return lax.broadcasted_iota(jnp.int32, shape, dim)


def rounded(v):
    return v.astype(BF16).astype(F32)


def lane(block, k):
    return total(jnp.where(iota(block.shape, 1) == k, block, 0.0))


def total(v):
    return jnp.sum(v, axis=1, keepdims=True)


def exchange(blocks, axes):
    return lax.all_to_all(blocks, axes, 0, 0)


def packed(blocks, own):
    k = iota(blocks[0].shape, 1)
    rolled = [b if own * i % LANES == 0 else pltpu.roll(b, own * i % LANES, 1) for i, b in enumerate(blocks)]
    outs = []
    for q in range(own * len(blocks) // LANES):
        out = None
        for i, b in enumerate(rolled):
            at = own * i - LANES * q
            if at + own <= 0 or at >= LANES:
                continue
            out = b if out is None else jnp.where(k < at, out, b)
        outs.append(out)
    return jnp.concatenate(outs, axis=1)


def block_of(dense, i, own):
    q, s = divmod(own * i, LANES)
    out = dense[:, LANES * q : LANES * (q + 1)]
    if s == 0:
        return out
    out = pltpu.roll(out, LANES - s, 1)
    if s + own > LANES:
        after = pltpu.roll(dense[:, LANES * (q + 1) : LANES * (q + 2)], LANES - s, 1)
        out = jnp.where(iota(out.shape, 1) < LANES - s, out, after)
    return out


def step_of(own):
    return LANES // math.gcd(own, LANES)


def pack_kernel(x_hbm, b_hbm, amp_hbm, noise_hbm, cols_ref, rows_ref, b_out_ref, consts_ref, x_ref, b_ref, amp_ref, noise_ref, sems):
    own = x_ref.shape[1]
    pairs = ((x_hbm, x_ref), (b_hbm, b_ref), (amp_hbm, amp_ref), (noise_hbm, noise_ref))
    copies = [pltpu.make_async_copy(src, dst, sems.at[i]) for i, (src, dst) in enumerate(pairs)]
    for copy in copies:
        copy.start()
    for copy in copies:
        copy.wait()
    b = b_ref[...]
    hi = rounded(b)
    block = jnp.concatenate([x_ref[...].astype(F32), hi, b - hi], axis=0).astype(BF16)
    block = jnp.concatenate([block, jnp.zeros((block.shape[0], LANES - own), BF16)], axis=1)
    for i in range(cols_ref.shape[0]):
        cols_ref[i] = block
    for i in range(rows_ref.shape[0]):
        rows_ref[i] = block
    b_out_ref[...] = jnp.concatenate([b, jnp.zeros((b.shape[0], LANES - own), F32)], axis=1)
    diagonal = iota((8, 8), 0) == iota((8, 8), 1)
    amp = total(jnp.where(diagonal, jnp.broadcast_to(amp_ref[...], (8, 8)), 0.0))
    noise = total(jnp.where(diagonal, jnp.broadcast_to(noise_ref[...], (8, 8)), 0.0))
    consts_ref[...] = jnp.where(iota((8, LANES), 1) == 0, amp, noise)


def operand(block, features, own, is_row):
    x = block[:features].astype(F32)
    half = 0.5 * jnp.sum(x * x, axis=0, keepdims=True)
    h1 = rounded(half)
    h2 = rounded(half - h1)
    h3 = half - h1 - h2
    k = iota((16, LANES), 0)
    at = 0 if is_row else 3
    pieces = jnp.where(k == at, -h1, jnp.where(k == at + 1, -h2, jnp.where(k == at + 2, -h3, 0.0)))
    ones = jnp.where((k >= 3 - at) & (k < 6 - at), 1.0, 0.0)
    return jnp.concatenate([x, pieces + ones], axis=0).T[:own].astype(BF16)


def tile_product(rows_ref, cols_ref, vec_ref, scale, height, width):
    n_rows, n_cols = rows_ref.shape[0], cols_ref.shape[0]
    outs = []
    for at in range(0, n_rows, height):
        rows = rows_ref[at : at + height, :]
        acc = jnp.zeros((vec_ref.shape[0], height), F32)
        for c in range(0, n_cols, width):
            inner = lax.dot_general(
                cols_ref[c : c + width, :], rows, (((1,), (1,)), ((), ())), preferred_element_type=F32
            )
            e = jnp.exp2(inner * scale)
            hi = e.astype(BF16)
            lo = (e - hi.astype(F32)).astype(BF16)
            vec = vec_ref[:, c : c + width]
            acc += jnp.dot(vec, hi, preferred_element_type=F32)
            acc += jnp.dot(vec, lo, preferred_element_type=F32)
        outs.append(acc[:8] + acc[8:])
    return jnp.concatenate(outs, axis=1)


def targets_of(ref, i, features):
    pieces = ref[i, features : features + 16].astype(F32)
    return pieces[:8] + pieces[8:]


def packed_all(blocks, own):
    step = step_of(own)
    return jnp.concatenate([packed(blocks[i : i + step], own) for i in range(0, len(blocks), step)], axis=1)


def first_kernel(scale, own, features, height, width, gcols_ref, grows_ref, own_b_ref, rows_ref, cols_ref, out_ref, vec_ref):
    n_c, n_r = gcols_ref.shape[0], grows_ref.shape[0]
    step = step_of(own)
    for i in range(n_c):
        cols_ref[own * i : own * (i + 1), :] = operand(gcols_ref[i], features, own, False)
    for i in range(0, n_c, step):
        pieces = [gcols_ref[j, features : features + 16].astype(F32) for j in range(i, i + step)]
        vec_ref[:, own * i : own * (i + step)] = packed(pieces, own).astype(BF16)
    for i in range(n_r):
        rows_ref[own * i : own * (i + 1), :] = operand(grows_ref[i], features, own, True)
    t = tile_product(rows_ref, cols_ref, vec_ref, scale, height, width)
    b = packed_all([targets_of(grows_ref, i, features) for i in range(n_r)], own)
    own_b = own_b_ref[...]
    beb, norm = total(b * t), total(own_b * own_b)
    k = iota((8, LANES), 1)
    for i in range(n_r):
        out_ref[i] = jnp.where(k < own, block_of(t, i, own), jnp.where(k == own, beb, norm))


def image_kernel(own, parts_ref, own_b_ref, consts_ref, w_ref, out_ref):
    consts = consts_ref[...]
    amp, noise = consts[:, :1], consts[:, 1:2]
    e = parts_ref[0]
    for j in range(1, parts_ref.shape[0]):
        e = e + parts_ref[j]
    k = iota((8, LANES), 1)
    message = jnp.where(k < own, amp * e + noise * own_b_ref[...], e)
    w_ref[...] = message
    for i in range(out_ref.shape[0]):
        out_ref[i] = message


def residual_kernel(own, features, gw_ref, gcols_ref, w_ref, own_b_ref, consts_ref, vec_ref, out_ref, stats_ref):
    n_c = gcols_ref.shape[0]
    step = step_of(own)
    consts = consts_ref[...]
    amp, noise = consts[:, :1], consts[:, 1:2]
    sums = gw_ref[0]
    for i in range(1, n_c):
        sums = sums + gw_ref[i]
    beb, norm = lane(sums, own), lane(sums, own + 1)
    curve = amp * beb + noise * norm
    alpha = norm / curve
    keep = iota((8, LANES), 1) < own
    w = jnp.where(keep, w_ref[...], 0.0)
    own_r = own_b_ref[...] - alpha * w
    for i in range(out_ref.shape[0]):
        out_ref[i] = own_r
    for i in range(0, n_c, step):
        r = packed([targets_of(gcols_ref, j, features) - alpha * gw_ref[j] for j in range(i, i + step)], own)
        hi = rounded(r)
        vec_ref[:, own * i : own * (i + step)] = jnp.concatenate([hi, r - hi], axis=0).astype(BF16)
    k = iota((8, LANES), 1)
    stats = jnp.zeros((8, LANES), F32)
    for j, v in enumerate((alpha, norm, curve, total(own_r * own_r), total(own_r * w))):
        stats = jnp.where(k == j, v, stats)
    stats_ref[...] = stats


def second_kernel(scale, height, width, rows_ref, cols_ref, vec_ref, out_ref):
    out_ref[...] = tile_product(rows_ref, cols_ref, vec_ref, scale, height, width)


def dots_kernel(own, t_ref, gr_ref, stats_ref, out_ref):
    n_r = gr_ref.shape[0]
    t = t_ref[...]
    rer = total(packed_all([gr_ref[i] for i in range(n_r)], own) * t)
    stats = stats_ref[...]
    rr, rw = stats[:, 3:4], stats[:, 4:5]
    k = iota((8, LANES), 1)
    scalars = jnp.where(k == own, rer, jnp.where(k == own + 1, rr, rw))
    for i in range(n_r):
        out_ref[i] = jnp.where(k < own, block_of(t, i, own), scalars)


def scalars_kernel(own, parts_ref, out_ref, sum_ref):
    e = parts_ref[0]
    for j in range(1, parts_ref.shape[0]):
        e = e + parts_ref[j]
    sum_ref[...] = e
    sub, k = iota((8, LANES), 0), iota((8, LANES), 1)
    row = jnp.zeros((8, LANES), F32)
    for j in range(3):
        row = jnp.where(k == 8 * j + sub, lane(e, own + j), row)
    row = jnp.sum(row, axis=0, keepdims=True)
    out_ref[...] = jnp.broadcast_to(row, out_ref.shape)


def last_kernel(own, gs_ref, stats_ref, sum_ref, w_ref, b_ref, consts_ref, x_ref, r_ref):
    row = jnp.sum(gs_ref[...], axis=0, keepdims=True)
    sub, k = iota((8, LANES), 0), iota((8, LANES), 1)
    rows = jnp.broadcast_to(row, (8, LANES))
    rer, rr, rw = (total(jnp.where(k == 8 * j + sub, rows, 0.0)) for j in range(3))
    stats, consts = stats_ref[...], consts_ref[...]
    alpha, norm, curve = stats[:, :1], stats[:, 1:2], stats[:, 2:3]
    amp, noise = consts[:, :1], consts[:, 1:2]
    b, w = b_ref[...], w_ref[...]
    r = b - alpha * w
    beta = rr / norm
    direction = r + beta * b
    image = amp * sum_ref[...] + noise * r + beta * w
    curve2 = amp * rer + noise * rr + 2.0 * beta * rw + beta * beta * curve
    alpha2 = rr / curve2
    x_ref[...] = (alpha * b + alpha2 * direction)[:, :own]
    r_ref[...] = (r - alpha2 * image)[:, :own]


def shards(samples, targets, amplitude, noise):
    own, features = samples.shape
    n_c, n_r = group(COLS), group(ROWS)
    scale = 4.0 * 2.0 / features * LOG2E
    depth = features + 16
    height, width = HEIGHT, WIDTH

    def array(*shape, dtype=F32):
        return jax.ShapeDtypeStruct(shape, dtype)

    tile = array(8, LANES)
    given = (samples.T, targets.T, amplitude.reshape(1, -1), noise.reshape(1, -1))
    mcols, mrows, b, consts = pl.pallas_call(
        pack_kernel,
        out_shape=(array(n_c, depth, LANES, dtype=BF16), array(n_r, depth, LANES, dtype=BF16), tile, tile),
        in_specs=[pl.BlockSpec(memory_space=pltpu.HBM)] * 4,
        scratch_shapes=[pltpu.VMEM(v.shape, v.dtype) for v in given] + [pltpu.SemaphoreType.DMA((4,))],
        compiler_params=WHOLE,
    )(*given)
    grows = exchange(mrows, ROWS)
    gcols = exchange(mcols, COLS)
    rows, cols, parts = pl.pallas_call(
        functools.partial(first_kernel, scale, own, features, height, width),
        out_shape=(
            array(n_r * own, depth, dtype=BF16),
            array(n_c * own, depth, dtype=BF16),
            array(n_r, 8, LANES),
        ),
        scratch_shapes=[pltpu.VMEM((16, n_c * own), BF16)],
        compiler_params=LARGE,
    )(gcols, grows, b)
    parts = exchange(parts, ROWS)
    w, message = pl.pallas_call(
        functools.partial(image_kernel, own),
        out_shape=(tile, array(n_c, 8, LANES)),
        compiler_params=SMALL,
    )(parts, b, consts)
    gw = exchange(message, COLS)
    vec, message, stats = pl.pallas_call(
        functools.partial(residual_kernel, own, features),
        out_shape=(array(16, n_c * own, dtype=BF16), array(n_r, 8, LANES), tile),
        compiler_params=SMALL,
    )(gw, gcols, w, b, consts)
    gr = exchange(message, ROWS)
    t = pl.pallas_call(
        functools.partial(second_kernel, scale, height, width),
        out_shape=array(8, n_r * own),
        compiler_params=LARGE,
        cost_estimate=pl.CostEstimate(
            flops=2 * 2 * 256 * n_r * n_c * own * own,
            bytes_accessed=n_r * n_c * own * own,
            transcendentals=n_r * n_c * own * own,
        ),
    )(rows, cols, vec)
    parts = pl.pallas_call(
        functools.partial(dots_kernel, own),
        out_shape=array(n_r, 8, LANES),
        compiler_params=SMALL,
    )(t, gr, stats)
    parts = exchange(parts, ROWS)
    message, sums = pl.pallas_call(
        functools.partial(scalars_kernel, own),
        out_shape=(array(n_c, LANES), tile),
        compiler_params=SMALL,
    )(parts)
    gs = exchange(message, COLS)
    x, r = pl.pallas_call(
        functools.partial(last_kernel, own),
        out_shape=(array(8, own), array(8, own)),
        compiler_params=SMALL,
    )(gs, stats, sums, w, b, consts)
    return x.T, r.T


HEIGHT, WIDTH = 256, 512


def solution(mesh):
    fine = Mesh(mesh.devices.reshape(SIZES), AXES)
    split = P(AXES, None)
    return jax.shard_map(
        shards,
        mesh=fine,
        in_specs=(split, split, P(), P()),
        out_specs=(split, split),
        check_vma=False,
    )
```

```python
import functools
import math

import jax
import jax.numpy as jnp
import numpy as np
from jax import lax
from jax.experimental import pallas as pl
from jax.experimental.pallas import tpu as pltpu
from jax.sharding import Mesh
from jax.sharding import PartitionSpec as P

AXES = ("yh", "z", "core", "x", "yl")
SIZES = (4, 8, 2, 4, 2)
COLS = ("yh", "x", "yl")
ROWS = ("z", "core")
LANES = 128
LOG2E = 1.4426950408889634
F32 = jnp.float32
BF16 = jnp.bfloat16
SMALL = pltpu.CompilerParams(vmem_limit_bytes=4 * 1024 * 1024)
LARGE = pltpu.CompilerParams(vmem_limit_bytes=24 * 1024 * 1024)
WHOLE = pltpu.CompilerParams(vmem_limit_bytes=60 * 1024 * 1024)


def group(axes):
    return int(np.prod([SIZES[AXES.index(a)] for a in axes]))


def iota(shape, dim):
    return lax.broadcasted_iota(jnp.int32, shape, dim)


def rounded(v):
    return v.astype(BF16).astype(F32)


def lane(block, k):
    return total(jnp.where(iota(block.shape, 1) == k, block, 0.0))


def total(v):
    return jnp.sum(v, axis=1, keepdims=True)


def exchange(blocks, axes):
    return lax.all_to_all(blocks, axes, 0, 0)


def packed(blocks, own):
    k = iota(blocks[0].shape, 1)
    rolled = [b if own * i % LANES == 0 else pltpu.roll(b, own * i % LANES, 1) for i, b in enumerate(blocks)]
    outs = []
    for q in range(own * len(blocks) // LANES):
        out = None
        for i, b in enumerate(rolled):
            at = own * i - LANES * q
            if at + own <= 0 or at >= LANES:
                continue
            out = b if out is None else jnp.where(k < at, out, b)
        outs.append(out)
    return jnp.concatenate(outs, axis=1)


def block_of(dense, i, own):
    q, s = divmod(own * i, LANES)
    out = dense[:, LANES * q : LANES * (q + 1)]
    if s == 0:
        return out
    out = pltpu.roll(out, LANES - s, 1)
    if s + own > LANES:
        after = pltpu.roll(dense[:, LANES * (q + 1) : LANES * (q + 2)], LANES - s, 1)
        out = jnp.where(iota(out.shape, 1) < LANES - s, out, after)
    return out


def step_of(own):
    return LANES // math.gcd(own, LANES)


def pack_kernel(x_hbm, b_hbm, amp_hbm, noise_hbm, cols_ref, rows_ref, b_out_ref, consts_ref, x_ref, b_ref, amp_ref, noise_ref, sems):
    own = x_ref.shape[1]
    pairs = ((x_hbm, x_ref), (b_hbm, b_ref), (amp_hbm, amp_ref), (noise_hbm, noise_ref))
    copies = [pltpu.make_async_copy(src, dst, sems.at[i]) for i, (src, dst) in enumerate(pairs)]
    for copy in copies:
        copy.start()
    for copy in copies:
        copy.wait()
    b = b_ref[...]
    features, hole = x_ref.shape[0], LANES - own
    b_out = jnp.concatenate([b, jnp.zeros((8, hole), F32)], axis=1)
    lo = b_out - rounded(b_out)
    pieces = [pltpu.roll(lo, own - hole * i, 1) for i in range(own // hole)]
    pieces += [jnp.zeros((8, LANES), F32)] * (features // 8 - len(pieces))
    x = jnp.concatenate([x_ref[...].astype(F32), jnp.zeros((features, hole), F32)], axis=1)
    x = jnp.where(iota(x.shape, 1) < own, x, jnp.concatenate(pieces, axis=0))
    block = jnp.concatenate([x, rounded(b_out)], axis=0).astype(BF16)
    for i in range(cols_ref.shape[0]):
        cols_ref[i] = block
    for i in range(rows_ref.shape[0]):
        rows_ref[i] = block
    b_out_ref[...] = b_out
    diagonal = iota((8, 8), 0) == iota((8, 8), 1)
    amp = total(jnp.where(diagonal, jnp.broadcast_to(amp_ref[...], (8, 8)), 0.0))
    noise = total(jnp.where(diagonal, jnp.broadcast_to(noise_ref[...], (8, 8)), 0.0))
    consts_ref[...] = jnp.where(iota((8, LANES), 1) == 0, amp, noise)


def operand(block, features, own, is_row):
    x = block[:features]
    half = 0.5 * jnp.sum(x * x, axis=0, keepdims=True)
    h1 = rounded(half)
    h2 = rounded(half - h1)
    h3 = half - h1 - h2
    k = iota((16, LANES), 0)
    at = 0 if is_row else 3
    pieces = jnp.where(k == at, -h1, jnp.where(k == at + 1, -h2, jnp.where(k == at + 2, -h3, 0.0)))
    ones = jnp.where((k >= 3 - at) & (k < 6 - at), 1.0, 0.0)
    return jnp.concatenate([x, pieces + ones], axis=0).T[:own].astype(BF16)


def tile_product(rows_ref, cols_ref, vec_ref, scale, height, width):
    n_rows, n_cols = rows_ref.shape[0], cols_ref.shape[0]
    outs = []
    for at in range(0, n_rows, height):
        rows = rows_ref[at : at + height, :]
        acc = jnp.zeros((vec_ref.shape[0], height), F32)
        for c in range(0, n_cols, width):
            inner = lax.dot_general(
                cols_ref[c : c + width, :], rows, (((1,), (1,)), ((), ())), preferred_element_type=F32
            )
            e = jnp.exp2(inner * scale)
            hi = e.astype(BF16)
            lo = (e - hi.astype(F32)).astype(BF16)
            vec = vec_ref[:, c : c + width]
            acc += jnp.dot(vec, hi, preferred_element_type=F32)
            acc += jnp.dot(vec, lo, preferred_element_type=F32)
        outs.append(acc[:8] + acc[8:])
    return jnp.concatenate(outs, axis=1)


def targets_of(block, features, own):
    hole = LANES - own
    k = iota((8, LANES), 1)
    lo = None
    for i in reversed(range(own // hole)):
        piece = pltpu.roll(block[8 * i : 8 * (i + 1)], hole * (i + 1), 1)
        lo = piece if lo is None else jnp.where(k < hole * (i + 1), piece, lo)
    return block[features : features + 8], lo


def packed_all(blocks, own):
    step = step_of(own)
    return jnp.concatenate([packed(blocks[i : i + step], own) for i in range(0, len(blocks), step)], axis=1)


def columns_kernel(own, features, gcols_ref, cols_ref, vec_ref):
    n_c = gcols_ref.shape[0]
    step = step_of(own)
    for i in range(0, n_c, step):
        pieces = []
        for j in range(i, i + step):
            block = gcols_ref[j].astype(F32)
            cols_ref[own * j : own * (j + 1), :] = operand(block, features, own, False)
            pieces.append(jnp.concatenate(targets_of(block, features, own), axis=0))
        vec_ref[:, own * i : own * (i + step)] = packed(pieces, own).astype(BF16)


def first_kernel(scale, own, features, height, width, grows_ref, cols_ref, vec_ref, own_b_ref, rows_ref, out_ref):
    n_r = grows_ref.shape[0]
    targets = []
    for i in range(n_r):
        block = grows_ref[i].astype(F32)
        rows_ref[own * i : own * (i + 1), :] = operand(block, features, own, True)
        hi, lo = targets_of(block, features, own)
        targets.append(hi + lo)
    t = tile_product(rows_ref, cols_ref, vec_ref, scale, height, width)
    b = packed_all(targets, own)
    own_b = own_b_ref[...]
    beb, norm = total(b * t), total(own_b * own_b)
    k = iota((8, LANES), 1)
    for i in range(n_r):
        out_ref[i] = jnp.where(k < own, block_of(t, i, own), jnp.where(k == own, beb, norm))


def image_kernel(own, parts_ref, own_b_ref, consts_ref, w_ref, out_ref):
    consts = consts_ref[...]
    amp, noise = consts[:, :1], consts[:, 1:2]
    e = parts_ref[0]
    for j in range(1, parts_ref.shape[0]):
        e = e + parts_ref[j]
    k = iota((8, LANES), 1)
    message = jnp.where(k < own, amp * e + noise * own_b_ref[...], e)
    w_ref[...] = message
    for i in range(out_ref.shape[0]):
        out_ref[i] = message


def residual_kernel(own, gw_ref, b_ref, w_ref, own_b_ref, consts_ref, vec_ref, out_ref, stats_ref):
    n_c = gw_ref.shape[0]
    step = step_of(own)
    consts = consts_ref[...]
    amp, noise = consts[:, :1], consts[:, 1:2]
    sums = gw_ref[0]
    for i in range(1, n_c):
        sums = sums + gw_ref[i]
    beb, norm = lane(sums, own), lane(sums, own + 1)
    curve = amp * beb + noise * norm
    alpha = norm / curve
    keep = iota((8, LANES), 1) < own
    w = jnp.where(keep, w_ref[...], 0.0)
    own_r = own_b_ref[...] - alpha * w
    for i in range(out_ref.shape[0]):
        out_ref[i] = own_r
    for i in range(0, n_c, step):
        at = slice(own * i, own * (i + step))
        b = b_ref[:, at].astype(F32)
        r = b[:8] + b[8:] - alpha * packed([gw_ref[j] for j in range(i, i + step)], own)
        hi = rounded(r)
        vec_ref[:, at] = jnp.concatenate([hi, r - hi], axis=0).astype(BF16)
    k = iota((8, LANES), 1)
    stats = jnp.zeros((8, LANES), F32)
    for j, v in enumerate((alpha, norm, curve, total(own_r * own_r), total(own_r * w))):
        stats = jnp.where(k == j, v, stats)
    stats_ref[...] = stats


def second_kernel(scale, height, width, rows_ref, cols_ref, vec_ref, out_ref):
    out_ref[...] = tile_product(rows_ref, cols_ref, vec_ref, scale, height, width)


def dots_kernel(own, t_ref, gr_ref, stats_ref, out_ref):
    n_r = gr_ref.shape[0]
    t = t_ref[...]
    rer = total(packed_all([gr_ref[i] for i in range(n_r)], own) * t)
    stats = stats_ref[...]
    rr, rw = stats[:, 3:4], stats[:, 4:5]
    k = iota((8, LANES), 1)
    scalars = jnp.where(k == own, rer, jnp.where(k == own + 1, rr, rw))
    for i in range(n_r):
        out_ref[i] = jnp.where(k < own, block_of(t, i, own), scalars)


def scalars_kernel(own, parts_ref, out_ref, sum_ref):
    e = parts_ref[0]
    for j in range(1, parts_ref.shape[0]):
        e = e + parts_ref[j]
    sum_ref[...] = e
    sub, k = iota((8, LANES), 0), iota((8, LANES), 1)
    row = jnp.zeros((8, LANES), F32)
    for j in range(3):
        row = jnp.where(k == 8 * j + sub, lane(e, own + j), row)
    row = jnp.sum(row, axis=0, keepdims=True)
    out_ref[...] = jnp.broadcast_to(row, out_ref.shape)


def last_kernel(own, gs_ref, stats_ref, sum_ref, w_ref, b_ref, consts_ref, x_ref, r_ref):
    row = jnp.sum(gs_ref[...], axis=0, keepdims=True)
    sub, k = iota((8, LANES), 0), iota((8, LANES), 1)
    rows = jnp.broadcast_to(row, (8, LANES))
    rer, rr, rw = (total(jnp.where(k == 8 * j + sub, rows, 0.0)) for j in range(3))
    stats, consts = stats_ref[...], consts_ref[...]
    alpha, norm, curve = stats[:, :1], stats[:, 1:2], stats[:, 2:3]
    amp, noise = consts[:, :1], consts[:, 1:2]
    b, w = b_ref[...], w_ref[...]
    r = b - alpha * w
    beta = rr / norm
    direction = r + beta * b
    image = amp * sum_ref[...] + noise * r + beta * w
    curve2 = amp * rer + noise * rr + 2.0 * beta * rw + beta * beta * curve
    alpha2 = rr / curve2
    x_ref[...] = (alpha * b + alpha2 * direction)[:, :own]
    r_ref[...] = (r - alpha2 * image)[:, :own]


def shards(samples, targets, amplitude, noise):
    own, features = samples.shape
    n_c, n_r = group(COLS), group(ROWS)
    scale = 4.0 * 2.0 / features * LOG2E
    depth = features + 16
    height, width = HEIGHT, WIDTH

    def array(*shape, dtype=F32):
        return jax.ShapeDtypeStruct(shape, dtype)

    tile = array(8, LANES)
    given = (samples.T, targets.T, amplitude.reshape(1, -1), noise.reshape(1, -1))
    mcols, mrows, b, consts = pl.pallas_call(
        pack_kernel,
        out_shape=(array(n_c, features + 8, LANES, dtype=BF16), array(n_r, features + 8, LANES, dtype=BF16), tile, tile),
        in_specs=[pl.BlockSpec(memory_space=pltpu.HBM)] * 4,
        scratch_shapes=[pltpu.VMEM(v.shape, v.dtype) for v in given] + [pltpu.SemaphoreType.DMA((4,))],
        compiler_params=WHOLE,
    )(*given)
    gcols = exchange(mcols, COLS)
    mrows, gcols = lax.optimization_barrier((mrows, gcols))
    grows = exchange(mrows, ROWS)
    cols, vec = pl.pallas_call(
        functools.partial(columns_kernel, own, features),
        out_shape=(array(n_c * own, depth, dtype=BF16), array(16, n_c * own, dtype=BF16)),
        compiler_params=LARGE,
        cost_estimate=pl.CostEstimate(flops=10**9, bytes_accessed=10**6, transcendentals=0),
    )(gcols)
    rows, parts = pl.pallas_call(
        functools.partial(first_kernel, scale, own, features, height, width),
        out_shape=(array(n_r * own, depth, dtype=BF16), array(n_r, 8, LANES)),
        compiler_params=LARGE,
    )(grows, cols, vec, b)
    parts = exchange(parts, ROWS)
    w, message = pl.pallas_call(
        functools.partial(image_kernel, own),
        out_shape=(tile, array(n_c, 8, LANES)),
        compiler_params=SMALL,
    )(parts, b, consts)
    gw = exchange(message, COLS)
    vec, message, stats = pl.pallas_call(
        functools.partial(residual_kernel, own),
        out_shape=(array(16, n_c * own, dtype=BF16), array(n_r, 8, LANES), tile),
        compiler_params=SMALL,
    )(gw, vec, w, b, consts)
    gr = exchange(message, ROWS)
    t = pl.pallas_call(
        functools.partial(second_kernel, scale, height, width),
        out_shape=array(8, n_r * own),
        compiler_params=LARGE,
        cost_estimate=pl.CostEstimate(
            flops=2 * 2 * 256 * n_r * n_c * own * own,
            bytes_accessed=n_r * n_c * own * own,
            transcendentals=n_r * n_c * own * own,
        ),
    )(rows, cols, vec)
    parts = pl.pallas_call(
        functools.partial(dots_kernel, own),
        out_shape=array(n_r, 8, LANES),
        compiler_params=SMALL,
    )(t, gr, stats)
    parts = exchange(parts, ROWS)
    message, sums = pl.pallas_call(
        functools.partial(scalars_kernel, own),
        out_shape=(array(n_c, LANES), tile),
        compiler_params=SMALL,
    )(parts)
    gs = exchange(message, COLS)
    x, r = pl.pallas_call(
        functools.partial(last_kernel, own),
        out_shape=(array(8, own), array(8, own)),
        compiler_params=SMALL,
    )(gs, stats, sums, w, b, consts)
    return x.T, r.T


HEIGHT, WIDTH = 256, 512


def solution(mesh):
    fine = Mesh(mesh.devices.reshape(SIZES), AXES)
    split = P(AXES, None)
    return jax.shard_map(
        shards,
        mesh=fine,
        in_specs=(split, split, P(), P()),
        out_specs=(split, split),
        check_vma=False,
    )
```

```python
import functools
import math

import jax
import jax.numpy as jnp
import numpy as np
from jax import lax
from jax.experimental import pallas as pl
from jax.experimental.pallas import tpu as pltpu
from jax.sharding import Mesh
from jax.sharding import PartitionSpec as P

AXES = ("yh", "z", "core", "x", "yl")
SIZES = (4, 8, 2, 4, 2)
COLS = ("yh", "z")
ROWS = ("core", "x", "yl")
LANES = 128
LOG2E = 1.4426950408889634
F32 = jnp.float32
BF16 = jnp.bfloat16
SMALL = pltpu.CompilerParams(vmem_limit_bytes=4 * 1024 * 1024)
LARGE = pltpu.CompilerParams(vmem_limit_bytes=24 * 1024 * 1024)
WHOLE = pltpu.CompilerParams(vmem_limit_bytes=60 * 1024 * 1024)


def group(axes):
    return int(np.prod([SIZES[AXES.index(a)] for a in axes]))


def iota(shape, dim):
    return lax.broadcasted_iota(jnp.int32, shape, dim)


def rounded(v):
    return v.astype(BF16).astype(F32)


def lane(block, k):
    return total(jnp.where(iota(block.shape, 1) == k, block, 0.0))


def total(v):
    return jnp.sum(v, axis=1, keepdims=True)


def exchange(blocks, axes):
    return lax.all_to_all(blocks, axes, 0, 0)


def packed(blocks, own):
    k = iota(blocks[0].shape, 1)
    rolled = [b if own * i % LANES == 0 else pltpu.roll(b, own * i % LANES, 1) for i, b in enumerate(blocks)]
    outs = []
    for q in range(own * len(blocks) // LANES):
        out = None
        for i, b in enumerate(rolled):
            at = own * i - LANES * q
            if at + own <= 0 or at >= LANES:
                continue
            out = b if out is None else jnp.where(k < at, out, b)
        outs.append(out)
    return jnp.concatenate(outs, axis=1)


def block_of(dense, i, own):
    q, s = divmod(own * i, LANES)
    out = dense[:, LANES * q : LANES * (q + 1)]
    if s == 0:
        return out
    out = pltpu.roll(out, LANES - s, 1)
    if s + own > LANES:
        after = pltpu.roll(dense[:, LANES * (q + 1) : LANES * (q + 2)], LANES - s, 1)
        out = jnp.where(iota(out.shape, 1) < LANES - s, out, after)
    return out


def step_of(own):
    return LANES // math.gcd(own, LANES)


def pack_kernel(x_hbm, b_hbm, amp_hbm, noise_hbm, cols_ref, rows_ref, b_out_ref, consts_ref, x_ref, b_ref, amp_ref, noise_ref, sems):
    own = x_ref.shape[1]
    pairs = ((x_hbm, x_ref), (b_hbm, b_ref), (amp_hbm, amp_ref), (noise_hbm, noise_ref))
    copies = [pltpu.make_async_copy(src, dst, sems.at[i]) for i, (src, dst) in enumerate(pairs)]
    for copy in copies:
        copy.start()
    for copy in copies:
        copy.wait()
    b = b_ref[...]
    features, hole = x_ref.shape[0], LANES - own
    b_out = jnp.concatenate([b, jnp.zeros((8, hole), F32)], axis=1)
    lo = b_out - rounded(b_out)
    pieces = [pltpu.roll(lo, own - hole * i, 1) for i in range(own // hole)]
    pieces += [jnp.zeros((8, LANES), F32)] * (features // 8 - len(pieces))
    x = jnp.concatenate([x_ref[...].astype(F32), jnp.zeros((features, hole), F32)], axis=1)
    x = jnp.where(iota(x.shape, 1) < own, x, jnp.concatenate(pieces, axis=0))
    block = jnp.concatenate([x, rounded(b_out)], axis=0).astype(BF16)
    for i in range(cols_ref.shape[0]):
        cols_ref[i] = block
    for i in range(rows_ref.shape[0]):
        rows_ref[i] = block
    b_out_ref[...] = b_out
    diagonal = iota((8, 8), 0) == iota((8, 8), 1)
    amp = total(jnp.where(diagonal, jnp.broadcast_to(amp_ref[...], (8, 8)), 0.0))
    noise = total(jnp.where(diagonal, jnp.broadcast_to(noise_ref[...], (8, 8)), 0.0))
    consts_ref[...] = jnp.where(iota((8, LANES), 1) == 0, amp, noise)


def operand(block, features, own, is_row):
    x = block[:features]
    half = 0.5 * jnp.sum(x * x, axis=0, keepdims=True)
    h1 = rounded(half)
    h2 = rounded(half - h1)
    h3 = half - h1 - h2
    k = iota((16, LANES), 0)
    at = 0 if is_row else 3
    pieces = jnp.where(k == at, -h1, jnp.where(k == at + 1, -h2, jnp.where(k == at + 2, -h3, 0.0)))
    ones = jnp.where((k >= 3 - at) & (k < 6 - at), 1.0, 0.0)
    return jnp.concatenate([x, pieces + ones], axis=0).T[:own].astype(BF16)


def tile_product(rows_ref, cols_ref, vec_ref, scale, height, width):
    n_rows, n_cols = rows_ref.shape[0], cols_ref.shape[0]
    outs = []
    for at in range(0, n_rows, height):
        rows = rows_ref[at : at + height, :]
        acc = jnp.zeros((vec_ref.shape[0], height), F32)
        for c in range(0, n_cols, width):
            inner = lax.dot_general(
                cols_ref[c : c + width, :], rows, (((1,), (1,)), ((), ())), preferred_element_type=F32
            )
            e = jnp.exp2(inner * scale)
            hi = e.astype(BF16)
            lo = (e - hi.astype(F32)).astype(BF16)
            vec = vec_ref[:, c : c + width]
            acc += jnp.dot(vec, hi, preferred_element_type=F32)
            acc += jnp.dot(vec, lo, preferred_element_type=F32)
        outs.append(acc[:8] + acc[8:])
    return jnp.concatenate(outs, axis=1)


def targets_of(block, features, own):
    hole = LANES - own
    k = iota((8, LANES), 1)
    lo = None
    for i in reversed(range(own // hole)):
        piece = pltpu.roll(block[8 * i : 8 * (i + 1)], hole * (i + 1), 1)
        lo = piece if lo is None else jnp.where(k < hole * (i + 1), piece, lo)
    return block[features : features + 8], lo


def packed_all(blocks, own):
    step = step_of(own)
    return jnp.concatenate([packed(blocks[i : i + step], own) for i in range(0, len(blocks), step)], axis=1)


def columns_kernel(own, features, gcols_ref, cols_ref, vec_ref):
    n_c = gcols_ref.shape[0]
    step = step_of(own)
    for i in range(0, n_c, step):
        pieces = []
        for j in range(i, i + step):
            block = gcols_ref[j].astype(F32)
            cols_ref[own * j : own * (j + 1), :] = operand(block, features, own, False)
            pieces.append(jnp.concatenate(targets_of(block, features, own), axis=0))
        vec_ref[:, own * i : own * (i + step)] = packed(pieces, own).astype(BF16)


def first_kernel(scale, own, features, height, width, grows_ref, cols_ref, vec_ref, own_b_ref, rows_ref, out_ref):
    n_r = grows_ref.shape[0]
    targets = []
    for i in range(n_r):
        block = grows_ref[i].astype(F32)
        rows_ref[own * i : own * (i + 1), :] = operand(block, features, own, True)
        hi, lo = targets_of(block, features, own)
        targets.append(hi + lo)
    t = tile_product(rows_ref, cols_ref, vec_ref, scale, height, width)
    b = packed_all(targets, own)
    own_b = own_b_ref[...]
    beb, norm = total(b * t), total(own_b * own_b)
    k = iota((8, LANES), 1)
    for i in range(n_r):
        out_ref[i] = jnp.where(k < own, block_of(t, i, own), jnp.where(k == own, beb, norm))


def image_kernel(own, parts_ref, own_b_ref, consts_ref, w_ref, out_ref):
    consts = consts_ref[...]
    amp, noise = consts[:, :1], consts[:, 1:2]
    e = parts_ref[0]
    for j in range(1, parts_ref.shape[0]):
        e = e + parts_ref[j]
    k = iota((8, LANES), 1)
    message = jnp.where(k < own, amp * e + noise * own_b_ref[...], e)
    w_ref[...] = message
    for i in range(out_ref.shape[0]):
        out_ref[i] = message


def residual_kernel(own, gw_ref, b_ref, w_ref, own_b_ref, consts_ref, vec_ref, out_ref, stats_ref):
    n_c = gw_ref.shape[0]
    step = step_of(own)
    consts = consts_ref[...]
    amp, noise = consts[:, :1], consts[:, 1:2]
    sums = gw_ref[0]
    for i in range(1, n_c):
        sums = sums + gw_ref[i]
    beb, norm = lane(sums, own), lane(sums, own + 1)
    curve = amp * beb + noise * norm
    alpha = norm / curve
    keep = iota((8, LANES), 1) < own
    w = jnp.where(keep, w_ref[...], 0.0)
    own_r = own_b_ref[...] - alpha * w
    for i in range(out_ref.shape[0]):
        out_ref[i] = own_r
    for i in range(0, n_c, step):
        at = slice(own * i, own * (i + step))
        b = b_ref[:, at].astype(F32)
        r = b[:8] + b[8:] - alpha * packed([gw_ref[j] for j in range(i, i + step)], own)
        hi = rounded(r)
        vec_ref[:, at] = jnp.concatenate([hi, r - hi], axis=0).astype(BF16)
    k = iota((8, LANES), 1)
    stats = jnp.zeros((8, LANES), F32)
    for j, v in enumerate((alpha, norm, curve, total(own_r * own_r), total(own_r * w))):
        stats = jnp.where(k == j, v, stats)
    stats_ref[...] = stats


def second_kernel(scale, height, width, rows_ref, cols_ref, vec_ref, out_ref):
    out_ref[...] = tile_product(rows_ref, cols_ref, vec_ref, scale, height, width)


def dots_kernel(own, t_ref, gr_ref, stats_ref, out_ref):
    n_r = gr_ref.shape[0]
    t = t_ref[...]
    rer = total(packed_all([gr_ref[i] for i in range(n_r)], own) * t)
    stats = stats_ref[...]
    rr, rw = stats[:, 3:4], stats[:, 4:5]
    k = iota((8, LANES), 1)
    scalars = jnp.where(k == own, rer, jnp.where(k == own + 1, rr, rw))
    for i in range(n_r):
        out_ref[i] = jnp.where(k < own, block_of(t, i, own), scalars)


def scalars_kernel(own, parts_ref, out_ref, sum_ref):
    e = parts_ref[0]
    for j in range(1, parts_ref.shape[0]):
        e = e + parts_ref[j]
    sum_ref[...] = e
    sub, k = iota((8, LANES), 0), iota((8, LANES), 1)
    row = jnp.zeros((8, LANES), F32)
    for j in range(3):
        row = jnp.where(k == 8 * j + sub, lane(e, own + j), row)
    row = jnp.sum(row, axis=0, keepdims=True)
    out_ref[...] = jnp.broadcast_to(row, out_ref.shape)


def last_kernel(own, gs_ref, stats_ref, sum_ref, w_ref, b_ref, consts_ref, x_ref, r_ref):
    row = jnp.sum(gs_ref[...], axis=0, keepdims=True)
    sub, k = iota((8, LANES), 0), iota((8, LANES), 1)
    rows = jnp.broadcast_to(row, (8, LANES))
    rer, rr, rw = (total(jnp.where(k == 8 * j + sub, rows, 0.0)) for j in range(3))
    stats, consts = stats_ref[...], consts_ref[...]
    alpha, norm, curve = stats[:, :1], stats[:, 1:2], stats[:, 2:3]
    amp, noise = consts[:, :1], consts[:, 1:2]
    b, w = b_ref[...], w_ref[...]
    r = b - alpha * w
    beta = rr / norm
    direction = r + beta * b
    image = amp * sum_ref[...] + noise * r + beta * w
    curve2 = amp * rer + noise * rr + 2.0 * beta * rw + beta * beta * curve
    alpha2 = rr / curve2
    x_ref[...] = (alpha * b + alpha2 * direction)[:, :own]
    r_ref[...] = (r - alpha2 * image)[:, :own]


def shards(samples, targets, amplitude, noise):
    own, features = samples.shape
    n_c, n_r = group(COLS), group(ROWS)
    scale = 4.0 * 2.0 / features * LOG2E
    depth = features + 16
    height, width = HEIGHT, WIDTH

    def array(*shape, dtype=F32):
        return jax.ShapeDtypeStruct(shape, dtype)

    tile = array(8, LANES)
    given = (samples.T, targets.T, amplitude.reshape(1, -1), noise.reshape(1, -1))
    mcols, mrows, b, consts = pl.pallas_call(
        pack_kernel,
        out_shape=(array(n_c, features + 8, LANES, dtype=BF16), array(n_r, features + 8, LANES, dtype=BF16), tile, tile),
        in_specs=[pl.BlockSpec(memory_space=pltpu.HBM)] * 4,
        scratch_shapes=[pltpu.VMEM(v.shape, v.dtype) for v in given] + [pltpu.SemaphoreType.DMA((4,))],
        compiler_params=WHOLE,
    )(*given)
    gcols = exchange(mcols, COLS)
    mrows, gcols = lax.optimization_barrier((mrows, gcols))
    grows = exchange(mrows, ROWS)
    cols, vec = pl.pallas_call(
        functools.partial(columns_kernel, own, features),
        out_shape=(array(n_c * own, depth, dtype=BF16), array(16, n_c * own, dtype=BF16)),
        compiler_params=LARGE,
        cost_estimate=pl.CostEstimate(flops=10**9, bytes_accessed=10**6, transcendentals=0),
    )(gcols)
    rows, parts = pl.pallas_call(
        functools.partial(first_kernel, scale, own, features, height, width),
        out_shape=(array(n_r * own, depth, dtype=BF16), array(n_r, 8, LANES)),
        compiler_params=LARGE,
    )(grows, cols, vec, b)
    parts = exchange(parts, ROWS)
    w, message = pl.pallas_call(
        functools.partial(image_kernel, own),
        out_shape=(tile, array(n_c, 8, LANES)),
        compiler_params=SMALL,
    )(parts, b, consts)
    gw = exchange(message, COLS)
    vec, message, stats = pl.pallas_call(
        functools.partial(residual_kernel, own),
        out_shape=(array(16, n_c * own, dtype=BF16), array(n_r, 8, LANES), tile),
        compiler_params=SMALL,
    )(gw, vec, w, b, consts)
    gr = exchange(message, ROWS)
    t = pl.pallas_call(
        functools.partial(second_kernel, scale, height, width),
        out_shape=array(8, n_r * own),
        compiler_params=LARGE,
        cost_estimate=pl.CostEstimate(
            flops=2 * 2 * 256 * n_r * n_c * own * own,
            bytes_accessed=n_r * n_c * own * own,
            transcendentals=n_r * n_c * own * own,
        ),
    )(rows, cols, vec)
    parts = pl.pallas_call(
        functools.partial(dots_kernel, own),
        out_shape=array(n_r, 8, LANES),
        compiler_params=SMALL,
    )(t, gr, stats)
    parts = exchange(parts, ROWS)
    message, sums = pl.pallas_call(
        functools.partial(scalars_kernel, own),
        out_shape=(array(n_c, LANES), tile),
        compiler_params=SMALL,
    )(parts)
    gs = exchange(message, COLS)
    x, r = pl.pallas_call(
        functools.partial(last_kernel, own),
        out_shape=(array(8, own), array(8, own)),
        compiler_params=SMALL,
    )(gs, stats, sums, w, b, consts)
    return x.T, r.T


HEIGHT, WIDTH = 256, 512


def solution(mesh):
    fine = Mesh(mesh.devices.reshape(SIZES), AXES)
    split = P(AXES, None)
    return jax.shard_map(
        shards,
        mesh=fine,
        in_specs=(split, split, P(), P()),
        out_specs=(split, split),
        check_vma=False,
    )
```

```python
import functools
import math

import jax
import jax.numpy as jnp
import numpy as np
from jax import lax
from jax.experimental import pallas as pl
from jax.experimental.pallas import tpu as pltpu
from jax.sharding import Mesh
from jax.sharding import PartitionSpec as P

AXES = ("yh", "z", "core", "x", "yl")
SIZES = (4, 8, 2, 4, 2)
COLS = ("z", "yh")
ROWS = ("core", "x", "yl")
LANES = 128
LOG2E = 1.4426950408889634
F32 = jnp.float32
BF16 = jnp.bfloat16
SMALL = pltpu.CompilerParams(vmem_limit_bytes=4 * 1024 * 1024)
LARGE = pltpu.CompilerParams(vmem_limit_bytes=24 * 1024 * 1024)


def group(axes):
    return int(np.prod([SIZES[AXES.index(a)] for a in axes]))


def iota(shape, dim):
    return lax.broadcasted_iota(jnp.int32, shape, dim)


def rounded(v):
    return v.astype(BF16).astype(F32)


def lane(block, k):
    return total(jnp.where(iota(block.shape, 1) == k, block, 0.0))


def total(v):
    return jnp.sum(v, axis=1, keepdims=True)


def exchange(blocks, axes):
    return lax.all_to_all(blocks, axes, 0, 0)


def packed(blocks, own):
    k = iota(blocks[0].shape, 1)
    rolled = [b if own * i % LANES == 0 else pltpu.roll(b, own * i % LANES, 1) for i, b in enumerate(blocks)]
    outs = []
    for q in range(own * len(blocks) // LANES):
        out = None
        for i, b in enumerate(rolled):
            at = own * i - LANES * q
            if at + own <= 0 or at >= LANES:
                continue
            out = b if out is None else jnp.where(k < at, out, b)
        outs.append(out)
    return jnp.concatenate(outs, axis=1)


def block_of(dense, i, own):
    q, s = divmod(own * i, LANES)
    out = dense[:, LANES * q : LANES * (q + 1)]
    if s == 0:
        return out
    out = pltpu.roll(out, LANES - s, 1)
    if s + own > LANES:
        after = pltpu.roll(dense[:, LANES * (q + 1) : LANES * (q + 2)], LANES - s, 1)
        out = jnp.where(iota(out.shape, 1) < LANES - s, out, after)
    return out


def step_of(own):
    return LANES // math.gcd(own, LANES)


def pack_kernel(x_ref, b_ref, cols_ref, rows_ref, b_out_ref):
    own = x_ref.shape[1]
    b = b_ref[...]
    features, hole = x_ref.shape[0], LANES - own
    b_out = jnp.concatenate([b, jnp.zeros((8, hole), F32)], axis=1)
    lo = b_out - rounded(b_out)
    pieces = [pltpu.roll(lo, own - hole * i, 1) for i in range(own // hole)]
    pieces += [jnp.zeros((8, LANES), F32)] * (features // 8 - len(pieces))
    x = jnp.concatenate([x_ref[...].astype(F32), jnp.zeros((features, hole), F32)], axis=1)
    x = jnp.where(iota(x.shape, 1) < own, x, jnp.concatenate(pieces, axis=0))
    block = jnp.concatenate([x, rounded(b_out)], axis=0).astype(BF16)
    for i in range(cols_ref.shape[0]):
        cols_ref[i] = block
    for i in range(rows_ref.shape[0]):
        rows_ref[i] = block
    b_out_ref[...] = b_out


def operand(block, features, own, is_row):
    x = block[:features]
    half = 0.5 * jnp.sum(x * x, axis=0, keepdims=True)
    h1 = rounded(half)
    h2 = rounded(half - h1)
    h3 = half - h1 - h2
    k = iota((16, LANES), 0)
    at = 0 if is_row else 3
    pieces = jnp.where(k == at, -h1, jnp.where(k == at + 1, -h2, jnp.where(k == at + 2, -h3, 0.0)))
    ones = jnp.where((k >= 3 - at) & (k < 6 - at), 1.0, 0.0)
    return jnp.concatenate([x, pieces + ones], axis=0).T[:own].astype(BF16)


def tile_product(rows_ref, cols_ref, vec_ref, scale, height, width):
    n_rows, n_cols = rows_ref.shape[0], cols_ref.shape[0]
    outs = []
    for at in range(0, n_rows, height):
        rows = rows_ref[at : at + height, :]
        acc = jnp.zeros((vec_ref.shape[0], height), F32)
        for c in range(0, n_cols, width):
            inner = lax.dot_general(
                cols_ref[c : c + width, :], rows, (((1,), (1,)), ((), ())), preferred_element_type=F32
            )
            e = jnp.exp2(inner * scale)
            hi = e.astype(BF16)
            lo = (e - hi.astype(F32)).astype(BF16)
            vec = vec_ref[:, c : c + width]
            acc += jnp.dot(vec, hi, preferred_element_type=F32)
            acc += jnp.dot(vec, lo, preferred_element_type=F32)
        outs.append(acc[:8] + acc[8:])
    return jnp.concatenate(outs, axis=1)


def targets_of(block, features, own):
    hole = LANES - own
    k = iota((8, LANES), 1)
    lo = None
    for i in reversed(range(own // hole)):
        piece = pltpu.roll(block[8 * i : 8 * (i + 1)], hole * (i + 1), 1)
        lo = piece if lo is None else jnp.where(k < hole * (i + 1), piece, lo)
    return block[features : features + 8], lo


def packed_all(blocks, own):
    step = step_of(own)
    return jnp.concatenate([packed(blocks[i : i + step], own) for i in range(0, len(blocks), step)], axis=1)


def columns_kernel(own, features, gcols_ref, amp_ref, noise_ref, cols_ref, vec_ref, consts_ref):
    diagonal = iota((8, 8), 0) == iota((8, 8), 1)
    amp = total(jnp.where(diagonal, jnp.broadcast_to(amp_ref[...], (8, 8)), 0.0))
    noise = total(jnp.where(diagonal, jnp.broadcast_to(noise_ref[...], (8, 8)), 0.0))
    consts_ref[...] = jnp.where(iota((8, LANES), 1) == 0, amp, noise)
    n_c = gcols_ref.shape[0]
    step = step_of(own)
    for i in range(0, n_c, step):
        pieces = []
        for j in range(i, i + step):
            block = gcols_ref[j].astype(F32)
            cols_ref[own * j : own * (j + 1), :] = operand(block, features, own, False)
            pieces.append(jnp.concatenate(targets_of(block, features, own), axis=0))
        vec_ref[:, own * i : own * (i + step)] = packed(pieces, own).astype(BF16)


def first_kernel(scale, own, features, height, width, grows_ref, cols_ref, vec_ref, own_b_ref, rows_ref, out_ref):
    n_r = grows_ref.shape[0]
    targets = []
    for i in range(n_r):
        block = grows_ref[i].astype(F32)
        rows_ref[own * i : own * (i + 1), :] = operand(block, features, own, True)
        hi, lo = targets_of(block, features, own)
        targets.append(hi + lo)
    t = tile_product(rows_ref, cols_ref, vec_ref, scale, height, width)
    b = packed_all(targets, own)
    own_b = own_b_ref[...]
    beb, norm = total(b * t), total(own_b * own_b)
    k = iota((8, LANES), 1)
    for i in range(n_r):
        out_ref[i] = jnp.where(k < own, block_of(t, i, own), jnp.where(k == own, beb, norm))


def image_kernel(own, parts_ref, own_b_ref, consts_ref, w_ref, out_ref):
    consts = consts_ref[...]
    amp, noise = consts[:, :1], consts[:, 1:2]
    e = parts_ref[0]
    for j in range(1, parts_ref.shape[0]):
        e = e + parts_ref[j]
    k = iota((8, LANES), 1)
    message = jnp.where(k < own, amp * e + noise * own_b_ref[...], e)
    w_ref[...] = message
    for i in range(out_ref.shape[0]):
        out_ref[i] = message


def residual_kernel(own, gw_ref, w_ref, own_b_ref, consts_ref, out_ref, stats_ref):
    n_c = gw_ref.shape[0]
    consts = consts_ref[...]
    amp, noise = consts[:, :1], consts[:, 1:2]
    sums = gw_ref[0]
    for i in range(1, n_c):
        sums = sums + gw_ref[i]
    beb, norm = lane(sums, own), lane(sums, own + 1)
    curve = amp * beb + noise * norm
    alpha = norm / curve
    keep = iota((8, LANES), 1) < own
    w = jnp.where(keep, w_ref[...], 0.0)
    own_r = own_b_ref[...] - alpha * w
    for i in range(out_ref.shape[0]):
        out_ref[i] = own_r
    k = iota((8, LANES), 1)
    stats = jnp.zeros((8, LANES), F32)
    for j, v in enumerate((alpha, norm, curve, total(own_r * own_r), total(own_r * w))):
        stats = jnp.where(k == j, v, stats)
    stats_ref[...] = stats


def second_kernel(scale, own, height, width, rows_ref, cols_ref, b_ref, gw_ref, stats_ref, out_ref, vec_ref):
    n_c = gw_ref.shape[0]
    step = step_of(own)
    alpha = stats_ref[:, :1]
    for i in range(0, n_c, step):
        at = slice(own * i, own * (i + step))
        b = b_ref[:, at].astype(F32)
        r = b[:8] + b[8:] - alpha * packed([gw_ref[j] for j in range(i, i + step)], own)
        hi = rounded(r)
        vec_ref[:, at] = jnp.concatenate([hi, r - hi], axis=0).astype(BF16)
    out_ref[...] = tile_product(rows_ref, cols_ref, vec_ref, scale, height, width)


def dots_kernel(own, t_ref, gr_ref, stats_ref, out_ref):
    n_r = gr_ref.shape[0]
    t = t_ref[...]
    rer = total(packed_all([gr_ref[i] for i in range(n_r)], own) * t)
    stats = stats_ref[...]
    rr, rw = stats[:, 3:4], stats[:, 4:5]
    k = iota((8, LANES), 1)
    scalars = jnp.where(k == own, rer, jnp.where(k == own + 1, rr, rw))
    for i in range(n_r):
        out_ref[i] = jnp.where(k < own, block_of(t, i, own), scalars)


def scalars_kernel(own, parts_ref, out_ref, sum_ref):
    e = parts_ref[0]
    for j in range(1, parts_ref.shape[0]):
        e = e + parts_ref[j]
    sum_ref[...] = e
    sub, k = iota((8, LANES), 0), iota((8, LANES), 1)
    row = jnp.zeros((8, LANES), F32)
    for j in range(3):
        row = jnp.where(k == 8 * j + sub, lane(e, own + j), row)
    row = jnp.sum(row, axis=0, keepdims=True)
    out_ref[...] = jnp.broadcast_to(row, out_ref.shape)


def last_kernel(own, gs_ref, stats_ref, sum_ref, w_ref, b_ref, consts_ref, x_ref, r_ref):
    row = jnp.sum(gs_ref[...], axis=0, keepdims=True)
    sub, k = iota((8, LANES), 0), iota((8, LANES), 1)
    rows = jnp.broadcast_to(row, (8, LANES))
    rer, rr, rw = (total(jnp.where(k == 8 * j + sub, rows, 0.0)) for j in range(3))
    stats, consts = stats_ref[...], consts_ref[...]
    alpha, norm, curve = stats[:, :1], stats[:, 1:2], stats[:, 2:3]
    amp, noise = consts[:, :1], consts[:, 1:2]
    b, w = b_ref[...], w_ref[...]
    r = b - alpha * w
    beta = rr / norm
    direction = r + beta * b
    image = amp * sum_ref[...] + noise * r + beta * w
    curve2 = amp * rer + noise * rr + 2.0 * beta * rw + beta * beta * curve
    alpha2 = rr / curve2
    x_ref[...] = (alpha * b + alpha2 * direction)[:, :own]
    r_ref[...] = (r - alpha2 * image)[:, :own]


def shards(samples, targets, amplitude, noise):
    own, features = samples.shape
    n_c, n_r = group(COLS), group(ROWS)
    scale = 4.0 * 2.0 / features * LOG2E
    depth = features + 16
    height, width = HEIGHT, WIDTH

    def array(*shape, dtype=F32):
        return jax.ShapeDtypeStruct(shape, dtype)

    tile = array(8, LANES)
    mcols, mrows, b = pl.pallas_call(
        pack_kernel,
        out_shape=(
            array(n_c, features + 8, LANES, dtype=BF16),
            array(n_r, features + 8, LANES, dtype=BF16),
            tile,
        ),
        compiler_params=SMALL,
    )(samples.T, targets.T)
    gcols = exchange(mcols, COLS)
    mrows, gcols = lax.optimization_barrier((mrows, gcols))
    grows = exchange(mrows, ROWS)
    cols, vec, consts = pl.pallas_call(
        functools.partial(columns_kernel, own, features),
        out_shape=(array(n_c * own, depth, dtype=BF16), array(16, n_c * own, dtype=BF16), tile),
        compiler_params=LARGE,
        cost_estimate=pl.CostEstimate(flops=10**9, bytes_accessed=10**6, transcendentals=0),
    )(gcols, amplitude.reshape(1, -1), noise.reshape(1, -1))
    rows, parts = pl.pallas_call(
        functools.partial(first_kernel, scale, own, features, height, width),
        out_shape=(array(n_r * own, depth, dtype=BF16), array(n_r, 8, LANES)),
        compiler_params=LARGE,
    )(grows, cols, vec, b)
    parts = exchange(parts, ROWS)
    w, message = pl.pallas_call(
        functools.partial(image_kernel, own),
        out_shape=(tile, array(n_c, 8, LANES)),
        compiler_params=SMALL,
    )(parts, b, consts)
    gw = exchange(message, COLS)
    message, stats = pl.pallas_call(
        functools.partial(residual_kernel, own),
        out_shape=(array(n_r, 8, LANES), tile),
        compiler_params=SMALL,
    )(gw, w, b, consts)
    gr = exchange(message, ROWS)
    t = pl.pallas_call(
        functools.partial(second_kernel, scale, own, height, width),
        out_shape=array(8, n_r * own),
        scratch_shapes=[pltpu.VMEM((16, n_c * own), BF16)],
        compiler_params=LARGE,
        cost_estimate=pl.CostEstimate(
            flops=2 * 2 * 256 * n_r * n_c * own * own,
            bytes_accessed=n_r * n_c * own * own,
            transcendentals=n_r * n_c * own * own,
        ),
    )(rows, cols, vec, gw, stats)
    parts = pl.pallas_call(
        functools.partial(dots_kernel, own),
        out_shape=array(n_r, 8, LANES),
        compiler_params=SMALL,
    )(t, gr, stats)
    parts = exchange(parts, ROWS)
    message, sums = pl.pallas_call(
        functools.partial(scalars_kernel, own),
        out_shape=(array(n_c, LANES), tile),
        compiler_params=SMALL,
    )(parts)
    gs = exchange(message, COLS)
    x, r = pl.pallas_call(
        functools.partial(last_kernel, own),
        out_shape=(array(8, own), array(8, own)),
        compiler_params=SMALL,
    )(gs, stats, sums, w, b, consts)
    return x.T, r.T


HEIGHT, WIDTH = 256, 512


def solution(mesh):
    fine = Mesh(mesh.devices.reshape(SIZES), AXES)
    split = P(AXES, None)
    return jax.shard_map(
        shards,
        mesh=fine,
        in_specs=(split, split, P(), P()),
        out_specs=(split, split),
        check_vma=False,
    )
```

```python
import functools
import math

import jax
import jax.numpy as jnp
import numpy as np
from jax import lax
from jax.experimental import pallas as pl
from jax.experimental.pallas import tpu as pltpu
from jax.sharding import Mesh
from jax.sharding import PartitionSpec as P

AXES = ("yh", "z", "core", "x", "yl")
SIZES = (4, 8, 2, 4, 2)
COLS = ("z", "yh")
ROWS = ("core", "x", "yl")
LANES = 128
LOG2E = 1.4426950408889634
F32 = jnp.float32
BF16 = jnp.bfloat16
SMALL = pltpu.CompilerParams(vmem_limit_bytes=4 * 1024 * 1024)
LARGE = pltpu.CompilerParams(vmem_limit_bytes=24 * 1024 * 1024)


def group(axes):
    return int(np.prod([SIZES[AXES.index(a)] for a in axes]))


def iota(shape, dim):
    return lax.broadcasted_iota(jnp.int32, shape, dim)


def rounded(v):
    return v.astype(BF16).astype(F32)


def lane(block, k):
    return total(jnp.where(iota(block.shape, 1) == k, block, 0.0))


def total(v):
    return jnp.sum(v, axis=1, keepdims=True)


def exchange(blocks, axes):
    return lax.all_to_all(blocks, axes, 0, 0)


def packed(blocks, own):
    k = iota(blocks[0].shape, 1)
    rolled = [b if own * i % LANES == 0 else pltpu.roll(b, own * i % LANES, 1) for i, b in enumerate(blocks)]
    outs = []
    for q in range(own * len(blocks) // LANES):
        out = None
        for i, b in enumerate(rolled):
            at = own * i - LANES * q
            if at + own <= 0 or at >= LANES:
                continue
            out = b if out is None else jnp.where(k < at, out, b)
        outs.append(out)
    return jnp.concatenate(outs, axis=1)


def block_of(dense, i, own):
    q, s = divmod(own * i, LANES)
    out = dense[:, LANES * q : LANES * (q + 1)]
    if s == 0:
        return out
    out = pltpu.roll(out, LANES - s, 1)
    if s + own > LANES:
        after = pltpu.roll(dense[:, LANES * (q + 1) : LANES * (q + 2)], LANES - s, 1)
        out = jnp.where(iota(out.shape, 1) < LANES - s, out, after)
    return out


def step_of(own):
    return LANES // math.gcd(own, LANES)


def pack_kernel(x_hbm, b_hbm, cols_ref, rows_ref, b_out_ref, x_ref, b_ref, sems):
    copies = [pltpu.make_async_copy(x_hbm, x_ref, sems.at[0]), pltpu.make_async_copy(b_hbm, b_ref, sems.at[1])]
    for copy in copies:
        copy.start()
    for copy in copies:
        copy.wait()
    own = b_ref.shape[1]
    b = b_ref[...]
    features, hole = x_ref.shape[0], LANES - own
    b_out = jnp.concatenate([b, jnp.zeros((8, hole), F32)], axis=1)
    hi = rounded(b_out)
    pieces = [pltpu.roll(b_out - hi, own - hole * i, 1) for i in range(own // hole)]
    pieces += [jnp.zeros((8, LANES), F32)] * (features // 8 - len(pieces))
    x = jnp.concatenate([x_ref[...].astype(F32), jnp.zeros((features, hole), F32)], axis=1)
    x = jnp.where(iota(x.shape, 1) < own, x, jnp.concatenate(pieces, axis=0))
    block = jnp.concatenate([x, hi], axis=0).astype(BF16)
    for i in range(cols_ref.shape[0]):
        cols_ref[i] = block
    for i in range(rows_ref.shape[0]):
        rows_ref[i] = block
    b_out_ref[...] = b_out


def operand(block, features, own, is_row):
    x = block[:features]
    half = 0.5 * jnp.sum(x * x, axis=0, keepdims=True)
    h1 = rounded(half)
    h2 = rounded(half - h1)
    h3 = half - h1 - h2
    k = iota((16, LANES), 0)
    at = 0 if is_row else 3
    pieces = jnp.where(k == at, -h1, jnp.where(k == at + 1, -h2, jnp.where(k == at + 2, -h3, 0.0)))
    ones = jnp.where((k >= 3 - at) & (k < 6 - at), 1.0, 0.0)
    return jnp.concatenate([x, pieces + ones], axis=0).T[:own].astype(BF16)


def tile_product(rows_ref, cols_ref, vec_ref, scale, height, width):
    n_rows, n_cols = rows_ref.shape[0], cols_ref.shape[0]
    outs = []
    for at in range(0, n_rows, height):
        rows = rows_ref[at : at + height, :]
        acc = jnp.zeros((vec_ref.shape[0], height), F32)
        for c in range(0, n_cols, width):
            inner = lax.dot_general(
                cols_ref[c : c + width, :], rows, (((1,), (1,)), ((), ())), preferred_element_type=F32
            )
            e = jnp.exp2(inner * scale)
            hi = e.astype(BF16)
            lo = (e - hi.astype(F32)).astype(BF16)
            vec = vec_ref[:, c : c + width]
            acc += jnp.dot(vec, hi, preferred_element_type=F32)
            acc += jnp.dot(vec, lo, preferred_element_type=F32)
        outs.append(acc[:8] + acc[8:])
    return jnp.concatenate(outs, axis=1)


def targets_of(block, features, own):
    hole = LANES - own
    k = iota((8, LANES), 1)
    lo = None
    for i in reversed(range(own // hole)):
        piece = pltpu.roll(block[8 * i : 8 * (i + 1)], hole * (i + 1), 1)
        lo = piece if lo is None else jnp.where(k < hole * (i + 1), piece, lo)
    return block[features : features + 8], lo


def packed_all(blocks, own):
    step = step_of(own)
    return jnp.concatenate([packed(blocks[i : i + step], own) for i in range(0, len(blocks), step)], axis=1)


def columns_kernel(own, features, gcols_ref, amp_ref, noise_ref, cols_ref, vec_ref, consts_ref):
    diagonal = iota((8, 8), 0) == iota((8, 8), 1)
    amp = total(jnp.where(diagonal, jnp.broadcast_to(amp_ref[...], (8, 8)), 0.0))
    noise = total(jnp.where(diagonal, jnp.broadcast_to(noise_ref[...], (8, 8)), 0.0))
    consts_ref[...] = jnp.where(iota((8, LANES), 1) == 0, amp, noise)
    n_c = gcols_ref.shape[0]
    step = step_of(own)
    for i in range(0, n_c, step):
        pieces = []
        for j in range(i, i + step):
            block = gcols_ref[j].astype(F32)
            cols_ref[own * j : own * (j + 1), :] = operand(block, features, own, False)
            pieces.append(jnp.concatenate(targets_of(block, features, own), axis=0))
        vec_ref[:, own * i : own * (i + step)] = packed(pieces, own).astype(BF16)


def first_kernel(scale, own, features, height, width, grows_ref, cols_ref, vec_ref, own_b_ref, rows_ref, out_ref):
    n_r = grows_ref.shape[0]
    targets = []
    for i in range(n_r):
        block = grows_ref[i].astype(F32)
        rows_ref[own * i : own * (i + 1), :] = operand(block, features, own, True)
        hi, lo = targets_of(block, features, own)
        targets.append(hi + lo)
    t = tile_product(rows_ref, cols_ref, vec_ref, scale, height, width)
    b = packed_all(targets, own)
    own_b = own_b_ref[...]
    beb, norm = total(b * t), total(own_b * own_b)
    k = iota((8, LANES), 1)
    for i in range(n_r):
        out_ref[i] = jnp.where(k < own, block_of(t, i, own), jnp.where(k == own, beb, norm))


def image_kernel(own, parts_ref, own_b_ref, consts_ref, w_ref, out_ref):
    consts = consts_ref[...]
    amp, noise = consts[:, :1], consts[:, 1:2]
    e = parts_ref[0]
    for j in range(1, parts_ref.shape[0]):
        e = e + parts_ref[j]
    k = iota((8, LANES), 1)
    message = jnp.where(k < own, amp * e + noise * own_b_ref[...], e)
    w_ref[...] = message
    for i in range(out_ref.shape[0]):
        out_ref[i] = message


def residual_kernel(own, gw_ref, w_ref, own_b_ref, consts_ref, out_ref, stats_ref):
    n_c = gw_ref.shape[0]
    consts = consts_ref[...]
    amp, noise = consts[:, :1], consts[:, 1:2]
    sums = gw_ref[0]
    for i in range(1, n_c):
        sums = sums + gw_ref[i]
    beb, norm = lane(sums, own), lane(sums, own + 1)
    curve = amp * beb + noise * norm
    alpha = norm / curve
    keep = iota((8, LANES), 1) < own
    w = jnp.where(keep, w_ref[...], 0.0)
    own_r = own_b_ref[...] - alpha * w
    for i in range(out_ref.shape[0]):
        out_ref[i] = own_r
    k = iota((8, LANES), 1)
    stats = jnp.zeros((8, LANES), F32)
    for j, v in enumerate((alpha, norm, curve, total(own_r * own_r), total(own_r * w))):
        stats = jnp.where(k == j, v, stats)
    stats_ref[...] = stats


def second_kernel(scale, own, height, width, rows_ref, cols_ref, b_ref, gw_ref, stats_ref, out_ref, vec_ref):
    n_c = gw_ref.shape[0]
    step = step_of(own)
    alpha = stats_ref[:, :1]
    for i in range(0, n_c, step):
        at = slice(own * i, own * (i + step))
        b = b_ref[:, at].astype(F32)
        r = b[:8] + b[8:] - alpha * packed([gw_ref[j] for j in range(i, i + step)], own)
        hi = rounded(r)
        vec_ref[:, at] = jnp.concatenate([hi, r - hi], axis=0).astype(BF16)
    out_ref[...] = tile_product(rows_ref, cols_ref, vec_ref, scale, height, width)


def dots_kernel(own, t_ref, gr_ref, stats_ref, out_ref):
    n_r = gr_ref.shape[0]
    t = t_ref[...]
    rer = total(packed_all([gr_ref[i] for i in range(n_r)], own) * t)
    stats = stats_ref[...]
    rr, rw = stats[:, 3:4], stats[:, 4:5]
    k = iota((8, LANES), 1)
    scalars = jnp.where(k == own, rer, jnp.where(k == own + 1, rr, rw))
    for i in range(n_r):
        out_ref[i] = jnp.where(k < own, block_of(t, i, own), scalars)


def scalars_kernel(own, parts_ref, out_ref, sum_ref):
    e = parts_ref[0]
    for j in range(1, parts_ref.shape[0]):
        e = e + parts_ref[j]
    sum_ref[...] = e
    sub, k = iota((8, LANES), 0), iota((8, LANES), 1)
    row = jnp.zeros((8, LANES), F32)
    for j in range(3):
        row = jnp.where(k == 8 * j + sub, lane(e, own + j), row)
    row = jnp.sum(row, axis=0, keepdims=True)
    out_ref[...] = jnp.broadcast_to(row, out_ref.shape)


def last_kernel(own, gs_ref, stats_ref, sum_ref, w_ref, b_ref, consts_ref, x_ref, r_ref):
    row = jnp.sum(gs_ref[...], axis=0, keepdims=True)
    sub, k = iota((8, LANES), 0), iota((8, LANES), 1)
    rows = jnp.broadcast_to(row, (8, LANES))
    rer, rr, rw = (total(jnp.where(k == 8 * j + sub, rows, 0.0)) for j in range(3))
    stats, consts = stats_ref[...], consts_ref[...]
    alpha, norm, curve = stats[:, :1], stats[:, 1:2], stats[:, 2:3]
    amp, noise = consts[:, :1], consts[:, 1:2]
    b, w = b_ref[...], w_ref[...]
    r = b - alpha * w
    beta = rr / norm
    direction = r + beta * b
    image = amp * sum_ref[...] + noise * r + beta * w
    curve2 = amp * rer + noise * rr + 2.0 * beta * rw + beta * beta * curve
    alpha2 = rr / curve2
    x_ref[...] = (alpha * b + alpha2 * direction)[:, :own]
    r_ref[...] = (r - alpha2 * image)[:, :own]


def shards(samples, targets, amplitude, noise):
    own, features = samples.shape
    n_c, n_r = group(COLS), group(ROWS)
    scale = 4.0 * 2.0 / features * LOG2E
    depth = features + 16
    height, width = HEIGHT, WIDTH

    def array(*shape, dtype=F32):
        return jax.ShapeDtypeStruct(shape, dtype)

    tile = array(8, LANES)
    given = [pltpu.with_memory_space_constraint(v, pltpu.HBM) for v in (samples.T, targets.T)]
    mcols, mrows, b = pl.pallas_call(
        pack_kernel,
        out_shape=(
            array(n_c, features + 8, LANES, dtype=BF16),
            pltpu.VMEM((n_r, features + 8, LANES), BF16),
            tile,
        ),
        in_specs=[pl.BlockSpec(memory_space=pltpu.HBM)] * 2,
        scratch_shapes=[pltpu.VMEM(v.shape, v.dtype) for v in given] + [pltpu.SemaphoreType.DMA((2,))],
        compiler_params=SMALL,
    )(*given)
    gcols = exchange(mcols, COLS)
    mrows, gcols = lax.optimization_barrier((mrows, gcols))
    grows = exchange(mrows, ROWS)
    cols, vec, consts = pl.pallas_call(
        functools.partial(columns_kernel, own, features),
        out_shape=(array(n_c * own, depth, dtype=BF16), array(16, n_c * own, dtype=BF16), tile),
        compiler_params=LARGE,
        cost_estimate=pl.CostEstimate(flops=10**9, bytes_accessed=10**6, transcendentals=0),
    )(gcols, amplitude.reshape(1, -1), noise.reshape(1, -1))
    rows, parts = pl.pallas_call(
        functools.partial(first_kernel, scale, own, features, height, width),
        out_shape=(array(n_r * own, depth, dtype=BF16), array(n_r, 8, LANES)),
        compiler_params=LARGE,
    )(grows, cols, vec, b)
    parts = exchange(parts, ROWS)
    w, message = pl.pallas_call(
        functools.partial(image_kernel, own),
        out_shape=(tile, array(n_c, 8, LANES)),
        compiler_params=SMALL,
    )(parts, b, consts)
    gw = exchange(message, COLS)
    message, stats = pl.pallas_call(
        functools.partial(residual_kernel, own),
        out_shape=(pltpu.VMEM((n_r, 8, LANES), F32), tile),
        compiler_params=SMALL,
    )(gw, w, b, consts)
    gr = exchange(message, ROWS)
    t = pl.pallas_call(
        functools.partial(second_kernel, scale, own, height, width),
        out_shape=array(8, n_r * own),
        scratch_shapes=[pltpu.VMEM((16, n_c * own), BF16)],
        compiler_params=LARGE,
        cost_estimate=pl.CostEstimate(
            flops=2 * 2 * 256 * n_r * n_c * own * own,
            bytes_accessed=n_r * n_c * own * own,
            transcendentals=n_r * n_c * own * own,
        ),
    )(rows, cols, vec, gw, stats)
    parts = pl.pallas_call(
        functools.partial(dots_kernel, own),
        out_shape=array(n_r, 8, LANES),
        compiler_params=SMALL,
    )(t, gr, stats)
    parts = exchange(parts, ROWS)
    message, sums = pl.pallas_call(
        functools.partial(scalars_kernel, own),
        out_shape=(array(n_c, LANES), tile),
        compiler_params=SMALL,
    )(parts)
    gs = exchange(message, COLS)
    x, r = pl.pallas_call(
        functools.partial(last_kernel, own),
        out_shape=(array(8, own), array(8, own)),
        compiler_params=SMALL,
    )(gs, stats, sums, w, b, consts)
    return x.T, r.T


HEIGHT, WIDTH = 256, 512


def solution(mesh):
    fine = Mesh(mesh.devices.reshape(SIZES), AXES)
    split = P(AXES, None)
    return jax.shard_map(
        shards,
        mesh=fine,
        in_specs=(split, split, P(), P()),
        out_specs=(split, split),
        check_vma=False,
    )
```

```python
import functools
import math

import jax
import jax.numpy as jnp
import numpy as np
from jax import lax
from jax.experimental import pallas as pl
from jax.experimental.pallas import tpu as pltpu
from jax.sharding import Mesh
from jax.sharding import PartitionSpec as P

AXES = ("yh", "z", "core", "x", "yl")
SIZES = (4, 8, 2, 4, 2)
COLS = ("z", "yh")
ROWS = ("core", "x", "yl")
CHIP = "core"
CHIPS = ("x", "yl")
LANES = 128
LOG2E = 1.4426950408889634
F32 = jnp.float32
BF16 = jnp.bfloat16
SMALL = pltpu.CompilerParams(vmem_limit_bytes=4 * 1024 * 1024)
LARGE = pltpu.CompilerParams(vmem_limit_bytes=24 * 1024 * 1024)


def group(axes):
    return int(np.prod([SIZES[AXES.index(a)] for a in axes]))


def iota(shape, dim):
    return lax.broadcasted_iota(jnp.int32, shape, dim)


def rounded(v):
    return v.astype(BF16).astype(F32)


def lane(block, k):
    return total(jnp.where(iota(block.shape, 1) == k, block, 0.0))


def total(v):
    return jnp.sum(v, axis=1, keepdims=True)


def exchange(blocks, axes):
    return lax.all_to_all(blocks, axes, 0, 0)


def packed(blocks, own):
    k = iota(blocks[0].shape, 1)
    rolled = [b if own * i % LANES == 0 else pltpu.roll(b, own * i % LANES, 1) for i, b in enumerate(blocks)]
    outs = []
    for q in range(own * len(blocks) // LANES):
        out = None
        for i, b in enumerate(rolled):
            at = own * i - LANES * q
            if at + own <= 0 or at >= LANES:
                continue
            out = b if out is None else jnp.where(k < at, out, b)
        outs.append(out)
    return jnp.concatenate(outs, axis=1)


def block_of(dense, i, own):
    q, s = divmod(own * i, LANES)
    out = dense[:, LANES * q : LANES * (q + 1)]
    if s == 0:
        return out
    out = pltpu.roll(out, LANES - s, 1)
    if s + own > LANES:
        after = pltpu.roll(dense[:, LANES * (q + 1) : LANES * (q + 2)], LANES - s, 1)
        out = jnp.where(iota(out.shape, 1) < LANES - s, out, after)
    return out


def step_of(own):
    return LANES // math.gcd(own, LANES)


def pack_kernel(x_hbm, b_hbm, cols_ref, rows_ref, b_out_ref, x_ref, b_ref, sems):
    copies = [pltpu.make_async_copy(x_hbm, x_ref, sems.at[0]), pltpu.make_async_copy(b_hbm, b_ref, sems.at[1])]
    for copy in copies:
        copy.start()
    for copy in copies:
        copy.wait()
    own = b_ref.shape[1]
    b = b_ref[...]
    features, hole = x_ref.shape[0], LANES - own
    b_out = jnp.concatenate([b, jnp.zeros((8, hole), F32)], axis=1)
    hi = rounded(b_out)
    pieces = [pltpu.roll(b_out - hi, own - hole * i, 1) for i in range(own // hole)]
    pieces += [jnp.zeros((8, LANES), F32)] * (features // 8 - len(pieces))
    x = jnp.concatenate([x_ref[...].astype(F32), jnp.zeros((features, hole), F32)], axis=1)
    x = jnp.where(iota(x.shape, 1) < own, x, jnp.concatenate(pieces, axis=0))
    block = jnp.concatenate([x, hi], axis=0).astype(BF16)
    for i in range(cols_ref.shape[0]):
        cols_ref[i] = block
    for i in range(rows_ref.shape[0]):
        rows_ref[i] = block
    b_out_ref[...] = b_out


def operand(block, features, own, is_row):
    x = block[:features]
    half = 0.5 * jnp.sum(x * x, axis=0, keepdims=True)
    h1 = rounded(half)
    h2 = rounded(half - h1)
    h3 = half - h1 - h2
    k = iota((16, LANES), 0)
    at = 0 if is_row else 3
    pieces = jnp.where(k == at, -h1, jnp.where(k == at + 1, -h2, jnp.where(k == at + 2, -h3, 0.0)))
    ones = jnp.where((k >= 3 - at) & (k < 6 - at), 1.0, 0.0)
    return jnp.concatenate([x, pieces + ones], axis=0).T[:own].astype(BF16)


def tile_product(rows_ref, cols_ref, vec_ref, scale, height, width):
    n_rows, n_cols = rows_ref.shape[0], cols_ref.shape[0]
    outs = []
    for at in range(0, n_rows, height):
        rows = rows_ref[at : at + height, :]
        acc = jnp.zeros((vec_ref.shape[0], height), F32)
        for c in range(0, n_cols, width):
            inner = lax.dot_general(
                cols_ref[c : c + width, :], rows, (((1,), (1,)), ((), ())), preferred_element_type=F32
            )
            e = jnp.exp2(inner * scale)
            hi = e.astype(BF16)
            lo = (e - hi.astype(F32)).astype(BF16)
            vec = vec_ref[:, c : c + width]
            acc += jnp.dot(vec, hi, preferred_element_type=F32)
            acc += jnp.dot(vec, lo, preferred_element_type=F32)
        outs.append(acc[:8] + acc[8:])
    return jnp.concatenate(outs, axis=1)


def targets_of(block, features, own):
    hole = LANES - own
    k = iota((8, LANES), 1)
    lo = None
    for i in reversed(range(own // hole)):
        piece = pltpu.roll(block[8 * i : 8 * (i + 1)], hole * (i + 1), 1)
        lo = piece if lo is None else jnp.where(k < hole * (i + 1), piece, lo)
    return block[features : features + 8], lo


def packed_all(blocks, own):
    step = step_of(own)
    return jnp.concatenate([packed(blocks[i : i + step], own) for i in range(0, len(blocks), step)], axis=1)


def columns_kernel(own, features, gcols_ref, amp_ref, noise_ref, cols_ref, vec_ref, consts_ref):
    diagonal = iota((8, 8), 0) == iota((8, 8), 1)
    amp = total(jnp.where(diagonal, jnp.broadcast_to(amp_ref[...], (8, 8)), 0.0))
    noise = total(jnp.where(diagonal, jnp.broadcast_to(noise_ref[...], (8, 8)), 0.0))
    consts_ref[...] = jnp.where(iota((8, LANES), 1) == 0, amp, noise)
    n_c = gcols_ref.shape[0]
    step = step_of(own)
    for i in range(0, n_c, step):
        pieces = []
        for j in range(i, i + step):
            block = gcols_ref[j].astype(F32)
            cols_ref[own * j : own * (j + 1), :] = operand(block, features, own, False)
            pieces.append(jnp.concatenate(targets_of(block, features, own), axis=0))
        vec_ref[:, own * i : own * (i + step)] = packed(pieces, own).astype(BF16)


def first_kernel(scale, own, features, height, width, grows_ref, cols_ref, vec_ref, rows_ref, out_ref, b_ref):
    n_r = grows_ref.shape[0]
    targets = []
    for i in range(n_r):
        block = grows_ref[i].astype(F32)
        rows_ref[own * i : own * (i + 1), :] = operand(block, features, own, True)
        hi, lo = targets_of(block, features, own)
        targets.append(hi + lo)
    b_ref[...] = packed_all(targets, own)
    out_ref[...] = tile_product(rows_ref, cols_ref, vec_ref, scale, height, width)


def chip_kernel(parts_ref, out_ref):
    e = parts_ref[0]
    for j in range(1, parts_ref.shape[0]):
        e = e + parts_ref[j]
    for i in range(out_ref.shape[0]):
        out_ref[i] = e


def image_kernel(own, parts_ref, b_ref, own_b_ref, consts_ref, w_ref, own_w_ref, out_ref, blocks_ref):
    consts = consts_ref[...]
    amp, noise = consts[:, :1], consts[:, 1:2]
    e = parts_ref[0]
    for j in range(1, parts_ref.shape[0]):
        e = e + parts_ref[j]
    b = b_ref[...]
    w = amp * e + noise * b
    w_ref[...] = w
    curve, norm = total(b * w), total(b * b)
    for i in range(blocks_ref.shape[0]):
        blocks_ref[i] = block_of(e, i, own)
    me = 0
    for axis in ROWS:
        me = me * group((axis,)) + lax.axis_index(axis)
    own_w = amp * blocks_ref[me] + noise * own_b_ref[...]
    own_w_ref[...] = own_w
    k = iota((8, LANES), 1)
    message = jnp.where(k < own, own_w, jnp.where(k == own, curve, norm))
    for i in range(out_ref.shape[0]):
        out_ref[i] = message


def second_kernel(scale, own, height, width, rows_ref, cols_ref, vec_ref, gw_ref, w_ref, b_ref, out_ref, stats_ref, res_ref):
    n_c, n_r = gw_ref.shape[0], out_ref.shape[0]
    step = step_of(own)
    sums = gw_ref[0]
    for i in range(1, n_c):
        sums = sums + gw_ref[i]
    curve, norm = lane(sums, own), lane(sums, own + 1)
    alpha = norm / curve
    for i in range(0, n_c, step):
        at = slice(own * i, own * (i + step))
        b = vec_ref[:, at].astype(F32)
        r = b[:8] + b[8:] - alpha * packed([gw_ref[j] for j in range(i, i + step)], own)
        hi = rounded(r)
        res_ref[:, at] = jnp.concatenate([hi, r - hi], axis=0).astype(BF16)
    w = w_ref[...]
    r = b_ref[...] - alpha * w
    k = iota((8, LANES), 1)
    stats = jnp.zeros((8, LANES), F32)
    for j, v in enumerate((alpha, norm, curve, total(r * r), total(r * w))):
        stats = jnp.where(k == j, v, stats)
    stats_ref[...] = stats
    t = tile_product(rows_ref, cols_ref, res_ref, scale, height, width)
    rer = total(r * t)
    for i in range(n_r):
        out_ref[i] = jnp.where(k < own, block_of(t, i, own), rer)


def scalars_kernel(own, parts_ref, stats_ref, out_ref, sum_ref):
    e = parts_ref[0]
    for j in range(1, parts_ref.shape[0]):
        e = e + parts_ref[j]
    sum_ref[...] = e
    sub, k = iota((8, LANES), 0), iota((8, LANES), 1)
    row = jnp.zeros((8, LANES), F32)
    stats = stats_ref[...]
    for j, v in enumerate((lane(e, own), stats[:, 3:4], stats[:, 4:5])):
        row = jnp.where(k == 8 * j + sub, v, row)
    row = jnp.sum(row, axis=0, keepdims=True)
    out_ref[...] = jnp.broadcast_to(row, out_ref.shape)


def last_kernel(own, gs_ref, stats_ref, sum_ref, w_ref, b_ref, consts_ref, x_ref, r_ref):
    row = jnp.sum(gs_ref[...], axis=0, keepdims=True)
    sub, k = iota((8, LANES), 0), iota((8, LANES), 1)
    rows = jnp.broadcast_to(row, (8, LANES))
    rer, rr, rw = (total(jnp.where(k == 8 * j + sub, rows, 0.0)) for j in range(3))
    stats, consts = stats_ref[...], consts_ref[...]
    alpha, norm, curve = stats[:, :1], stats[:, 1:2], stats[:, 2:3]
    amp, noise = consts[:, :1], consts[:, 1:2]
    b, w = b_ref[...], w_ref[...]
    r = b - alpha * w
    beta = rr / norm
    direction = r + beta * b
    image = amp * sum_ref[...] + noise * r + beta * w
    curve2 = amp * rer + noise * rr + 2.0 * beta * rw + beta * beta * curve
    alpha2 = rr / curve2
    x_ref[...] = (alpha * b + alpha2 * direction)[:, :own]
    r_ref[...] = (r - alpha2 * image)[:, :own]


def shards(samples, targets, amplitude, noise):
    own, features = samples.shape
    n_c, n_r = group(COLS), group(ROWS)
    scale = 4.0 * 2.0 / features * LOG2E
    depth = features + 16
    height, width = HEIGHT, WIDTH

    def array(*shape, dtype=F32):
        return jax.ShapeDtypeStruct(shape, dtype)

    tile = array(8, LANES)
    given = [pltpu.with_memory_space_constraint(v, pltpu.HBM) for v in (samples.T, targets.T)]
    mcols, mrows, b = pl.pallas_call(
        pack_kernel,
        out_shape=(
            array(n_c, features + 8, LANES, dtype=BF16),
            pltpu.VMEM((n_r, features + 8, LANES), BF16),
            tile,
        ),
        in_specs=[pl.BlockSpec(memory_space=pltpu.HBM)] * 2,
        scratch_shapes=[pltpu.VMEM(v.shape, v.dtype) for v in given] + [pltpu.SemaphoreType.DMA((2,))],
        compiler_params=SMALL,
    )(*given)
    gcols = exchange(mcols, COLS)
    mrows, gcols = lax.optimization_barrier((mrows, gcols))
    grows = exchange(mrows, ROWS)
    cols, vec, consts = pl.pallas_call(
        functools.partial(columns_kernel, own, features),
        out_shape=(array(n_c * own, depth, dtype=BF16), array(16, n_c * own, dtype=BF16), tile),
        compiler_params=LARGE,
        cost_estimate=pl.CostEstimate(flops=10**9, bytes_accessed=10**6, transcendentals=0),
    )(gcols, amplitude.reshape(1, -1), noise.reshape(1, -1))
    rows, t, b_rows = pl.pallas_call(
        functools.partial(first_kernel, scale, own, features, height, width),
        out_shape=(array(n_r * own, depth, dtype=BF16), array(8, n_r * own), array(8, n_r * own)),
        compiler_params=LARGE,
    )(grows, cols, vec)
    parts = pl.pallas_call(
        chip_kernel, out_shape=array(group(CHIPS), 8, n_r * own), compiler_params=SMALL
    )(lax.all_gather(t, CHIP))
    parts = exchange(parts, CHIPS)
    w_rows, w, message = pl.pallas_call(
        functools.partial(image_kernel, own),
        out_shape=(array(8, n_r * own), tile, array(n_c, 8, LANES)),
        scratch_shapes=[pltpu.VMEM((n_r, 8, LANES), F32)],
        compiler_params=SMALL,
    )(parts, b_rows, b, consts)
    gw = exchange(message, COLS)
    parts, stats = pl.pallas_call(
        functools.partial(second_kernel, scale, own, height, width),
        out_shape=(array(n_r, 8, LANES), tile),
        scratch_shapes=[pltpu.VMEM((16, n_c * own), BF16)],
        compiler_params=LARGE,
    )(rows, cols, vec, gw, w_rows, b_rows)
    parts = exchange(parts, ROWS)
    message, sums = pl.pallas_call(
        functools.partial(scalars_kernel, own),
        out_shape=(array(n_c, LANES), tile),
        compiler_params=SMALL,
    )(parts, stats)
    gs = exchange(message, COLS)
    x, r = pl.pallas_call(
        functools.partial(last_kernel, own),
        out_shape=(array(8, own), array(8, own)),
        compiler_params=SMALL,
    )(gs, stats, sums, w, b, consts)
    return x.T, r.T


HEIGHT, WIDTH = 256, 512


def solution(mesh):
    fine = Mesh(mesh.devices.reshape(SIZES), AXES)
    split = P(AXES, None)
    return jax.shard_map(
        shards,
        mesh=fine,
        in_specs=(split, split, P(), P()),
        out_specs=(split, split),
        check_vma=False,
    )
```

```python
import functools
import math

import jax
import jax.numpy as jnp
import numpy as np
from jax import lax
from jax.experimental import pallas as pl
from jax.experimental.pallas import tpu as pltpu
from jax.sharding import Mesh
from jax.sharding import PartitionSpec as P

AXES = ("yh", "z", "core", "x", "yl")
SIZES = (4, 8, 2, 4, 2)
COLS = ("z", "yh")
ROWS = ("core", "x", "yl")
CHIP = "core"
CHIPS = ("x", "yl")
LANES = 128
LOG2E = 1.4426950408889634
F32 = jnp.float32
BF16 = jnp.bfloat16
SMALL = pltpu.CompilerParams(vmem_limit_bytes=4 * 1024 * 1024)
LARGE = pltpu.CompilerParams(vmem_limit_bytes=24 * 1024 * 1024)


def group(axes):
    return int(np.prod([SIZES[AXES.index(a)] for a in axes]))


def iota(shape, dim):
    return lax.broadcasted_iota(jnp.int32, shape, dim)


def rounded(v):
    return v.astype(BF16).astype(F32)


def lane(block, k):
    return total(jnp.where(iota(block.shape, 1) == k, block, 0.0))


def total(v):
    return jnp.sum(v, axis=1, keepdims=True)


def exchange(blocks, axes):
    return lax.all_to_all(blocks, axes, 0, 0)


def packed(blocks, own):
    k = iota(blocks[0].shape, 1)
    rolled = [b if own * i % LANES == 0 else pltpu.roll(b, own * i % LANES, 1) for i, b in enumerate(blocks)]
    outs = []
    for q in range(own * len(blocks) // LANES):
        out = None
        for i, b in enumerate(rolled):
            at = own * i - LANES * q
            if at + own <= 0 or at >= LANES:
                continue
            out = b if out is None else jnp.where(k < at, out, b)
        outs.append(out)
    return jnp.concatenate(outs, axis=1)


def block_of(dense, i, own):
    q, s = divmod(own * i, LANES)
    out = dense[:, LANES * q : LANES * (q + 1)]
    if s == 0:
        return out
    out = pltpu.roll(out, LANES - s, 1)
    if s + own > LANES:
        after = pltpu.roll(dense[:, LANES * (q + 1) : LANES * (q + 2)], LANES - s, 1)
        out = jnp.where(iota(out.shape, 1) < LANES - s, out, after)
    return out


def step_of(own):
    return LANES // math.gcd(own, LANES)


def pack_kernel(x_hbm, b_hbm, cols_ref, rows_ref, b_out_ref, x_ref, b_ref, sems):
    copies = [pltpu.make_async_copy(x_hbm, x_ref, sems.at[0]), pltpu.make_async_copy(b_hbm, b_ref, sems.at[1])]
    for copy in copies:
        copy.start()
    for copy in copies:
        copy.wait()
    own = b_ref.shape[1]
    b = b_ref[...]
    features, hole = x_ref.shape[0], LANES - own
    b_out = jnp.concatenate([b, jnp.zeros((8, hole), F32)], axis=1)
    hi = rounded(b_out)
    pieces = [pltpu.roll(b_out - hi, own - hole * i, 1) for i in range(own // hole)]
    pieces += [jnp.zeros((8, LANES), F32)] * (features // 8 - len(pieces))
    x = jnp.concatenate([x_ref[...].astype(F32), jnp.zeros((features, hole), F32)], axis=1)
    x = jnp.where(iota(x.shape, 1) < own, x, jnp.concatenate(pieces, axis=0))
    block = jnp.concatenate([x, hi], axis=0).astype(BF16)
    for i in range(cols_ref.shape[0]):
        cols_ref[i] = block
    for i in range(rows_ref.shape[0]):
        rows_ref[i] = block
    b_out_ref[...] = b_out


def operand(block, features, own, is_row):
    x = block[:features]
    half = 0.5 * jnp.sum(x * x, axis=0, keepdims=True)
    h1 = rounded(half)
    h2 = rounded(half - h1)
    h3 = half - h1 - h2
    k = iota((16, LANES), 0)
    at = 0 if is_row else 3
    pieces = jnp.where(k == at, -h1, jnp.where(k == at + 1, -h2, jnp.where(k == at + 2, -h3, 0.0)))
    ones = jnp.where((k >= 3 - at) & (k < 6 - at), 1.0, 0.0)
    return jnp.concatenate([x, pieces + ones], axis=0).T[:own].astype(BF16)


def tile_product(rows_ref, cols_ref, vec_ref, scale, height, width):
    n_rows, n_cols = rows_ref.shape[0], cols_ref.shape[0]
    outs = []
    for at in range(0, n_rows, height):
        rows = rows_ref[at : at + height, :]
        acc = jnp.zeros((vec_ref.shape[0], height), F32)
        for c in range(0, n_cols, width):
            inner = lax.dot_general(
                cols_ref[c : c + width, :], rows, (((1,), (1,)), ((), ())), preferred_element_type=F32
            )
            e = jnp.exp2(inner * scale)
            hi = e.astype(BF16)
            lo = (e - hi.astype(F32)).astype(BF16)
            vec = vec_ref[:, c : c + width]
            acc += jnp.dot(vec, hi, preferred_element_type=F32)
            acc += jnp.dot(vec, lo, preferred_element_type=F32)
        outs.append(acc[:8] + acc[8:])
    return jnp.concatenate(outs, axis=1)


def targets_of(block, features, own):
    hole = LANES - own
    k = iota((8, LANES), 1)
    lo = None
    for i in reversed(range(own // hole)):
        piece = pltpu.roll(block[8 * i : 8 * (i + 1)], hole * (i + 1), 1)
        lo = piece if lo is None else jnp.where(k < hole * (i + 1), piece, lo)
    return block[features : features + 8], lo


def packed_all(blocks, own):
    step = step_of(own)
    return jnp.concatenate([packed(blocks[i : i + step], own) for i in range(0, len(blocks), step)], axis=1)


def columns_kernel(own, features, gcols_ref, amp_ref, noise_ref, cols_ref, vec_ref, consts_ref):
    diagonal = iota((8, 8), 0) == iota((8, 8), 1)
    amp = total(jnp.where(diagonal, jnp.broadcast_to(amp_ref[...], (8, 8)), 0.0))
    noise = total(jnp.where(diagonal, jnp.broadcast_to(noise_ref[...], (8, 8)), 0.0))
    consts_ref[...] = jnp.where(iota((8, LANES), 1) == 0, amp, noise)
    n_c = gcols_ref.shape[0]
    step = step_of(own)
    for i in range(0, n_c, step):
        pieces = []
        for j in range(i, i + step):
            block = gcols_ref[j].astype(F32)
            cols_ref[own * j : own * (j + 1), :] = operand(block, features, own, False)
            pieces.append(jnp.concatenate(targets_of(block, features, own), axis=0))
        vec_ref[:, own * i : own * (i + step)] = packed(pieces, own).astype(BF16)


def first_kernel(scale, own, features, height, width, grows_ref, cols_ref, vec_ref, rows_ref, out_ref, b_ref):
    n_r = grows_ref.shape[0]
    targets = []
    for i in range(n_r):
        block = grows_ref[i].astype(F32)
        rows_ref[own * i : own * (i + 1), :] = operand(block, features, own, True)
        hi, lo = targets_of(block, features, own)
        targets.append(hi + lo)
    b_ref[...] = packed_all(targets, own)
    out_ref[...] = tile_product(rows_ref, cols_ref, vec_ref, scale, height, width)


def chip_kernel(parts_ref, out_ref):
    e = parts_ref[0]
    for j in range(1, parts_ref.shape[0]):
        e = e + parts_ref[j]
    for i in range(out_ref.shape[0]):
        out_ref[i] = e


def image_kernel(own, parts_ref, b_ref, own_b_ref, consts_ref, vec_ref, own_w_ref, out_ref, blocks_ref):
    consts = consts_ref[...]
    amp, noise = consts[:, :1], consts[:, 1:2]
    e = parts_ref[0]
    for j in range(1, parts_ref.shape[0]):
        e = e + parts_ref[j]
    b = b_ref[...]
    w = amp * e + noise * b
    hi = rounded(w)
    vec_ref[...] = jnp.concatenate([hi, w - hi], axis=0).astype(BF16)
    curve, norm = total(b * w), total(b * b)
    for i in range(blocks_ref.shape[0]):
        blocks_ref[i] = block_of(e, i, own)
    me = 0
    for axis in ROWS:
        me = me * group((axis,)) + lax.axis_index(axis)
    own_w = amp * blocks_ref[me] + noise * own_b_ref[...]
    own_w_ref[...] = own_w
    k = iota((8, LANES), 1)
    message = jnp.where(k < own, own_w, jnp.where(k == own, curve, norm))
    for i in range(out_ref.shape[0]):
        out_ref[i] = message


def second_kernel(scale, height, width, rows_ref, cols_ref, vec_ref, out_ref):
    out_ref[...] = tile_product(cols_ref, rows_ref, vec_ref, scale, height, width)


def dots_kernel(own, u_ref, gw_ref, vec_ref, out_ref, stats_ref):
    n_c = gw_ref.shape[0]
    sums = gw_ref[0]
    for i in range(1, n_c):
        sums = sums + gw_ref[i]
    curve, norm = lane(sums, own), lane(sums, own + 1)
    alpha = norm / curve
    u = u_ref[...]
    w = packed_all([gw_ref[i] for i in range(n_c)], own)
    b = vec_ref[...].astype(F32)
    r = b[:8] + b[8:] - alpha * w
    rr, rw, ru = total(r * r), total(r * w), total(r * u)
    k = iota((8, LANES), 1)
    for i in range(n_c):
        out_ref[i] = jnp.where(k < own, block_of(u, i, own), ru)
    stats = jnp.zeros((8, LANES), F32)
    for j, v in enumerate((alpha, norm, curve, rr, rw)):
        stats = jnp.where(k == j, v, stats)
    stats_ref[...] = stats


def scalars_kernel(own, parts_ref, stats_ref, out_ref, sum_ref):
    e = parts_ref[0]
    for j in range(1, parts_ref.shape[0]):
        e = e + parts_ref[j]
    sum_ref[...] = e
    stats = stats_ref[...]
    sub, k = iota((8, LANES), 0), iota((8, LANES), 1)
    row = jnp.zeros((8, LANES), F32)
    for j, v in enumerate((lane(e, own), stats[:, 3:4], stats[:, 4:5])):
        row = jnp.where(k == 8 * j + sub, v, row)
    row = jnp.sum(row, axis=0, keepdims=True)
    out_ref[...] = jnp.broadcast_to(row, out_ref.shape)


def last_kernel(own, gs_ref, stats_ref, sum_ref, w_ref, b_ref, consts_ref, x_ref, r_ref):
    row = jnp.sum(gs_ref[...], axis=0, keepdims=True)
    sub, k = iota((8, LANES), 0), iota((8, LANES), 1)
    rows = jnp.broadcast_to(row, (8, LANES))
    ru, rr, rw = (total(jnp.where(k == 8 * j + sub, rows, 0.0)) for j in range(3))
    stats, consts = stats_ref[...], consts_ref[...]
    alpha, norm, curve = stats[:, :1], stats[:, 1:2], stats[:, 2:3]
    amp, noise = consts[:, :1], consts[:, 1:2]
    b, w = b_ref[...], w_ref[...]
    r = b - alpha * w
    beta = rr / norm
    direction = r + beta * b
    image = w - alpha * (amp * sum_ref[...] + noise * w) + beta * w
    curve2 = rw - alpha * (amp * ru + noise * rw) + 2.0 * beta * rw + beta * beta * curve
    alpha2 = rr / curve2
    x_ref[...] = (alpha * b + alpha2 * direction)[:, :own]
    r_ref[...] = (r - alpha2 * image)[:, :own]


def shards(samples, targets, amplitude, noise):
    own, features = samples.shape
    n_c, n_r = group(COLS), group(ROWS)
    scale = 4.0 * 2.0 / features * LOG2E
    depth = features + 16
    height, width = HEIGHT, WIDTH

    def array(*shape, dtype=F32):
        return jax.ShapeDtypeStruct(shape, dtype)

    tile = array(8, LANES)
    given = [pltpu.with_memory_space_constraint(v, pltpu.HBM) for v in (samples.T, targets.T)]
    mcols, mrows, b = pl.pallas_call(
        pack_kernel,
        out_shape=(
            array(n_c, features + 8, LANES, dtype=BF16),
            pltpu.VMEM((n_r, features + 8, LANES), BF16),
            tile,
        ),
        in_specs=[pl.BlockSpec(memory_space=pltpu.HBM)] * 2,
        scratch_shapes=[pltpu.VMEM(v.shape, v.dtype) for v in given] + [pltpu.SemaphoreType.DMA((2,))],
        compiler_params=SMALL,
    )(*given)
    gcols = exchange(mcols, COLS)
    mrows, gcols = lax.optimization_barrier((mrows, gcols))
    grows = exchange(mrows, ROWS)
    cols, vec, consts = pl.pallas_call(
        functools.partial(columns_kernel, own, features),
        out_shape=(array(n_c * own, depth, dtype=BF16), array(16, n_c * own, dtype=BF16), tile),
        compiler_params=LARGE,
        cost_estimate=pl.CostEstimate(flops=10**9, bytes_accessed=10**6, transcendentals=0),
    )(gcols, amplitude.reshape(1, -1), noise.reshape(1, -1))
    rows, t, b_rows = pl.pallas_call(
        functools.partial(first_kernel, scale, own, features, height, width),
        out_shape=(array(n_r * own, depth, dtype=BF16), array(8, n_r * own), array(8, n_r * own)),
        compiler_params=LARGE,
    )(grows, cols, vec)
    parts = pl.pallas_call(
        chip_kernel, out_shape=array(group(CHIPS), 8, n_r * own), compiler_params=SMALL
    )(lax.all_gather(t, CHIP))
    parts = exchange(parts, CHIPS)
    w_vec, w, message = pl.pallas_call(
        functools.partial(image_kernel, own),
        out_shape=(array(16, n_r * own, dtype=BF16), tile, array(n_c, 8, LANES)),
        scratch_shapes=[pltpu.VMEM((n_r, 8, LANES), F32)],
        compiler_params=SMALL,
    )(parts, b_rows, b, consts)
    gw = exchange(message, COLS)
    u = pl.pallas_call(
        functools.partial(second_kernel, scale, height, width),
        out_shape=array(8, n_c * own),
        compiler_params=LARGE,
        cost_estimate=pl.CostEstimate(
            flops=2 * 2 * 256 * n_r * n_c * own * own,
            bytes_accessed=n_r * n_c * own * own,
            transcendentals=n_r * n_c * own * own,
        ),
    )(rows, cols, w_vec)
    parts, stats = pl.pallas_call(
        functools.partial(dots_kernel, own),
        out_shape=(array(n_c, 8, LANES), tile),
        compiler_params=SMALL,
    )(u, gw, vec)
    parts = exchange(parts, COLS)
    message, sums = pl.pallas_call(
        functools.partial(scalars_kernel, own),
        out_shape=(array(n_r, LANES), tile),
        compiler_params=SMALL,
    )(parts, stats)
    gs = exchange(message, ROWS)
    x, r = pl.pallas_call(
        functools.partial(last_kernel, own),
        out_shape=(array(8, own), array(8, own)),
        compiler_params=SMALL,
    )(gs, stats, sums, w, b, consts)
    return x.T, r.T


HEIGHT, WIDTH = 256, 512


def solution(mesh):
    fine = Mesh(mesh.devices.reshape(SIZES), AXES)
    split = P(AXES, None)
    return jax.shard_map(
        shards,
        mesh=fine,
        in_specs=(split, split, P(), P()),
        out_specs=(split, split),
        check_vma=False,
    )
```

```python
import functools
import math

import jax
import jax.numpy as jnp
import numpy as np
from jax import lax
from jax.experimental import pallas as pl
from jax.experimental.pallas import tpu as pltpu
from jax.sharding import Mesh
from jax.sharding import PartitionSpec as P

AXES = ("yh", "z", "core", "x", "yl")
SIZES = (4, 8, 2, 4, 2)
COLS = ("z", "yh")
ROWS = ("core", "x", "yl")
CHIP = "core"
CHIPS = ("x", "yl")
LANES = 128
LOG2E = 1.4426950408889634
F32 = jnp.float32
BF16 = jnp.bfloat16
SMALL = pltpu.CompilerParams(vmem_limit_bytes=4 * 1024 * 1024)
LARGE = pltpu.CompilerParams(vmem_limit_bytes=24 * 1024 * 1024)


def group(axes):
    return int(np.prod([SIZES[AXES.index(a)] for a in axes]))


def iota(shape, dim):
    return lax.broadcasted_iota(jnp.int32, shape, dim)


def rounded(v):
    return v.astype(BF16).astype(F32)


def lane(block, k):
    return total(jnp.where(iota(block.shape, 1) == k, block, 0.0))


def total(v):
    return jnp.sum(v, axis=1, keepdims=True)


def exchange(blocks, axes):
    return lax.all_to_all(blocks, axes, 0, 0)


def packed(blocks, own):
    k = iota(blocks[0].shape, 1)
    rolled = [b if own * i % LANES == 0 else pltpu.roll(b, own * i % LANES, 1) for i, b in enumerate(blocks)]
    outs = []
    for q in range(own * len(blocks) // LANES):
        out = None
        for i, b in enumerate(rolled):
            at = own * i - LANES * q
            if at + own <= 0 or at >= LANES:
                continue
            out = b if out is None else jnp.where(k < at, out, b)
        outs.append(out)
    return jnp.concatenate(outs, axis=1)


def block_of(dense, i, own):
    q, s = divmod(own * i, LANES)
    out = dense[:, LANES * q : LANES * (q + 1)]
    if s == 0:
        return out
    out = pltpu.roll(out, LANES - s, 1)
    if s + own > LANES:
        after = pltpu.roll(dense[:, LANES * (q + 1) : LANES * (q + 2)], LANES - s, 1)
        out = jnp.where(iota(out.shape, 1) < LANES - s, out, after)
    return out


def step_of(own):
    return LANES // math.gcd(own, LANES)


def pack_kernel(x_hbm, b_hbm, cols_ref, rows_ref, b_out_ref, x_ref, b_ref, sems):
    copies = [pltpu.make_async_copy(x_hbm, x_ref, sems.at[0]), pltpu.make_async_copy(b_hbm, b_ref, sems.at[1])]
    for copy in copies:
        copy.start()
    for copy in copies:
        copy.wait()
    own = b_ref.shape[1]
    b = b_ref[...]
    features, hole = x_ref.shape[0], LANES - own
    b_out = jnp.concatenate([b, jnp.zeros((8, hole), F32)], axis=1)
    hi = rounded(b_out)
    pieces = [pltpu.roll(b_out - hi, own - hole * i, 1) for i in range(own // hole)]
    pieces += [jnp.zeros((8, LANES), F32)] * (features // 8 - len(pieces))
    x = jnp.concatenate([x_ref[...].astype(F32), jnp.zeros((features, hole), F32)], axis=1)
    x = jnp.where(iota(x.shape, 1) < own, x, jnp.concatenate(pieces, axis=0))
    block = jnp.concatenate([x, hi], axis=0).astype(BF16)
    for i in range(cols_ref.shape[0]):
        cols_ref[i] = block
    for i in range(rows_ref.shape[0]):
        rows_ref[i] = block
    b_out_ref[...] = b_out


def operand(block, features, own, is_row):
    x = block[:features]
    half = 0.5 * jnp.sum(x * x, axis=0, keepdims=True)
    h1 = rounded(half)
    h2 = rounded(half - h1)
    h3 = half - h1 - h2
    k = iota((16, LANES), 0)
    at = 0 if is_row else 3
    pieces = jnp.where(k == at, -h1, jnp.where(k == at + 1, -h2, jnp.where(k == at + 2, -h3, 0.0)))
    ones = jnp.where((k >= 3 - at) & (k < 6 - at), 1.0, 0.0)
    return jnp.concatenate([x, pieces + ones], axis=0).T[:own].astype(BF16)


def tile_product(rows_ref, cols_ref, vec_ref, scale, height, width):
    n_rows, n_cols = rows_ref.shape[0], cols_ref.shape[0]
    outs = []
    for at in range(0, n_rows, height):
        rows = rows_ref[at : at + height, :]
        acc = jnp.zeros((vec_ref.shape[0], height), F32)
        for c in range(0, n_cols, width):
            inner = lax.dot_general(
                cols_ref[c : c + width, :], rows, (((1,), (1,)), ((), ())), preferred_element_type=F32
            )
            e = jnp.exp2(inner * scale)
            hi = e.astype(BF16)
            lo = (e - hi.astype(F32)).astype(BF16)
            vec = vec_ref[:, c : c + width]
            acc += jnp.dot(vec, hi, preferred_element_type=F32)
            acc += jnp.dot(vec, lo, preferred_element_type=F32)
        outs.append(acc[:8] + acc[8:])
    return jnp.concatenate(outs, axis=1)


def targets_of(block, features, own):
    hole = LANES - own
    k = iota((8, LANES), 1)
    lo = None
    for i in reversed(range(own // hole)):
        piece = pltpu.roll(block[8 * i : 8 * (i + 1)], hole * (i + 1), 1)
        lo = piece if lo is None else jnp.where(k < hole * (i + 1), piece, lo)
    return block[features : features + 8], lo


def packed_all(blocks, own):
    step = step_of(own)
    return jnp.concatenate([packed(blocks[i : i + step], own) for i in range(0, len(blocks), step)], axis=1)


def columns_kernel(own, features, gcols_ref, amp_ref, noise_ref, cols_ref, vec_ref, consts_ref):
    diagonal = iota((8, 8), 0) == iota((8, 8), 1)
    amp = total(jnp.where(diagonal, jnp.broadcast_to(amp_ref[...], (8, 8)), 0.0))
    noise = total(jnp.where(diagonal, jnp.broadcast_to(noise_ref[...], (8, 8)), 0.0))
    consts_ref[...] = jnp.where(iota((8, LANES), 1) == 0, amp, noise)
    n_c = gcols_ref.shape[0]
    step = step_of(own)
    for i in range(0, n_c, step):
        pieces = []
        for j in range(i, i + step):
            block = gcols_ref[j].astype(F32)
            cols_ref[own * j : own * (j + 1), :] = operand(block, features, own, False)
            pieces.append(jnp.concatenate(targets_of(block, features, own), axis=0))
        vec_ref[:, own * i : own * (i + step)] = packed(pieces, own).astype(BF16)


def first_kernel(scale, own, features, height, width, grows_ref, cols_ref, vec_ref, rows_ref, out_ref, b_ref):
    n_r = grows_ref.shape[0]
    targets = []
    for i in range(n_r):
        block = grows_ref[i].astype(F32)
        rows_ref[own * i : own * (i + 1), :] = operand(block, features, own, True)
        hi, lo = targets_of(block, features, own)
        targets.append(hi + lo)
    b_ref[...] = packed_all(targets, own)
    out_ref[...] = tile_product(rows_ref, cols_ref, vec_ref, scale, height, width)


def chip_kernel(parts_ref, out_ref):
    e = parts_ref[0]
    for j in range(1, parts_ref.shape[0]):
        e = e + parts_ref[j]
    for i in range(out_ref.shape[0]):
        out_ref[i] = e


def image_kernel(own, parts_ref, b_ref, own_b_ref, consts_ref, vec_ref, own_w_ref, out_ref, blocks_ref):
    consts = consts_ref[...]
    amp, noise = consts[:, :1], consts[:, 1:2]
    e = parts_ref[0]
    for j in range(1, parts_ref.shape[0]):
        e = e + parts_ref[j]
    b = b_ref[...]
    w = amp * e + noise * b
    hi = rounded(w)
    vec_ref[...] = jnp.concatenate([hi, w - hi], axis=0).astype(BF16)
    curve, norm = total(b * w), total(b * b)
    for i in range(blocks_ref.shape[0]):
        blocks_ref[i] = block_of(e, i, own)
    me = 0
    for axis in ROWS:
        me = me * group((axis,)) + lax.axis_index(axis)
    own_w = amp * blocks_ref[me] + noise * own_b_ref[...]
    own_w_ref[...] = own_w
    k = iota((8, LANES), 1)
    message = jnp.where(k < own, own_w, jnp.where(k == own, curve, norm))
    for i in range(out_ref.shape[0]):
        out_ref[i] = message


def second_kernel(scale, height, width, rows_ref, cols_ref, vec_ref, out_ref):
    out_ref[...] = tile_product(cols_ref, rows_ref, vec_ref, scale, height, width)


def spread(values):
    sub, k = iota((8, LANES), 0), iota((8, LANES), 1)
    row = jnp.zeros((8, LANES), F32)
    for j, v in enumerate(values):
        row = jnp.where(k == 8 * j + sub, v, row)
    return jnp.sum(row, axis=0, keepdims=True)


def gathered(row, n):
    sub, k = iota((8, LANES), 0), iota((8, LANES), 1)
    rows = jnp.broadcast_to(row, (8, LANES))
    return [total(jnp.where(k == 8 * j + sub, rows, 0.0)) for j in range(n)]


def dots_kernel(own, u_ref, gw_ref, vec_ref, out_ref, stats_ref):
    n_c = gw_ref.shape[0]
    sums = gw_ref[0]
    for i in range(1, n_c):
        sums = sums + gw_ref[i]
    curve, norm = lane(sums, own), lane(sums, own + 1)
    alpha = norm / curve
    w = packed_all([gw_ref[i] for i in range(n_c)], own)
    b = vec_ref[...].astype(F32)
    r = b[:8] + b[8:] - alpha * w
    out_ref[...] = jnp.broadcast_to(spread((total(r * u_ref[...]), total(r * r), total(r * w))), out_ref.shape)
    k = iota((8, LANES), 1)
    stats_ref[...] = jnp.where(k == 0, alpha, jnp.where(k == 1, norm, curve))


def scatter_kernel(own, gs_ref, u_ref, out_ref, sums_ref):
    ru, rr, rw = gathered(jnp.sum(gs_ref[...], axis=0, keepdims=True), 3)
    u = u_ref[...]
    k = iota((8, LANES), 1)
    for i in range(out_ref.shape[0]):
        out_ref[i] = jnp.where(k < own, block_of(u, i, own), ru)
    sums_ref[...] = jnp.where(k == 0, rr, rw)


def last_kernel(own, parts_ref, stats_ref, sums_ref, w_ref, b_ref, consts_ref, x_ref, r_ref):
    u = parts_ref[0]
    for j in range(1, parts_ref.shape[0]):
        u = u + parts_ref[j]
    ru, rr, rw = lane(u, own), sums_ref[:, :1], sums_ref[:, 1:2]
    stats, consts = stats_ref[...], consts_ref[...]
    alpha, norm, curve = stats[:, :1], stats[:, 1:2], stats[:, 2:3]
    amp, noise = consts[:, :1], consts[:, 1:2]
    b, w = b_ref[...], w_ref[...]
    r = b - alpha * w
    beta = rr / norm
    direction = r + beta * b
    image = w - alpha * (amp * u + noise * w) + beta * w
    curve2 = rw - alpha * (amp * ru + noise * rw) + 2.0 * beta * rw + beta * beta * curve
    alpha2 = rr / curve2
    x_ref[...] = (alpha * b + alpha2 * direction)[:, :own]
    r_ref[...] = (r - alpha2 * image)[:, :own]


def shards(samples, targets, amplitude, noise):
    own, features = samples.shape
    n_c, n_r = group(COLS), group(ROWS)
    scale = 4.0 * 2.0 / features * LOG2E
    depth = features + 16
    height, width = HEIGHT, WIDTH

    def array(*shape, dtype=F32):
        return jax.ShapeDtypeStruct(shape, dtype)

    tile = array(8, LANES)
    given = [pltpu.with_memory_space_constraint(v, pltpu.HBM) for v in (samples.T, targets.T)]
    mcols, mrows, b = pl.pallas_call(
        pack_kernel,
        out_shape=(
            array(n_c, features + 8, LANES, dtype=BF16),
            pltpu.VMEM((n_r, features + 8, LANES), BF16),
            tile,
        ),
        in_specs=[pl.BlockSpec(memory_space=pltpu.HBM)] * 2,
        scratch_shapes=[pltpu.VMEM(v.shape, v.dtype) for v in given] + [pltpu.SemaphoreType.DMA((2,))],
        compiler_params=SMALL,
    )(*given)
    gcols = exchange(mcols, COLS)
    mrows, gcols = lax.optimization_barrier((mrows, gcols))
    grows = exchange(mrows, ROWS)
    cols, vec, consts = pl.pallas_call(
        functools.partial(columns_kernel, own, features),
        out_shape=(array(n_c * own, depth, dtype=BF16), array(16, n_c * own, dtype=BF16), tile),
        compiler_params=LARGE,
        cost_estimate=pl.CostEstimate(flops=10**9, bytes_accessed=10**6, transcendentals=0),
    )(gcols, amplitude.reshape(1, -1), noise.reshape(1, -1))
    rows, t, b_rows = pl.pallas_call(
        functools.partial(first_kernel, scale, own, features, height, width),
        out_shape=(array(n_r * own, depth, dtype=BF16), array(8, n_r * own), array(8, n_r * own)),
        compiler_params=LARGE,
    )(grows, cols, vec)
    parts = pl.pallas_call(
        chip_kernel, out_shape=array(group(CHIPS), 8, n_r * own), compiler_params=SMALL
    )(lax.all_gather(t, CHIP))
    parts = exchange(parts, CHIPS)
    w_vec, w, message = pl.pallas_call(
        functools.partial(image_kernel, own),
        out_shape=(array(16, n_r * own, dtype=BF16), tile, array(n_c, 8, LANES)),
        scratch_shapes=[pltpu.VMEM((n_r, 8, LANES), F32)],
        compiler_params=SMALL,
    )(parts, b_rows, b, consts)
    gw = exchange(message, COLS)
    u = pl.pallas_call(
        functools.partial(second_kernel, scale, height, width),
        out_shape=array(8, n_c * own),
        compiler_params=LARGE,
        cost_estimate=pl.CostEstimate(
            flops=2 * 2 * 256 * n_r * n_c * own * own,
            bytes_accessed=n_r * n_c * own * own,
            transcendentals=n_r * n_c * own * own,
        ),
    )(rows, cols, w_vec)
    message, stats = pl.pallas_call(
        functools.partial(dots_kernel, own),
        out_shape=(array(n_r, LANES), tile),
        compiler_params=SMALL,
    )(u, gw, vec)
    gs = exchange(message, ROWS)
    parts, sums = pl.pallas_call(
        functools.partial(scatter_kernel, own),
        out_shape=(array(n_c, 8, LANES), tile),
        compiler_params=SMALL,
    )(gs, u)
    parts = exchange(parts, COLS)
    x, r = pl.pallas_call(
        functools.partial(last_kernel, own),
        out_shape=(array(8, own), array(8, own)),
        compiler_params=SMALL,
    )(parts, stats, sums, w, b, consts)
    return x.T, r.T


HEIGHT, WIDTH = 256, 512


def solution(mesh):
    fine = Mesh(mesh.devices.reshape(SIZES), AXES)
    split = P(AXES, None)
    return jax.shard_map(
        shards,
        mesh=fine,
        in_specs=(split, split, P(), P()),
        out_specs=(split, split),
        check_vma=False,
    )
```

```python
import functools
import math

import jax
import jax.numpy as jnp
import numpy as np
from jax import lax
from jax.experimental import pallas as pl
from jax.experimental.pallas import tpu as pltpu
from jax.sharding import Mesh
from jax.sharding import PartitionSpec as P

AXES = ("yh", "z", "core", "x", "yl")
SIZES = (4, 8, 2, 4, 2)
COLS = ("z", "yh")
ROWS = ("core", "x", "yl")
CHIP = "core"
CHIPS = ("x", "yl")
LANES = 128
LOG2E = 1.4426950408889634
F32 = jnp.float32
BF16 = jnp.bfloat16
SMALL = pltpu.CompilerParams(vmem_limit_bytes=4 * 1024 * 1024)
LARGE = pltpu.CompilerParams(vmem_limit_bytes=24 * 1024 * 1024)


def group(axes):
    return int(np.prod([SIZES[AXES.index(a)] for a in axes]))


def iota(shape, dim):
    return lax.broadcasted_iota(jnp.int32, shape, dim)


def rounded(v):
    return v.astype(BF16).astype(F32)


def lane(block, k):
    return total(jnp.where(iota(block.shape, 1) == k, block, 0.0))


def total(v):
    return jnp.sum(v, axis=1, keepdims=True)


def exchange(blocks, axes):
    return lax.all_to_all(blocks, axes, 0, 0)


def packed(blocks, own):
    k = iota(blocks[0].shape, 1)
    rolled = [b if own * i % LANES == 0 else pltpu.roll(b, own * i % LANES, 1) for i, b in enumerate(blocks)]
    outs = []
    for q in range(own * len(blocks) // LANES):
        out = None
        for i, b in enumerate(rolled):
            at = own * i - LANES * q
            if at + own <= 0 or at >= LANES:
                continue
            out = b if out is None else jnp.where(k < at, out, b)
        outs.append(out)
    return jnp.concatenate(outs, axis=1)


def block_of(dense, i, own):
    q, s = divmod(own * i, LANES)
    out = dense[:, LANES * q : LANES * (q + 1)]
    if s == 0:
        return out
    out = pltpu.roll(out, LANES - s, 1)
    if s + own > LANES:
        after = pltpu.roll(dense[:, LANES * (q + 1) : LANES * (q + 2)], LANES - s, 1)
        out = jnp.where(iota(out.shape, 1) < LANES - s, out, after)
    return out


def step_of(own):
    return LANES // math.gcd(own, LANES)


def pack_kernel(x_hbm, b_hbm, amp_hbm, noise_hbm, cols_ref, rows_ref, b_out_ref, consts_ref, x_ref, b_ref, amp_ref, noise_ref, sems):
    pairs = ((x_hbm, x_ref), (b_hbm, b_ref), (amp_hbm, amp_ref), (noise_hbm, noise_ref))
    copies = [pltpu.make_async_copy(src, dst, sems.at[i]) for i, (src, dst) in enumerate(pairs)]
    for copy in copies:
        copy.start()
    for copy in copies:
        copy.wait()
    own = b_ref.shape[1]
    b = b_ref[...]
    features, hole = x_ref.shape[0], LANES - own
    b_out = jnp.concatenate([b, jnp.zeros((8, hole), F32)], axis=1)
    hi = rounded(b_out)
    pieces = [pltpu.roll(b_out - hi, own - hole * i, 1) for i in range(own // hole)]
    pieces += [jnp.zeros((8, LANES), F32)] * (features // 8 - len(pieces))
    x = jnp.concatenate([x_ref[...].astype(F32), jnp.zeros((features, hole), F32)], axis=1)
    x = jnp.where(iota(x.shape, 1) < own, x, jnp.concatenate(pieces, axis=0))
    block = jnp.concatenate([x, hi], axis=0).astype(BF16)
    for i in range(cols_ref.shape[0]):
        cols_ref[i] = block
    for i in range(rows_ref.shape[0]):
        rows_ref[i] = block
    b_out_ref[...] = b_out
    diagonal = iota((8, 8), 0) == iota((8, 8), 1)
    amp = total(jnp.where(diagonal, jnp.broadcast_to(amp_ref[...], (8, 8)), 0.0))
    noise = total(jnp.where(diagonal, jnp.broadcast_to(noise_ref[...], (8, 8)), 0.0))
    consts_ref[...] = jnp.where(iota((8, LANES), 1) == 0, amp, noise)


def operand(block, features, own, is_row):
    x = block[:features]
    half = 0.5 * jnp.sum(x * x, axis=0, keepdims=True)
    h1 = rounded(half)
    h2 = rounded(half - h1)
    h3 = half - h1 - h2
    k = iota((16, LANES), 0)
    at = 0 if is_row else 3
    pieces = jnp.where(k == at, -h1, jnp.where(k == at + 1, -h2, jnp.where(k == at + 2, -h3, 0.0)))
    ones = jnp.where((k >= 3 - at) & (k < 6 - at), 1.0, 0.0)
    return jnp.concatenate([x, pieces + ones], axis=0).T[:own].astype(BF16)


def tile_product(rows_ref, cols_ref, vec_ref, scale, height, width):
    n_rows, n_cols = rows_ref.shape[0], cols_ref.shape[0]
    outs = []
    for at in range(0, n_rows, height):
        rows = rows_ref[at : at + height, :]
        acc = jnp.zeros((vec_ref.shape[0], height), F32)
        for c in range(0, n_cols, width):
            inner = lax.dot_general(
                cols_ref[c : c + width, :], rows, (((1,), (1,)), ((), ())), preferred_element_type=F32
            )
            e = jnp.exp2(inner * scale)
            hi = e.astype(BF16)
            lo = (e - hi.astype(F32)).astype(BF16)
            vec = vec_ref[:, c : c + width]
            acc += jnp.dot(vec, hi, preferred_element_type=F32)
            acc += jnp.dot(vec, lo, preferred_element_type=F32)
        outs.append(acc[:8] + acc[8:])
    return jnp.concatenate(outs, axis=1)


def targets_of(block, features, own):
    hole = LANES - own
    k = iota((8, LANES), 1)
    lo = None
    for i in reversed(range(own // hole)):
        piece = pltpu.roll(block[8 * i : 8 * (i + 1)], hole * (i + 1), 1)
        lo = piece if lo is None else jnp.where(k < hole * (i + 1), piece, lo)
    return block[features : features + 8], lo


def packed_all(blocks, own):
    step = step_of(own)
    return jnp.concatenate([packed(blocks[i : i + step], own) for i in range(0, len(blocks), step)], axis=1)


def columns_kernel(own, features, gcols_ref, cols_ref, vec_ref):
    n_c = gcols_ref.shape[0]
    step = step_of(own)
    for i in range(0, n_c, step):
        pieces = []
        for j in range(i, i + step):
            block = gcols_ref[j].astype(F32)
            cols_ref[own * j : own * (j + 1), :] = operand(block, features, own, False)
            pieces.append(jnp.concatenate(targets_of(block, features, own), axis=0))
        vec_ref[:, own * i : own * (i + step)] = packed(pieces, own).astype(BF16)


def first_kernel(scale, own, features, height, width, grows_ref, cols_ref, vec_ref, rows_ref, out_ref, b_ref):
    n_r = grows_ref.shape[0]
    targets = []
    for i in range(n_r):
        block = grows_ref[i].astype(F32)
        rows_ref[own * i : own * (i + 1), :] = operand(block, features, own, True)
        hi, lo = targets_of(block, features, own)
        targets.append(hi + lo)
    b_ref[...] = packed_all(targets, own)
    out_ref[...] = tile_product(rows_ref, cols_ref, vec_ref, scale, height, width)


def chip_kernel(parts_ref, out_ref):
    e = parts_ref[0]
    for j in range(1, parts_ref.shape[0]):
        e = e + parts_ref[j]
    for i in range(out_ref.shape[0]):
        out_ref[i] = e


def image_kernel(own, parts_ref, b_ref, own_b_ref, consts_ref, vec_ref, own_w_ref, out_ref, blocks_ref):
    consts = consts_ref[...]
    amp, noise = consts[:, :1], consts[:, 1:2]
    e = parts_ref[0]
    for j in range(1, parts_ref.shape[0]):
        e = e + parts_ref[j]
    b = b_ref[...]
    w = amp * e + noise * b
    hi = rounded(w)
    vec_ref[...] = jnp.concatenate([hi, w - hi], axis=0).astype(BF16)
    curve, norm = total(b * w), total(b * b)
    for i in range(blocks_ref.shape[0]):
        blocks_ref[i] = block_of(e, i, own)
    me = 0
    for axis in ROWS:
        me = me * group((axis,)) + lax.axis_index(axis)
    own_w = amp * blocks_ref[me] + noise * own_b_ref[...]
    own_w_ref[...] = own_w
    k = iota((8, LANES), 1)
    message = jnp.where(k < own, own_w, jnp.where(k == own, curve, norm))
    for i in range(out_ref.shape[0]):
        out_ref[i] = message


def second_kernel(scale, height, width, rows_ref, cols_ref, vec_ref, out_ref):
    out_ref[...] = tile_product(cols_ref, rows_ref, vec_ref, scale, height, width)


def spread(values):
    sub, k = iota((8, LANES), 0), iota((8, LANES), 1)
    row = jnp.zeros((8, LANES), F32)
    for j, v in enumerate(values):
        row = jnp.where(k == 8 * j + sub, v, row)
    return jnp.sum(row, axis=0, keepdims=True)


def gathered(row, n):
    sub, k = iota((8, LANES), 0), iota((8, LANES), 1)
    rows = jnp.broadcast_to(row, (8, LANES))
    return [total(jnp.where(k == 8 * j + sub, rows, 0.0)) for j in range(n)]


def dots_kernel(own, u_ref, gw_ref, vec_ref, out_ref, stats_ref):
    n_c = gw_ref.shape[0]
    sums = gw_ref[0]
    for i in range(1, n_c):
        sums = sums + gw_ref[i]
    curve, norm = lane(sums, own), lane(sums, own + 1)
    alpha = norm / curve
    w = packed_all([gw_ref[i] for i in range(n_c)], own)
    b = vec_ref[...].astype(F32)
    r = b[:8] + b[8:] - alpha * w
    out_ref[...] = jnp.broadcast_to(spread((total(r * u_ref[...]), total(r * r), total(r * w))), out_ref.shape)
    k = iota((8, LANES), 1)
    stats_ref[...] = jnp.where(k == 0, alpha, jnp.where(k == 1, norm, curve))


def scatter_kernel(own, gs_ref, u_ref, out_ref, sums_ref):
    ru, rr, rw = gathered(jnp.sum(gs_ref[...], axis=0, keepdims=True), 3)
    u = u_ref[...]
    k = iota((8, LANES), 1)
    for i in range(out_ref.shape[0]):
        out_ref[i] = jnp.where(k < own, block_of(u, i, own), ru)
    sums_ref[...] = jnp.where(k == 0, rr, rw)


def last_kernel(own, parts_ref, stats_ref, sums_ref, w_ref, b_ref, consts_ref, x_ref, r_ref):
    u = parts_ref[0]
    for j in range(1, parts_ref.shape[0]):
        u = u + parts_ref[j]
    ru, rr, rw = lane(u, own), sums_ref[:, :1], sums_ref[:, 1:2]
    stats, consts = stats_ref[...], consts_ref[...]
    alpha, norm, curve = stats[:, :1], stats[:, 1:2], stats[:, 2:3]
    amp, noise = consts[:, :1], consts[:, 1:2]
    b, w = b_ref[...], w_ref[...]
    r = b - alpha * w
    beta = rr / norm
    direction = r + beta * b
    image = w - alpha * (amp * u + noise * w) + beta * w
    curve2 = rw - alpha * (amp * ru + noise * rw) + 2.0 * beta * rw + beta * beta * curve
    alpha2 = rr / curve2
    x_ref[...] = (alpha * b + alpha2 * direction)[:, :own]
    r_ref[...] = (r - alpha2 * image)[:, :own]


def shards(samples, targets, amplitude, noise):
    own, features = samples.shape
    n_c, n_r = group(COLS), group(ROWS)
    scale = 4.0 * 2.0 / features * LOG2E
    depth = features + 16
    height, width = HEIGHT, WIDTH

    def array(*shape, dtype=F32):
        return jax.ShapeDtypeStruct(shape, dtype)

    tile = array(8, LANES)
    given = [pltpu.with_memory_space_constraint(v, pltpu.HBM) for v in (samples.T, targets.T, amplitude.reshape(1, -1), noise.reshape(1, -1))]
    mcols, mrows, b, consts = pl.pallas_call(
        pack_kernel,
        out_shape=(
            array(n_c, features + 8, LANES, dtype=BF16),
            array(n_r, features + 8, LANES, dtype=BF16),
            tile,
            tile,
        ),
        in_specs=[pl.BlockSpec(memory_space=pltpu.HBM)] * 4,
        scratch_shapes=[pltpu.VMEM(v.shape, v.dtype) for v in given] + [pltpu.SemaphoreType.DMA((4,))],
        compiler_params=SMALL,
    )(*given)
    grows = exchange(mrows, ROWS)
    mcols, grows = lax.optimization_barrier((mcols, grows))
    gcols = exchange(mcols, COLS)
    cols, vec = pl.pallas_call(
        functools.partial(columns_kernel, own, features),
        out_shape=(array(n_c * own, depth, dtype=BF16), array(16, n_c * own, dtype=BF16)),
        compiler_params=LARGE,
        cost_estimate=pl.CostEstimate(flops=10**9, bytes_accessed=10**6, transcendentals=0),
    )(gcols)
    rows, t, b_rows = pl.pallas_call(
        functools.partial(first_kernel, scale, own, features, height, width),
        out_shape=(array(n_r * own, depth, dtype=BF16), array(8, n_r * own), array(8, n_r * own)),
        compiler_params=LARGE,
    )(grows, cols, vec)
    parts = pl.pallas_call(
        chip_kernel, out_shape=array(group(CHIPS), 8, n_r * own), compiler_params=SMALL
    )(lax.all_gather(t, CHIP))
    parts = exchange(parts, CHIPS)
    w_vec, w, message = pl.pallas_call(
        functools.partial(image_kernel, own),
        out_shape=(array(16, n_r * own, dtype=BF16), tile, array(n_c, 8, LANES)),
        scratch_shapes=[pltpu.VMEM((n_r, 8, LANES), F32)],
        compiler_params=SMALL,
    )(parts, b_rows, b, consts)
    gw = exchange(message, COLS)
    u = pl.pallas_call(
        functools.partial(second_kernel, scale, height, width),
        out_shape=array(8, n_c * own),
        compiler_params=LARGE,
        cost_estimate=pl.CostEstimate(
            flops=2 * 2 * 256 * n_r * n_c * own * own,
            bytes_accessed=n_r * n_c * own * own,
            transcendentals=n_r * n_c * own * own,
        ),
    )(rows, cols, w_vec)
    message, stats = pl.pallas_call(
        functools.partial(dots_kernel, own),
        out_shape=(array(n_r, LANES), tile),
        compiler_params=SMALL,
    )(u, gw, vec)
    gs = exchange(message, ROWS)
    parts, sums = pl.pallas_call(
        functools.partial(scatter_kernel, own),
        out_shape=(array(n_c, 8, LANES), tile),
        compiler_params=SMALL,
    )(gs, u)
    parts = exchange(parts, COLS)
    x, r = pl.pallas_call(
        functools.partial(last_kernel, own),
        out_shape=(array(8, own), array(8, own)),
        compiler_params=SMALL,
    )(parts, stats, sums, w, b, consts)
    return x.T, r.T


HEIGHT, WIDTH = 256, 512


def solution(mesh):
    fine = Mesh(mesh.devices.reshape(SIZES), AXES)
    split = P(AXES, None)
    return jax.shard_map(
        shards,
        mesh=fine,
        in_specs=(split, split, P(), P()),
        out_specs=(split, split),
        check_vma=False,
    )
```

```python
import functools
import math

import jax
import jax.numpy as jnp
import numpy as np
from jax import lax
from jax.experimental import pallas as pl
from jax.experimental.pallas import tpu as pltpu
from jax.sharding import Mesh
from jax.sharding import PartitionSpec as P

AXES = ("yh", "z", "core", "x", "yl")
SIZES = (4, 8, 2, 4, 2)
COLS = ("z", "yh")
ROWS = ("core", "x", "yl")
CHIP = "core"
CHIPS = ("x", "yl")
LANES = 128
LOG2E = 1.4426950408889634
F32 = jnp.float32
BF16 = jnp.bfloat16
SMALL = pltpu.CompilerParams(vmem_limit_bytes=4 * 1024 * 1024)
LARGE = pltpu.CompilerParams(vmem_limit_bytes=24 * 1024 * 1024)


def group(axes):
    return int(np.prod([SIZES[AXES.index(a)] for a in axes]))


def iota(shape, dim):
    return lax.broadcasted_iota(jnp.int32, shape, dim)


def rounded(v):
    return v.astype(BF16).astype(F32)


def lane(block, k):
    return total(jnp.where(iota(block.shape, 1) == k, block, 0.0))


def total(v):
    return jnp.sum(v, axis=1, keepdims=True)


def exchange(blocks, axes):
    return lax.all_to_all(blocks, axes, 0, 0)


def packed(blocks, own):
    k = iota(blocks[0].shape, 1)
    rolled = [b if own * i % LANES == 0 else pltpu.roll(b, own * i % LANES, 1) for i, b in enumerate(blocks)]
    outs = []
    for q in range(own * len(blocks) // LANES):
        out = None
        for i, b in enumerate(rolled):
            at = own * i - LANES * q
            if at + own <= 0 or at >= LANES:
                continue
            out = b if out is None else jnp.where(k < at, out, b)
        outs.append(out)
    return jnp.concatenate(outs, axis=1)


def block_of(dense, i, own):
    q, s = divmod(own * i, LANES)
    out = dense[:, LANES * q : LANES * (q + 1)]
    if s == 0:
        return out
    out = pltpu.roll(out, LANES - s, 1)
    if s + own > LANES:
        after = pltpu.roll(dense[:, LANES * (q + 1) : LANES * (q + 2)], LANES - s, 1)
        out = jnp.where(iota(out.shape, 1) < LANES - s, out, after)
    return out


def step_of(own):
    return LANES // math.gcd(own, LANES)


def pack_kernel(x_hbm, b_hbm, amp_hbm, noise_hbm, cols_ref, rows_ref, b_out_ref, consts_ref, x_ref, b_ref, amp_ref, noise_ref, sems):
    pairs = ((x_hbm, x_ref), (b_hbm, b_ref), (amp_hbm, amp_ref), (noise_hbm, noise_ref))
    copies = [pltpu.make_async_copy(src, dst, sems.at[i]) for i, (src, dst) in enumerate(pairs)]
    for copy in copies:
        copy.start()
    for copy in copies:
        copy.wait()
    own = b_ref.shape[1]
    b = b_ref[...]
    features, hole = x_ref.shape[0], LANES - own
    b_out = jnp.concatenate([b, jnp.zeros((8, hole), F32)], axis=1)
    hi = rounded(b_out)
    pieces = [pltpu.roll(b_out - hi, own - hole * i, 1) for i in range(own // hole)]
    pieces += [jnp.zeros((8, LANES), F32)] * (features // 8 - len(pieces))
    x = jnp.concatenate([x_ref[...].astype(F32), jnp.zeros((features, hole), F32)], axis=1)
    x = jnp.where(iota(x.shape, 1) < own, x, jnp.concatenate(pieces, axis=0))
    block = jnp.concatenate([x, hi], axis=0).astype(BF16)
    for i in range(cols_ref.shape[0]):
        cols_ref[i] = block
    for i in range(rows_ref.shape[0]):
        rows_ref[i] = block
    b_out_ref[...] = b_out
    diagonal = iota((8, 8), 0) == iota((8, 8), 1)
    amp = total(jnp.where(diagonal, jnp.broadcast_to(amp_ref[...], (8, 8)), 0.0))
    noise = total(jnp.where(diagonal, jnp.broadcast_to(noise_ref[...], (8, 8)), 0.0))
    consts_ref[...] = jnp.where(iota((8, LANES), 1) == 0, amp, noise)


def operand(block, features, own, is_row):
    x = block[:features]
    half = 0.5 * jnp.sum(x * x, axis=0, keepdims=True)
    h1 = rounded(half)
    h2 = rounded(half - h1)
    h3 = half - h1 - h2
    k = iota((16, LANES), 0)
    at = 0 if is_row else 3
    pieces = jnp.where(k == at, -h1, jnp.where(k == at + 1, -h2, jnp.where(k == at + 2, -h3, 0.0)))
    ones = jnp.where((k >= 3 - at) & (k < 6 - at), 1.0, 0.0)
    return jnp.concatenate([x, pieces + ones], axis=0).T[:own].astype(BF16)


def tile_product(rows_ref, cols_ref, vec_ref, scale, height, width, ready=None):
    n_rows, n_cols = rows_ref.shape[0], cols_ref.shape[0]
    outs = []
    for at in range(0, n_rows, height):
        if ready:
            ready(at + height, 0)
        rows = rows_ref[at : at + height, :]
        acc = jnp.zeros((vec_ref.shape[0], height), F32)
        for c in range(0, n_cols, width):
            if ready:
                ready(at + 2 * height, c + 2 * width)
            inner = lax.dot_general(
                cols_ref[c : c + width, :], rows, (((1,), (1,)), ((), ())), preferred_element_type=F32
            )
            e = jnp.exp2(inner * scale)
            hi = e.astype(BF16)
            lo = (e - hi.astype(F32)).astype(BF16)
            vec = vec_ref[:, c : c + width]
            acc += jnp.dot(vec, hi, preferred_element_type=F32)
            acc += jnp.dot(vec, lo, preferred_element_type=F32)
        outs.append(acc[:8] + acc[8:])
    return jnp.concatenate(outs, axis=1)


def targets_of(block, features, own):
    hole = LANES - own
    k = iota((8, LANES), 1)
    lo = None
    for i in reversed(range(own // hole)):
        piece = pltpu.roll(block[8 * i : 8 * (i + 1)], hole * (i + 1), 1)
        lo = piece if lo is None else jnp.where(k < hole * (i + 1), piece, lo)
    return block[features : features + 8], lo


def packed_all(blocks, own):
    step = step_of(own)
    return jnp.concatenate([packed(blocks[i : i + step], own) for i in range(0, len(blocks), step)], axis=1)


def first_kernel(scale, own, features, height, width, gcols_ref, grows_ref, rows_ref, cols_ref, vec_ref, out_ref, b_ref):
    n_c, n_r = gcols_ref.shape[0], grows_ref.shape[0]
    step = step_of(own)
    done = {"rows": 0, "cols": 0}

    def ready(n_rows, n_cols):
        while done["cols"] < n_c and own * done["cols"] < n_cols:
            i = done["cols"]
            pieces = []
            for j in range(i, i + step):
                block = gcols_ref[j].astype(F32)
                cols_ref[own * j : own * (j + 1), :] = operand(block, features, own, False)
                pieces.append(jnp.concatenate(targets_of(block, features, own), axis=0))
            vec_ref[:, own * i : own * (i + step)] = packed(pieces, own).astype(BF16)
            done["cols"] = i + step
        while done["rows"] < n_r and own * done["rows"] < n_rows:
            i = done["rows"]
            targets = []
            for j in range(i, i + step):
                block = grows_ref[j].astype(F32)
                rows_ref[own * j : own * (j + 1), :] = operand(block, features, own, True)
                hi, lo = targets_of(block, features, own)
                targets.append(hi + lo)
            b_ref[:, own * i : own * (i + step)] = packed(targets, own)
            done["rows"] = i + step

    out_ref[...] = tile_product(rows_ref, cols_ref, vec_ref, scale, height, width, ready)


def chip_kernel(parts_ref, out_ref):
    e = parts_ref[0]
    for j in range(1, parts_ref.shape[0]):
        e = e + parts_ref[j]
    for i in range(out_ref.shape[0]):
        out_ref[i] = e


def image_kernel(own, parts_ref, b_ref, own_b_ref, consts_ref, vec_ref, own_w_ref, out_ref, blocks_ref):
    consts = consts_ref[...]
    amp, noise = consts[:, :1], consts[:, 1:2]
    e = parts_ref[0]
    for j in range(1, parts_ref.shape[0]):
        e = e + parts_ref[j]
    b = b_ref[...]
    w = amp * e + noise * b
    hi = rounded(w)
    vec_ref[...] = jnp.concatenate([hi, w - hi], axis=0).astype(BF16)
    curve, norm = total(b * w), total(b * b)
    for i in range(blocks_ref.shape[0]):
        blocks_ref[i] = block_of(e, i, own)
    me = 0
    for axis in ROWS:
        me = me * group((axis,)) + lax.axis_index(axis)
    own_w = amp * blocks_ref[me] + noise * own_b_ref[...]
    own_w_ref[...] = own_w
    k = iota((8, LANES), 1)
    message = jnp.where(k < own, own_w, jnp.where(k == own, curve, norm))
    for i in range(out_ref.shape[0]):
        out_ref[i] = message


def second_kernel(scale, height, width, rows_ref, cols_ref, vec_ref, out_ref):
    out_ref[...] = tile_product(cols_ref, rows_ref, vec_ref, scale, height, width)


def spread(values):
    sub, k = iota((8, LANES), 0), iota((8, LANES), 1)
    row = jnp.zeros((8, LANES), F32)
    for j, v in enumerate(values):
        row = jnp.where(k == 8 * j + sub, v, row)
    return jnp.sum(row, axis=0, keepdims=True)


def gathered(row, n):
    sub, k = iota((8, LANES), 0), iota((8, LANES), 1)
    rows = jnp.broadcast_to(row, (8, LANES))
    return [total(jnp.where(k == 8 * j + sub, rows, 0.0)) for j in range(n)]


def dots_kernel(own, u_ref, gw_ref, vec_ref, out_ref, stats_ref):
    n_c = gw_ref.shape[0]
    sums = gw_ref[0]
    for i in range(1, n_c):
        sums = sums + gw_ref[i]
    curve, norm = lane(sums, own), lane(sums, own + 1)
    alpha = norm / curve
    w = packed_all([gw_ref[i] for i in range(n_c)], own)
    b = vec_ref[...].astype(F32)
    r = b[:8] + b[8:] - alpha * w
    out_ref[...] = jnp.broadcast_to(spread((total(r * u_ref[...]), total(r * r), total(r * w))), out_ref.shape)
    k = iota((8, LANES), 1)
    stats_ref[...] = jnp.where(k == 0, alpha, jnp.where(k == 1, norm, curve))


def scatter_kernel(own, gs_ref, u_ref, out_ref, sums_ref):
    ru, rr, rw = gathered(jnp.sum(gs_ref[...], axis=0, keepdims=True), 3)
    u = u_ref[...]
    k = iota((8, LANES), 1)
    for i in range(out_ref.shape[0]):
        out_ref[i] = jnp.where(k < own, block_of(u, i, own), ru)
    sums_ref[...] = jnp.where(k == 0, rr, rw)


def last_kernel(own, parts_ref, stats_ref, sums_ref, w_ref, b_ref, consts_ref, x_ref, r_ref):
    u = parts_ref[0]
    for j in range(1, parts_ref.shape[0]):
        u = u + parts_ref[j]
    ru, rr, rw = lane(u, own), sums_ref[:, :1], sums_ref[:, 1:2]
    stats, consts = stats_ref[...], consts_ref[...]
    alpha, norm, curve = stats[:, :1], stats[:, 1:2], stats[:, 2:3]
    amp, noise = consts[:, :1], consts[:, 1:2]
    b, w = b_ref[...], w_ref[...]
    r = b - alpha * w
    beta = rr / norm
    direction = r + beta * b
    image = w - alpha * (amp * u + noise * w) + beta * w
    curve2 = rw - alpha * (amp * ru + noise * rw) + 2.0 * beta * rw + beta * beta * curve
    alpha2 = rr / curve2
    x_ref[...] = (alpha * b + alpha2 * direction)[:, :own]
    r_ref[...] = (r - alpha2 * image)[:, :own]


def shards(samples, targets, amplitude, noise):
    own, features = samples.shape
    n_c, n_r = group(COLS), group(ROWS)
    scale = 4.0 * 2.0 / features * LOG2E
    depth = features + 16
    height, width = HEIGHT, WIDTH

    def array(*shape, dtype=F32):
        return jax.ShapeDtypeStruct(shape, dtype)

    tile = array(8, LANES)
    given = [pltpu.with_memory_space_constraint(v, pltpu.HBM) for v in (samples.T, targets.T, amplitude.reshape(1, -1), noise.reshape(1, -1))]
    mcols, mrows, b, consts = pl.pallas_call(
        pack_kernel,
        out_shape=(
            array(n_c, features + 8, LANES, dtype=BF16),
            array(n_r, features + 8, LANES, dtype=BF16),
            tile,
            tile,
        ),
        in_specs=[pl.BlockSpec(memory_space=pltpu.HBM)] * 4,
        scratch_shapes=[pltpu.VMEM(v.shape, v.dtype) for v in given] + [pltpu.SemaphoreType.DMA((4,))],
        compiler_params=SMALL,
    )(*given)
    grows = exchange(mrows, ROWS)
    mcols, grows = lax.optimization_barrier((mcols, grows))
    gcols = exchange(mcols, COLS)
    rows, cols, vec, t, b_rows = pl.pallas_call(
        functools.partial(first_kernel, scale, own, features, height, width),
        out_shape=(
            array(n_r * own, depth, dtype=BF16),
            array(n_c * own, depth, dtype=BF16),
            array(16, n_c * own, dtype=BF16),
            array(8, n_r * own),
            array(8, n_r * own),
        ),
        compiler_params=LARGE,
    )(gcols, grows)
    parts = pl.pallas_call(
        chip_kernel, out_shape=array(group(CHIPS), 8, n_r * own), compiler_params=SMALL
    )(lax.all_gather(t, CHIP))
    parts = exchange(parts, CHIPS)
    w_vec, w, message = pl.pallas_call(
        functools.partial(image_kernel, own),
        out_shape=(array(16, n_r * own, dtype=BF16), tile, array(n_c, 8, LANES)),
        scratch_shapes=[pltpu.VMEM((n_r, 8, LANES), F32)],
        compiler_params=SMALL,
    )(parts, b_rows, b, consts)
    gw = exchange(message, COLS)
    u = pl.pallas_call(
        functools.partial(second_kernel, scale, height, width),
        out_shape=array(8, n_c * own),
        compiler_params=LARGE,
        cost_estimate=pl.CostEstimate(
            flops=2 * 2 * 256 * n_r * n_c * own * own,
            bytes_accessed=n_r * n_c * own * own,
            transcendentals=n_r * n_c * own * own,
        ),
    )(rows, cols, w_vec)
    message, stats = pl.pallas_call(
        functools.partial(dots_kernel, own),
        out_shape=(array(n_r, LANES), tile),
        compiler_params=SMALL,
    )(u, gw, vec)
    gs = exchange(message, ROWS)
    parts, sums = pl.pallas_call(
        functools.partial(scatter_kernel, own),
        out_shape=(array(n_c, 8, LANES), tile),
        compiler_params=SMALL,
    )(gs, u)
    parts = exchange(parts, COLS)
    x, r = pl.pallas_call(
        functools.partial(last_kernel, own),
        out_shape=(array(8, own), array(8, own)),
        compiler_params=SMALL,
    )(parts, stats, sums, w, b, consts)
    return x.T, r.T


HEIGHT, WIDTH = 256, 512


def solution(mesh):
    fine = Mesh(mesh.devices.reshape(SIZES), AXES)
    split = P(AXES, None)
    return jax.shard_map(
        shards,
        mesh=fine,
        in_specs=(split, split, P(), P()),
        out_specs=(split, split),
        check_vma=False,
    )
```

```python
import functools
import math

import jax
import jax.numpy as jnp
import numpy as np
from jax import lax
from jax.experimental import pallas as pl
from jax.experimental.pallas import tpu as pltpu
from jax.sharding import Mesh
from jax.sharding import PartitionSpec as P

AXES = ("yh", "z", "core", "x", "yl")
SIZES = (4, 8, 2, 4, 2)
COLS = ("z", "yh")
ROWS = ("core", "x", "yl")
CHIP = "core"
CHIPS = ("x", "yl")
LANES = 128
LOG2E = 1.4426950408889634
F32 = jnp.float32
BF16 = jnp.bfloat16
SMALL = pltpu.CompilerParams(vmem_limit_bytes=4 * 1024 * 1024)
LARGE = pltpu.CompilerParams(vmem_limit_bytes=24 * 1024 * 1024)


def group(axes):
    return int(np.prod([SIZES[AXES.index(a)] for a in axes]))


def iota(shape, dim):
    return lax.broadcasted_iota(jnp.int32, shape, dim)


def rounded(v):
    return v.astype(BF16).astype(F32)


def lane(block, k):
    return total(jnp.where(iota(block.shape, 1) == k, block, 0.0))


def total(v):
    return jnp.sum(v, axis=1, keepdims=True)


def exchange(blocks, axes):
    return lax.all_to_all(blocks, axes, 0, 0)


def packed(blocks, own):
    k = iota(blocks[0].shape, 1)
    rolled = [b if own * i % LANES == 0 else pltpu.roll(b, own * i % LANES, 1) for i, b in enumerate(blocks)]
    outs = []
    for q in range(own * len(blocks) // LANES):
        out = None
        for i, b in enumerate(rolled):
            at = own * i - LANES * q
            if at + own <= 0 or at >= LANES:
                continue
            out = b if out is None else jnp.where(k < at, out, b)
        outs.append(out)
    return jnp.concatenate(outs, axis=1)


def block_of(dense, i, own):
    q, s = divmod(own * i, LANES)
    out = dense[:, LANES * q : LANES * (q + 1)]
    if s == 0:
        return out
    out = pltpu.roll(out, LANES - s, 1)
    if s + own > LANES:
        after = pltpu.roll(dense[:, LANES * (q + 1) : LANES * (q + 2)], LANES - s, 1)
        out = jnp.where(iota(out.shape, 1) < LANES - s, out, after)
    return out


def step_of(own):
    return LANES // math.gcd(own, LANES)


def pack_kernel(x_hbm, b_hbm, amp_hbm, noise_hbm, cols_ref, rows_ref, b_out_ref, consts_ref, x_ref, b_ref, amp_ref, noise_ref, sems):
    pairs = ((x_hbm, x_ref), (b_hbm, b_ref), (amp_hbm, amp_ref), (noise_hbm, noise_ref))
    copies = [pltpu.make_async_copy(src, dst, sems.at[i]) for i, (src, dst) in enumerate(pairs)]
    for copy in copies:
        copy.start()
    for copy in copies:
        copy.wait()
    own = b_ref.shape[1]
    b = b_ref[...]
    features, hole = x_ref.shape[0], LANES - own
    b_out = jnp.concatenate([b, jnp.zeros((8, hole), F32)], axis=1)
    hi = rounded(b_out)
    pieces = [pltpu.roll(b_out - hi, own - hole * i, 1) for i in range(own // hole)]
    pieces += [jnp.zeros((8, LANES), F32)] * (features // 8 - len(pieces))
    x = jnp.concatenate([x_ref[...].astype(F32), jnp.zeros((features, hole), F32)], axis=1)
    x = jnp.where(iota(x.shape, 1) < own, x, jnp.concatenate(pieces, axis=0))
    block = jnp.concatenate([x, hi], axis=0).astype(BF16)
    for i in range(cols_ref.shape[0]):
        cols_ref[i] = block
    for i in range(rows_ref.shape[0]):
        rows_ref[i] = block
    b_out_ref[...] = b_out
    diagonal = iota((8, 8), 0) == iota((8, 8), 1)
    amp = total(jnp.where(diagonal, jnp.broadcast_to(amp_ref[...], (8, 8)), 0.0))
    noise = total(jnp.where(diagonal, jnp.broadcast_to(noise_ref[...], (8, 8)), 0.0))
    consts_ref[...] = jnp.where(iota((8, LANES), 1) == 0, amp, noise)


def operand(block, features, own, is_row):
    x = block[:features]
    half = 0.5 * jnp.sum(x * x, axis=0, keepdims=True)
    h1 = rounded(half)
    h2 = rounded(half - h1)
    h3 = half - h1 - h2
    k = iota((16, LANES), 0)
    at = 0 if is_row else 3
    pieces = jnp.where(k == at, -h1, jnp.where(k == at + 1, -h2, jnp.where(k == at + 2, -h3, 0.0)))
    ones = jnp.where((k >= 3 - at) & (k < 6 - at), 1.0, 0.0)
    return jnp.concatenate([x, pieces + ones], axis=0).T[:own].astype(BF16)


def tile_product(rows_ref, cols_ref, vec_ref, scale, height, width, ready=None):
    n_rows, n_cols = rows_ref.shape[0], cols_ref.shape[0]
    outs = []
    for at in range(0, n_rows, height):
        if ready:
            ready(at + height, 0)
        rows = rows_ref[at : at + height, :]
        acc = jnp.zeros((vec_ref.shape[0], height), F32)
        for c in range(0, n_cols, width):
            if ready:
                ready(at + 2 * height, c + 2 * width)
            inner = lax.dot_general(
                cols_ref[c : c + width, :], rows, (((1,), (1,)), ((), ())), preferred_element_type=F32
            )
            e = jnp.exp2(inner * scale)
            hi = e.astype(BF16)
            lo = (e - hi.astype(F32)).astype(BF16)
            vec = vec_ref[:, c : c + width]
            acc += jnp.dot(vec, hi, preferred_element_type=F32)
            acc += jnp.dot(vec, lo, preferred_element_type=F32)
        outs.append(acc[:8] + acc[8:])
    return jnp.concatenate(outs, axis=1)


def targets_of(block, features, own):
    hole = LANES - own
    k = iota((8, LANES), 1)
    lo = None
    for i in reversed(range(own // hole)):
        piece = pltpu.roll(block[8 * i : 8 * (i + 1)], hole * (i + 1), 1)
        lo = piece if lo is None else jnp.where(k < hole * (i + 1), piece, lo)
    return block[features : features + 8], lo


def packed_all(blocks, own):
    step = step_of(own)
    return jnp.concatenate([packed(blocks[i : i + step], own) for i in range(0, len(blocks), step)], axis=1)


def first_kernel(scale, own, features, height, width, gcols_ref, grows_ref, rows_ref, cols_ref, vec_ref, out_ref, b_ref):
    n_c, n_r = gcols_ref.shape[0], grows_ref.shape[0]
    step = step_of(own)
    done = {"rows": 0, "cols": 0}

    def ready(n_rows, n_cols):
        while done["cols"] < n_c and own * done["cols"] < n_cols:
            i = done["cols"]
            pieces = []
            for j in range(i, i + step):
                block = gcols_ref[j].astype(F32)
                cols_ref[own * j : own * (j + 1), :] = operand(block, features, own, False)
                pieces.append(jnp.concatenate(targets_of(block, features, own), axis=0))
            vec_ref[:, own * i : own * (i + step)] = packed(pieces, own).astype(BF16)
            done["cols"] = i + step
        while done["rows"] < n_r and own * done["rows"] < n_rows:
            i = done["rows"]
            targets = []
            for j in range(i, i + step):
                block = grows_ref[j].astype(F32)
                rows_ref[own * j : own * (j + 1), :] = operand(block, features, own, True)
                hi, lo = targets_of(block, features, own)
                targets.append(hi + lo)
            b_ref[:, own * i : own * (i + step)] = packed(targets, own)
            done["rows"] = i + step

    out_ref[...] = tile_product(rows_ref, cols_ref, vec_ref, scale, height, width, ready)


def chip_kernel(parts_ref, out_ref):
    e = parts_ref[0]
    for j in range(1, parts_ref.shape[0]):
        e = e + parts_ref[j]
    for i in range(out_ref.shape[0]):
        out_ref[i] = e


def image_kernel(own, parts_ref, b_ref, own_b_ref, consts_ref, vec_ref, own_w_ref, out_hbm, blocks_ref, out_ref, sem):
    consts = consts_ref[...]
    amp, noise = consts[:, :1], consts[:, 1:2]
    e = parts_ref[0]
    for j in range(1, parts_ref.shape[0]):
        e = e + parts_ref[j]
    b = b_ref[...]
    w = amp * e + noise * b
    curve, norm = total(b * w), total(b * b)
    for i in range(blocks_ref.shape[0]):
        blocks_ref[i] = block_of(e, i, own)
    me = 0
    for axis in ROWS:
        me = me * group((axis,)) + lax.axis_index(axis)
    own_w = amp * blocks_ref[me] + noise * own_b_ref[...]
    own_w_ref[...] = own_w
    k = iota((8, LANES), 1)
    message = jnp.where(k < own, own_w, jnp.where(k == own, curve, norm))
    for i in range(out_ref.shape[0]):
        out_ref[i] = message
    copy = pltpu.make_async_copy(out_ref, out_hbm, sem)
    copy.start()
    hi = rounded(w)
    vec_ref[...] = jnp.concatenate([hi, w - hi], axis=0).astype(BF16)
    copy.wait()


def second_kernel(scale, height, width, rows_ref, cols_ref, vec_ref, out_ref):
    out_ref[...] = tile_product(cols_ref, rows_ref, vec_ref, scale, height, width)


def spread(values):
    sub, k = iota((8, LANES), 0), iota((8, LANES), 1)
    row = jnp.zeros((8, LANES), F32)
    for j, v in enumerate(values):
        row = jnp.where(k == 8 * j + sub, v, row)
    return jnp.sum(row, axis=0, keepdims=True)


def gathered(row, n):
    sub, k = iota((8, LANES), 0), iota((8, LANES), 1)
    rows = jnp.broadcast_to(row, (8, LANES))
    return [total(jnp.where(k == 8 * j + sub, rows, 0.0)) for j in range(n)]


def dots_kernel(own, u_ref, gw_ref, vec_ref, out_ref, stats_ref):
    n_c = gw_ref.shape[0]
    sums = gw_ref[0]
    for i in range(1, n_c):
        sums = sums + gw_ref[i]
    curve, norm = lane(sums, own), lane(sums, own + 1)
    alpha = norm / curve
    w = packed_all([gw_ref[i] for i in range(n_c)], own)
    b = vec_ref[...].astype(F32)
    r = b[:8] + b[8:] - alpha * w
    out_ref[...] = jnp.broadcast_to(spread((total(r * u_ref[...]), total(r * r), total(r * w))), out_ref.shape)
    k = iota((8, LANES), 1)
    stats_ref[...] = jnp.where(k == 0, alpha, jnp.where(k == 1, norm, curve))


def scatter_kernel(own, gs_ref, u_ref, out_ref, sums_ref):
    ru, rr, rw = gathered(jnp.sum(gs_ref[...], axis=0, keepdims=True), 3)
    u = u_ref[...]
    k = iota((8, LANES), 1)
    for i in range(out_ref.shape[0]):
        out_ref[i] = jnp.where(k < own, block_of(u, i, own), ru)
    sums_ref[...] = jnp.where(k == 0, rr, rw)


def last_kernel(own, parts_ref, stats_ref, sums_ref, w_ref, b_ref, consts_ref, x_ref, r_ref):
    u = parts_ref[0]
    for j in range(1, parts_ref.shape[0]):
        u = u + parts_ref[j]
    ru, rr, rw = lane(u, own), sums_ref[:, :1], sums_ref[:, 1:2]
    stats, consts = stats_ref[...], consts_ref[...]
    alpha, norm, curve = stats[:, :1], stats[:, 1:2], stats[:, 2:3]
    amp, noise = consts[:, :1], consts[:, 1:2]
    b, w = b_ref[...], w_ref[...]
    r = b - alpha * w
    beta = rr / norm
    direction = r + beta * b
    image = w - alpha * (amp * u + noise * w) + beta * w
    curve2 = rw - alpha * (amp * ru + noise * rw) + 2.0 * beta * rw + beta * beta * curve
    alpha2 = rr / curve2
    x_ref[...] = (alpha * b + alpha2 * direction)[:, :own]
    r_ref[...] = (r - alpha2 * image)[:, :own]


def shards(samples, targets, amplitude, noise):
    own, features = samples.shape
    n_c, n_r = group(COLS), group(ROWS)
    scale = 4.0 * 2.0 / features * LOG2E
    depth = features + 16
    height, width = HEIGHT, WIDTH

    def array(*shape, dtype=F32):
        return jax.ShapeDtypeStruct(shape, dtype)

    tile = array(8, LANES)
    vmem = pl.BlockSpec(memory_space=pltpu.VMEM)
    given = [pltpu.with_memory_space_constraint(v, pltpu.HBM) for v in (samples.T, targets.T, amplitude.reshape(1, -1), noise.reshape(1, -1))]
    mcols, mrows, b, consts = pl.pallas_call(
        pack_kernel,
        out_shape=(
            array(n_c, features + 8, LANES, dtype=BF16),
            array(n_r, features + 8, LANES, dtype=BF16),
            tile,
            tile,
        ),
        in_specs=[pl.BlockSpec(memory_space=pltpu.HBM)] * 4,
        scratch_shapes=[pltpu.VMEM(v.shape, v.dtype) for v in given] + [pltpu.SemaphoreType.DMA((4,))],
        compiler_params=SMALL,
    )(*given)
    grows = exchange(mrows, ROWS)
    mcols, grows = lax.optimization_barrier((mcols, grows))
    gcols = exchange(mcols, COLS)
    rows, cols, vec, t, b_rows = pl.pallas_call(
        functools.partial(first_kernel, scale, own, features, height, width),
        out_shape=(
            array(n_r * own, depth, dtype=BF16),
            array(n_c * own, depth, dtype=BF16),
            array(16, n_c * own, dtype=BF16),
            array(8, n_r * own),
            array(8, n_r * own),
        ),
        compiler_params=LARGE,
    )(gcols, grows)
    parts = pl.pallas_call(
        chip_kernel, out_shape=array(group(CHIPS), 8, n_r * own), compiler_params=SMALL
    )(lax.all_gather(t, CHIP))
    parts = exchange(parts, CHIPS)
    w_vec, w, message = pl.pallas_call(
        functools.partial(image_kernel, own),
        out_shape=(array(16, n_r * own, dtype=BF16), tile, array(n_c, 8, LANES)),
        out_specs=(vmem, vmem, pl.BlockSpec(memory_space=pltpu.HBM)),
        scratch_shapes=[
            pltpu.VMEM((n_r, 8, LANES), F32),
            pltpu.VMEM((n_c, 8, LANES), F32),
            pltpu.SemaphoreType.DMA,
        ],
        compiler_params=SMALL,
    )(parts, b_rows, b, consts)
    gw = exchange(message, COLS)
    u = pl.pallas_call(
        functools.partial(second_kernel, scale, height, width),
        out_shape=array(8, n_c * own),
        compiler_params=LARGE,
        cost_estimate=pl.CostEstimate(
            flops=2 * 2 * 256 * n_r * n_c * own * own,
            bytes_accessed=n_r * n_c * own * own,
            transcendentals=n_r * n_c * own * own,
        ),
    )(rows, cols, w_vec)
    message, stats = pl.pallas_call(
        functools.partial(dots_kernel, own),
        out_shape=(array(n_r, LANES), tile),
        compiler_params=SMALL,
    )(u, gw, vec)
    gs = exchange(message, ROWS)
    parts, sums = pl.pallas_call(
        functools.partial(scatter_kernel, own),
        out_shape=(array(n_c, 8, LANES), tile),
        compiler_params=SMALL,
    )(gs, u)
    parts = exchange(parts, COLS)
    x, r = pl.pallas_call(
        functools.partial(last_kernel, own),
        out_shape=(array(8, own), array(8, own)),
        compiler_params=SMALL,
    )(parts, stats, sums, w, b, consts)
    return x.T, r.T


HEIGHT, WIDTH = 256, 256


def solution(mesh):
    fine = Mesh(mesh.devices.reshape(SIZES), AXES)
    split = P(AXES, None)
    return jax.shard_map(
        shards,
        mesh=fine,
        in_specs=(split, split, P(), P()),
        out_specs=(split, split),
        check_vma=False,
    )
```

```python
import functools
import math

import jax
import jax.numpy as jnp
import numpy as np
from jax import lax
from jax.experimental import pallas as pl
from jax.experimental.pallas import tpu as pltpu
from jax.sharding import Mesh
from jax.sharding import PartitionSpec as P

AXES = ("yh", "z", "core", "x", "yl")
SIZES = (4, 8, 2, 4, 2)
COLS = ("z", "yh")
ROWS = ("core", "x", "yl")
CHIP = "core"
CHIPS = ("x", "yl")
LANES = 128
LOG2E = 1.4426950408889634
F32 = jnp.float32
BF16 = jnp.bfloat16
SMALL = pltpu.CompilerParams(vmem_limit_bytes=4 * 1024 * 1024)
LARGE = pltpu.CompilerParams(vmem_limit_bytes=24 * 1024 * 1024)


def group(axes):
    return int(np.prod([SIZES[AXES.index(a)] for a in axes]))


def iota(shape, dim):
    return lax.broadcasted_iota(jnp.int32, shape, dim)


def rounded(v):
    return v.astype(BF16).astype(F32)


def lane(block, k):
    return total(jnp.where(iota(block.shape, 1) == k, block, 0.0))


def total(v):
    return jnp.sum(v, axis=1, keepdims=True)


def exchange(blocks, axes):
    return lax.all_to_all(blocks, axes, 0, 0)


def packed(blocks, own):
    k = iota(blocks[0].shape, 1)
    rolled = [b if own * i % LANES == 0 else pltpu.roll(b, own * i % LANES, 1) for i, b in enumerate(blocks)]
    outs = []
    for q in range(own * len(blocks) // LANES):
        out = None
        for i, b in enumerate(rolled):
            at = own * i - LANES * q
            if at + own <= 0 or at >= LANES:
                continue
            out = b if out is None else jnp.where(k < at, out, b)
        outs.append(out)
    return jnp.concatenate(outs, axis=1)


def block_of(dense, i, own):
    q, s = divmod(own * i, LANES)
    out = dense[:, LANES * q : LANES * (q + 1)]
    if s == 0:
        return out
    out = pltpu.roll(out, LANES - s, 1)
    if s + own > LANES:
        after = pltpu.roll(dense[:, LANES * (q + 1) : LANES * (q + 2)], LANES - s, 1)
        out = jnp.where(iota(out.shape, 1) < LANES - s, out, after)
    return out


def step_of(own):
    return LANES // math.gcd(own, LANES)


def pack_kernel(x_hbm, b_hbm, amp_hbm, noise_hbm, cols_ref, rows_ref, b_out_ref, consts_ref, x_ref, b_ref, amp_ref, noise_ref, sems):
    pairs = ((x_hbm, x_ref), (b_hbm, b_ref), (amp_hbm, amp_ref), (noise_hbm, noise_ref))
    copies = [pltpu.make_async_copy(src, dst, sems.at[i]) for i, (src, dst) in enumerate(pairs)]
    for copy in copies:
        copy.start()
    for copy in copies:
        copy.wait()
    own = b_ref.shape[1]
    b = b_ref[...]
    features, hole = x_ref.shape[0], LANES - own
    b_out = jnp.concatenate([b, jnp.zeros((8, hole), F32)], axis=1)
    hi = rounded(b_out)
    pieces = [pltpu.roll(b_out - hi, own - hole * i, 1) for i in range(own // hole)]
    pieces += [jnp.zeros((8, LANES), F32)] * (features // 8 - len(pieces))
    x = jnp.concatenate([x_ref[...].astype(F32), jnp.zeros((features, hole), F32)], axis=1)
    x = jnp.where(iota(x.shape, 1) < own, x, jnp.concatenate(pieces, axis=0))
    block = jnp.concatenate([x, hi], axis=0).astype(BF16)
    for i in range(cols_ref.shape[0]):
        cols_ref[i] = block
    for i in range(rows_ref.shape[0]):
        rows_ref[i] = block
    b_out_ref[...] = b_out
    diagonal = iota((8, 8), 0) == iota((8, 8), 1)
    amp = total(jnp.where(diagonal, jnp.broadcast_to(amp_ref[...], (8, 8)), 0.0))
    noise = total(jnp.where(diagonal, jnp.broadcast_to(noise_ref[...], (8, 8)), 0.0))
    consts_ref[...] = jnp.where(iota((8, LANES), 1) == 0, amp, noise)


def operand(block, features, own, is_row):
    x = block[:features]
    half = 0.5 * jnp.sum(x * x, axis=0, keepdims=True)
    h1 = rounded(half)
    h2 = rounded(half - h1)
    h3 = half - h1 - h2
    k = iota((16, LANES), 0)
    at = 0 if is_row else 3
    pieces = jnp.where(k == at, -h1, jnp.where(k == at + 1, -h2, jnp.where(k == at + 2, -h3, 0.0)))
    ones = jnp.where((k >= 3 - at) & (k < 6 - at), 1.0, 0.0)
    return jnp.concatenate([x, pieces + ones], axis=0).T[:own].astype(BF16)


def tile_product(rows_ref, cols_ref, vec_ref, scale, height, width, ready=None):
    n_rows, n_cols = rows_ref.shape[0], cols_ref.shape[0]
    outs = []
    for at in range(0, n_rows, height):
        if ready:
            ready(at + height, 0)
        rows = rows_ref[at : at + height, :]
        acc = jnp.zeros((vec_ref.shape[0], height), F32)
        for c in range(0, n_cols, width):
            if ready:
                ready(at + height, c + width)
            inner = lax.dot_general(
                cols_ref[c : c + width, :], rows, (((1,), (1,)), ((), ())), preferred_element_type=F32
            )
            e = jnp.exp2(inner * scale)
            hi = e.astype(BF16)
            lo = (e - hi.astype(F32)).astype(BF16)
            vec = vec_ref[:, c : c + width]
            acc += jnp.dot(vec, hi, preferred_element_type=F32)
            acc += jnp.dot(vec, lo, preferred_element_type=F32)
            if ready:
                ready(at + 2 * height, c + 2 * width)
        outs.append(acc[:8] + acc[8:])
    return jnp.concatenate(outs, axis=1)


def targets_of(block, features, own):
    hole = LANES - own
    k = iota((8, LANES), 1)
    lo = None
    for i in reversed(range(own // hole)):
        piece = pltpu.roll(block[8 * i : 8 * (i + 1)], hole * (i + 1), 1)
        lo = piece if lo is None else jnp.where(k < hole * (i + 1), piece, lo)
    return block[features : features + 8], lo


def packed_all(blocks, own):
    step = step_of(own)
    return jnp.concatenate([packed(blocks[i : i + step], own) for i in range(0, len(blocks), step)], axis=1)


def first_kernel(scale, own, features, height, width, gcols_ref, grows_ref, rows_ref, cols_ref, vec_ref, out_ref, b_ref):
    n_c, n_r = gcols_ref.shape[0], grows_ref.shape[0]
    step = step_of(own)
    done = {"rows": 0, "cols": 0}

    def ready(n_rows, n_cols):
        while done["cols"] < n_c and own * done["cols"] < n_cols:
            i = done["cols"]
            pieces = []
            for j in range(i, i + step):
                block = gcols_ref[j].astype(F32)
                cols_ref[own * j : own * (j + 1), :] = operand(block, features, own, False)
                pieces.append(jnp.concatenate(targets_of(block, features, own), axis=0))
            vec_ref[:, own * i : own * (i + step)] = packed(pieces, own).astype(BF16)
            done["cols"] = i + step
        while done["rows"] < n_r and own * done["rows"] < n_rows:
            i = done["rows"]
            targets = []
            for j in range(i, i + step):
                block = grows_ref[j].astype(F32)
                rows_ref[own * j : own * (j + 1), :] = operand(block, features, own, True)
                hi, lo = targets_of(block, features, own)
                targets.append(hi + lo)
            b_ref[:, own * i : own * (i + step)] = packed(targets, own)
            done["rows"] = i + step

    out_ref[...] = tile_product(rows_ref, cols_ref, vec_ref, scale, height, width, ready)


def chip_kernel(parts_ref, out_ref):
    e = parts_ref[0]
    for j in range(1, parts_ref.shape[0]):
        e = e + parts_ref[j]
    for i in range(out_ref.shape[0]):
        out_ref[i] = e


def image_kernel(own, parts_ref, b_ref, own_b_ref, consts_ref, vec_ref, own_w_ref, out_ref, blocks_ref):
    consts = consts_ref[...]
    amp, noise = consts[:, :1], consts[:, 1:2]
    e = parts_ref[0]
    for j in range(1, parts_ref.shape[0]):
        e = e + parts_ref[j]
    b = b_ref[...]
    w = amp * e + noise * b
    hi = rounded(w)
    vec_ref[...] = jnp.concatenate([hi, w - hi], axis=0).astype(BF16)
    curve, norm = total(b * w), total(b * b)
    for i in range(blocks_ref.shape[0]):
        blocks_ref[i] = block_of(e, i, own)
    me = 0
    for axis in ROWS:
        me = me * group((axis,)) + lax.axis_index(axis)
    own_w = amp * blocks_ref[me] + noise * own_b_ref[...]
    own_w_ref[...] = own_w
    k = iota((8, LANES), 1)
    message = jnp.where(k < own, own_w, jnp.where(k == own, curve, norm))
    for i in range(out_ref.shape[0]):
        out_ref[i] = message


def second_kernel(scale, height, width, rows_ref, cols_ref, vec_ref, out_ref):
    out_ref[...] = tile_product(cols_ref, rows_ref, vec_ref, scale, height, width)


def spread(values):
    sub, k = iota((8, LANES), 0), iota((8, LANES), 1)
    row = jnp.zeros((8, LANES), F32)
    for j, v in enumerate(values):
        row = jnp.where(k == 8 * j + sub, v, row)
    return jnp.sum(row, axis=0, keepdims=True)


def gathered(row, n):
    sub, k = iota((8, LANES), 0), iota((8, LANES), 1)
    rows = jnp.broadcast_to(row, (8, LANES))
    return [total(jnp.where(k == 8 * j + sub, rows, 0.0)) for j in range(n)]


def dots_kernel(own, u_ref, gw_ref, vec_ref, out_ref, stats_ref):
    n_c = gw_ref.shape[0]
    sums = gw_ref[0]
    for i in range(1, n_c):
        sums = sums + gw_ref[i]
    curve, norm = lane(sums, own), lane(sums, own + 1)
    alpha = norm / curve
    w = packed_all([gw_ref[i] for i in range(n_c)], own)
    b = vec_ref[...].astype(F32)
    r = b[:8] + b[8:] - alpha * w
    out_ref[...] = jnp.broadcast_to(spread((total(r * u_ref[...]), total(r * r), total(r * w))), out_ref.shape)
    k = iota((8, LANES), 1)
    stats_ref[...] = jnp.where(k == 0, alpha, jnp.where(k == 1, norm, curve))


def scatter_kernel(own, gs_ref, u_ref, out_ref, sums_ref):
    ru, rr, rw = gathered(jnp.sum(gs_ref[...], axis=0, keepdims=True), 3)
    u = u_ref[...]
    k = iota((8, LANES), 1)
    for i in range(out_ref.shape[0]):
        out_ref[i] = jnp.where(k < own, block_of(u, i, own), ru)
    sums_ref[...] = jnp.where(k == 0, rr, rw)


def last_kernel(own, parts_ref, stats_ref, sums_ref, w_ref, b_ref, consts_ref, x_ref, r_ref):
    u = parts_ref[0]
    for j in range(1, parts_ref.shape[0]):
        u = u + parts_ref[j]
    ru, rr, rw = lane(u, own), sums_ref[:, :1], sums_ref[:, 1:2]
    stats, consts = stats_ref[...], consts_ref[...]
    alpha, norm, curve = stats[:, :1], stats[:, 1:2], stats[:, 2:3]
    amp, noise = consts[:, :1], consts[:, 1:2]
    b, w = b_ref[...], w_ref[...]
    r = b - alpha * w
    beta = rr / norm
    direction = r + beta * b
    image = w - alpha * (amp * u + noise * w) + beta * w
    curve2 = rw - alpha * (amp * ru + noise * rw) + 2.0 * beta * rw + beta * beta * curve
    alpha2 = rr / curve2
    x_ref[...] = (alpha * b + alpha2 * direction)[:, :own]
    r_ref[...] = (r - alpha2 * image)[:, :own]


def shards(samples, targets, amplitude, noise):
    own, features = samples.shape
    n_c, n_r = group(COLS), group(ROWS)
    scale = 4.0 * 2.0 / features * LOG2E
    depth = features + 16
    height, width = HEIGHT, WIDTH

    def array(*shape, dtype=F32):
        return jax.ShapeDtypeStruct(shape, dtype)

    tile = array(8, LANES)
    given = [pltpu.with_memory_space_constraint(v, pltpu.HBM) for v in (samples.T, targets.T, amplitude.reshape(1, -1), noise.reshape(1, -1))]
    mcols, mrows, b, consts = pl.pallas_call(
        pack_kernel,
        out_shape=(
            array(n_c, features + 8, LANES, dtype=BF16),
            array(n_r, features + 8, LANES, dtype=BF16),
            tile,
            tile,
        ),
        in_specs=[pl.BlockSpec(memory_space=pltpu.HBM)] * 4,
        scratch_shapes=[pltpu.VMEM(v.shape, v.dtype) for v in given] + [pltpu.SemaphoreType.DMA((4,))],
        compiler_params=SMALL,
    )(*given)
    grows = exchange(mrows, ROWS)
    mcols, grows = lax.optimization_barrier((mcols, grows))
    gcols = exchange(mcols, COLS)
    rows, cols, vec, t, b_rows = pl.pallas_call(
        functools.partial(first_kernel, scale, own, features, height, width),
        out_shape=(
            array(n_r * own, depth, dtype=BF16),
            array(n_c * own, depth, dtype=BF16),
            array(16, n_c * own, dtype=BF16),
            array(8, n_r * own),
            array(8, n_r * own),
        ),
        compiler_params=LARGE,
    )(gcols, grows)
    parts = pl.pallas_call(
        chip_kernel, out_shape=array(group(CHIPS), 8, n_r * own), compiler_params=SMALL
    )(lax.all_gather(t, CHIP))
    parts = exchange(parts, CHIPS)
    w_vec, w, message = pl.pallas_call(
        functools.partial(image_kernel, own),
        out_shape=(array(16, n_r * own, dtype=BF16), tile, array(n_c, 8, LANES)),
        scratch_shapes=[pltpu.VMEM((n_r, 8, LANES), F32)],
        compiler_params=SMALL,
    )(parts, b_rows, b, consts)
    gw = exchange(message, COLS)
    u = pl.pallas_call(
        functools.partial(second_kernel, scale, height, width),
        out_shape=array(8, n_c * own),
        compiler_params=LARGE,
        cost_estimate=pl.CostEstimate(
            flops=2 * 2 * 256 * n_r * n_c * own * own,
            bytes_accessed=n_r * n_c * own * own,
            transcendentals=n_r * n_c * own * own,
        ),
    )(rows, cols, w_vec)
    message, stats = pl.pallas_call(
        functools.partial(dots_kernel, own),
        out_shape=(array(n_r, LANES), tile),
        compiler_params=SMALL,
    )(u, gw, vec)
    gs = exchange(message, ROWS)
    parts, sums = pl.pallas_call(
        functools.partial(scatter_kernel, own),
        out_shape=(array(n_c, 8, LANES), tile),
        compiler_params=SMALL,
    )(gs, u)
    parts = exchange(parts, COLS)
    x, r = pl.pallas_call(
        functools.partial(last_kernel, own),
        out_shape=(array(8, own), array(8, own)),
        compiler_params=SMALL,
    )(parts, stats, sums, w, b, consts)
    return x.T, r.T


HEIGHT, WIDTH = 256, 512


def solution(mesh):
    fine = Mesh(mesh.devices.reshape(SIZES), AXES)
    split = P(AXES, None)
    return jax.shard_map(
        shards,
        mesh=fine,
        in_specs=(split, split, P(), P()),
        out_specs=(split, split),
        check_vma=False,
    )
```
